128 devices in a mesh: gx: 8 (over y, z_hi), gy: 4 (over x), gz: 4 (over z_lo, core).
Axes of the slice: x: 4, y: 4, z: 4 (z_hi: 2, z_lo: 2; z = z_hi * 2 + z_lo), core: 2. Of those that a mesh axis runs over, the one named last changes fastest.
Arguments:
- pressure_now: float32 [256, 128, 512], P('gx', 'gy', 'gz'), may hold values from -6 to 6
- pressure_old: float32 [256, 128, 512], P('gx', 'gy', 'gz'), may hold values from -6 to 6
- cell_code: int32 [256, 128, 512], P('gx', 'gy', 'gz'), may hold values from 0 to 3
- surf_index: int32 [32, 2048], P(('gx', 'gz'), 'gy'), may hold values from -1 to 131071, as said below
- history: bfloat16 [540, 65536], P(None, ('gx', 'gz')), may hold values from -6 to 6
- dir_slot: int32 [512, 24], P(('gx', 'gz'), 'gy'), may hold values from -1 to 7, as said below
- delay: int32 [512, 24], P(('gx', 'gz'), 'gy'), may hold values from 0 to 32
- weights: bfloat16 [512, 24, 128, 128], P(('gx', 'gz'), 'gy'), may hold values from -0.0390625 to 0.0390625
Outputs:
- pressure_next: float32 [256, 128, 512], P('gx', 'gy', 'gz')
- pressure_prev: float32 [256, 128, 512], P('gx', 'gy', 'gz')
- far_field: float32 [512, 4096], P(('gx', 'gz'), 'gy')
The draws below stay inside these ranges and needn't reach their ends.
Inputs may be any that keep to these rules, and one draw needn't show every extreme that they name: `surf_index`: in each brick's 512 slots the live ones come first; -1 marks an empty slot. `dir_slot`: within a panel block, the 6 entries of one direction group have their live entries first and -1 for dead ones.
All inputs are finite; a program needn't handle non-finite values.
Results may differ from the reference program's by a relative error of at most 0.0003.
Values may be sent and summed in bfloat16 or wider, within the bound.
A program may use at most 128 MiB of HBM per device.

```python
import jax
import jax.numpy as jnp
from jax import lax

CX = 32
CY = 32
CZ = 128
SLOT = 512
STEPS = 4
NDIR = 4096
TW = 512
MAXOFF = 32
PB = 128
DB = 128
K_DEV = 6
NX = 256
NY = 128
NZ = 512
GROUPS = 32
PANELS = 65536
NPB = 512
DIR_BLOCKS = 8
HOLD = 540
N_GX = 8
N_GY = 4
N_GZ = 4


def draw_surf_index(key, part):
    key = jax.random.fold_in(key, 11)
    key_count, key_cell = jax.random.split(key)
    counts = jax.random.randint(key_count, (GROUPS, N_GY, 1), 0, SLOT + 1)
    counts = counts.at[0, 0, 0].set(SLOT)
    counts = counts.at[0, N_GY - 1, 0].set(SLOT // 2)
    cells = jax.random.randint(key_cell, (GROUPS, N_GY, SLOT), 0, CX * CY * CZ)
    cells = cells.at[0, 0, 0].set(CX * CY * CZ - 1)
    positions = jnp.arange(SLOT, dtype=jnp.int32)[None, None, :]
    placed = jnp.where(positions < counts, cells, -1)
    return placed.reshape(GROUPS, N_GY * SLOT).astype(jnp.int32)


def draw_dir_slot(key, part):
    key = jax.random.fold_in(key, 21)
    key_section, key_live, key_block = jax.random.split(key, 3)
    per_group = NPB // GROUPS
    section = jax.random.randint(key_section, (GROUPS, 1, 1, 1), 0, 4) == 0
    section = section.at[0, 0, 0, 0].set(True)
    sparse_live = jax.random.randint(key_live, (GROUPS, per_group, N_GY, 1), 1, K_DEV // 2 + 1)
    live = jnp.where(section, K_DEV, sparse_live)
    live = live.at[0, 0, 0, 0].set(K_DEV - 1)
    chosen = jax.random.randint(key_block, (GROUPS, per_group, N_GY, K_DEV), 0, DIR_BLOCKS)
    chosen = chosen.at[0, 0, 0, 0].set(DIR_BLOCKS - 1)
    positions = jnp.arange(K_DEV, dtype=jnp.int32)[None, None, None, :]
    placed = jnp.where(positions < live, chosen, -1)
    return placed.reshape(NPB, N_GY * K_DEV).astype(jnp.int32)


def draw_delay(key, part):
    key = jax.random.fold_in(key, 31)
    offsets = jax.random.randint(key, (NPB, N_GY * K_DEV), 0, MAXOFF + 1)
    offsets = offsets.at[0, 0].set(MAXOFF)
    offsets = offsets.at[0, 1].set(0)
    return offsets.astype(jnp.int32)


def set_ends(result, stream_key, smallest, largest):
    longest = result.shape.index(max(result.shape))
    spots = []
    for shift in (0, 1):
        where = [jax.random.randint(jax.random.fold_in(stream_key, axis), (), 0, length) for axis, length in enumerate(result.shape)]
        where[longest] = (where[longest] + shift) % result.shape[longest]
        spots.append(tuple(where))
    return result.at[spots[0]].set(smallest).at[spots[1]].set(largest)


def level_of(rng, shape, cuts, smallest, top_value):
    gain, own = 1.0, jax.random.fold_in(rng, 6)
    for dim, blocks in cuts:
        steps = jnp.exp(jax.random.uniform(jax.random.fold_in(own, dim), (blocks,), jnp.float32, smallest / len(cuts), top_value / len(cuts)))
        gain = gain * jnp.repeat(steps, shape[dim] // blocks).reshape([-1 if axis == dim else 1 for axis in range(len(shape))])
    return gain


def scatter_about(rng, extent, scale, most, pieces=(), kind=jnp.bfloat16):
    result = jax.random.normal(rng, extent, jnp.float32) * scale
    if len(pieces) > 0:
        result = level_of(rng, extent, pieces, -0.22, 0.18) * result
    return jnp.clip(result, min=-most, max=most).astype(kind)


def setup_inputs(seed: int = 0) -> dict:
    seeds = jax.random.split(jax.random.key(seed), 9)
    pressure_now = scatter_about(seeds[0], (NX, NY, NZ), 1.0, 6.0, ((0, 8), (1, 4), (2, 4)), jnp.float32)
    pressure_old = scatter_about(seeds[1], (NX, NY, NZ), 1.0, 6.0, ((0, 8), (1, 4), (2, 4)), jnp.float32)
    cell_code = set_ends(jax.random.randint(seeds[2], (NX, NY, NZ), 0, 4), jax.random.fold_in(seeds[2], 1), 0, 3).astype(jnp.int32)
    surf_index = draw_surf_index(jax.random.fold_in(seeds[8], 71), 0)
    history = scatter_about(seeds[4], (HOLD, PANELS), 1.0, 6.0, ((1, 32),))
    dir_slot = draw_dir_slot(jax.random.fold_in(seeds[8], 71), 0)
    delay = draw_delay(jax.random.fold_in(seeds[8], 71), 0)
    weights = scatter_about(seeds[7], (NPB, N_GY * K_DEV, PB, DB), (PANELS * K_DEV // (2 * DIR_BLOCKS)) ** -0.5, 0.0390625, ((0, 32), (1, 4)))
    return {"pressure_now": pressure_now, "pressure_old": pressure_old, "cell_code": cell_code, "surf_index": surf_index, "history": history, "dir_slot": dir_slot, "delay": delay, "weights": weights}


def coefficients(cell_code):
    speeds = jnp.where(cell_code == 0, 0.32, jnp.where(cell_code == 1, 0.26, jnp.where(cell_code == 2, 0.19, 0.11))).astype(jnp.float32)
    damping = jnp.where(cell_code == 0, 0.0, jnp.where(cell_code == 1, 0.02, jnp.where(cell_code == 2, 0.08, 0.3))).astype(jnp.float32)
    return speeds, damping


def neighbours(padded):
    middle = padded[1:-1, 1:-1, 1:-1]
    summed = padded[2:, 1:-1, 1:-1] + padded[:-2, 1:-1, 1:-1]
    summed = summed + padded[1:-1, 2:, 1:-1] + padded[1:-1, :-2, 1:-1]
    summed = summed + padded[1:-1, 1:-1, 2:] + padded[1:-1, 1:-1, :-2]
    return summed - 6.0 * middle


def leapfrog(current, earlier, speeds, damping, padded):
    return (2.0 * current - (1.0 - damping) * earlier + speeds * neighbours(padded)) / (1.0 + damping)


def record(field, surf_index):
    bricks = field.reshape(N_GX, CX, N_GY, CY, N_GZ, CZ).transpose(0, 4, 2, 1, 3, 5).reshape(N_GX * N_GZ, N_GY, CX * CY * CZ)
    places = surf_index.reshape(N_GX * N_GZ, N_GY, SLOT)
    values = jnp.take_along_axis(bricks, jnp.maximum(places, 0), axis=2)
    return jnp.where(places >= 0, values, 0.0).astype(jnp.bfloat16).reshape(-1)


def far_sum(signal, dir_slot, delay, weights):
    blocks = signal.reshape(TW + MAXOFF, NPB, PB)
    slicer = jax.vmap(lambda column, offset: lax.dynamic_slice_in_dim(column, offset, TW, 0), in_axes=(1, 0))
    summed = jnp.zeros((NDIR // DB + 1, TW, DB), jnp.float32)
    for entry in range(K_DEV * N_GY):
        sliced = slicer(blocks, delay[:, entry])
        contrib = jnp.einsum("btp,bpd->btd", sliced.astype(jnp.float32), weights[:, entry].astype(jnp.float32))
        target = jnp.where(dir_slot[:, entry] >= 0, (entry // K_DEV) * DIR_BLOCKS + dir_slot[:, entry], NDIR // DB).astype(jnp.int32)
        summed = summed + jax.ops.segment_sum(contrib, target, num_segments=NDIR // DB + 1)
    return summed[:-1].transpose(1, 0, 2).reshape(TW, NDIR)


def reference(pressure_now, pressure_old, cell_code, surf_index, history, dir_slot, delay, weights):
    speeds, damping = coefficients(cell_code)
    current, earlier = pressure_now, pressure_old
    recorded = []
    for step_index in range(STEPS):
        padded = jnp.pad(current, 1)
        current, earlier = leapfrog(current, earlier, speeds, damping, padded), current
        recorded.append(record(current, surf_index))
    samples = jnp.stack(recorded)
    signal = jnp.concatenate([history, samples], axis=0)
    return current, earlier, far_sum(signal, dir_slot, delay, weights)
```

```python
import functools

import jax
import jax.numpy as jnp
import numpy as np
from jax import lax
from jax.experimental import pallas as pl
from jax.experimental.pallas import tpu as pltpu
from jax.sharding import PartitionSpec as P

MESH = pl.DeviceIdType.MESH
F32 = jnp.float32
BF16 = jnp.bfloat16

STEPS = 4
CX, CY, CZ = 32, 32, 128
SLOT = 512
TW = 512
MAXOFF = 32
HOLD = 540
PB = 128
DB = 128
K_DEV = 6
BLOCKS = 16
ENTRIES = K_DEV * BLOCKS
PAIRS = ENTRIES // 2 + 4
TARGETS = 8
OWNERS = 32
ROWS = 16
NX_DEV, NY_DEV, NZ_DEV = 8, 4, 4
LOW, HIGH = 8, 40
PADROWS = 48


def coefficient_table():
    speeds = np.array([0.32, 0.26, 0.19, 0.11], np.float32).astype(np.float64)
    damping = np.array([0.0, 0.02, 0.08, 0.3], np.float32).astype(np.float64)
    here = (2.0 - 6.0 * speeds) / (1.0 + damping)
    before = -(1.0 - damping) / (1.0 + damping)
    around = speeds / (1.0 + damping)
    return [[float(np.float32(v)) for v in row] for row in (here, before, around)]


COEFFICIENTS = coefficient_table()


def hall_kernel(
    dir_ref, delay_ref, dirs_ref, surf_ref, hist_ref, now_ref, old_ref, code_ref, w_ref,
    next_ref, prev_ref, far_ref,
    field_a, field_b, codes, coef, ystage, zstage, xrecv, yrecv, zrecv,
    onehot, rounded, samp_send, samp_all, spad, lhs, wv,
    signal, trail, table, order, hist, part, core_recv, sums, totals, ring1, ring2, corr_out, corr_in,
    load_sem, halo_send, halo_recv, samp_ssem, samp_rsem,
    core_ssem, core_rsem, ring_send, ring_recv, corr_ssem, corr_rsem,
):
    fields = (field_a, field_b)
    gx, gy, gz = lax.axis_index("gx"), lax.axis_index("gy"), lax.axis_index("gz")
    y, z_hi = gx // 2, lax.rem(gx, 2)
    z_lo, core = gz // 2, lax.rem(gz, 2)
    z = z_hi * 2 + z_lo
    group = gx * 4 + gz
    is_owner = group == OWNERS - 1

    def place(yy, zz):
        return (yy * 2 + zz // 2, gy, lax.rem(zz, 2) * 2 + core)

    def ring_neighbour(axis, offset):
        if axis == "z":
            return place(y, lax.rem(z + offset, 4))
        return place(lax.rem(y + offset, 4), z)

    sibling = (gx, gy, z_lo * 2 + 1 - core)
    owner = (NX_DEV - 1, gy, NZ_DEV - 1)
    coords = (gx, gy, gz)
    extents = (NX_DEV, NY_DEV, NZ_DEV)

    def beside(axis, side):
        moved = list(coords)
        moved[axis] = coords[axis] + (1 if side else -1)
        return tuple(moved)

    def exists(axis, side):
        return coords[axis] < extents[axis] - 1 if side else coords[axis] > 0

    barrier = pltpu.get_barrier_semaphore()

    def greet(device):
        pl.semaphore_signal(barrier, inc=1, device_id=device, device_id_type=MESH)

    expected = jnp.int32(8)
    for axis in range(3):
        for side in range(2):
            @pl.when(exists(axis, side))
            def _():
                greet(beside(axis, side))
            expected = expected + exists(axis, side).astype(jnp.int32)
    greet(sibling)
    for axis in ("y", "z"):
        for offset in (1, 3):
            greet(ring_neighbour(axis, offset))
    for offset in range(1, NY_DEV):
        greet((gx, lax.rem(gy + offset, NY_DEV), gz))

    @pl.when(is_owner)
    def _():
        def greet_one(member, carry):
            greet((member // 4, gy, lax.rem(member, 4)))
            return carry
        lax.fori_loop(0, OWNERS - 1, greet_one, 0)

    expected = expected + jnp.where(is_owner, 0, 1)

    loads = [
        pltpu.make_async_copy(now_ref, field_a.at[pl.ds(1, CX), pl.ds(LOW, CY)], load_sem.at[0]),
        pltpu.make_async_copy(hist_ref, hist, load_sem.at[3]),
        pltpu.make_async_copy(w_ref, wv.at[pl.ds(0, ENTRIES)], load_sem.at[4]),
        pltpu.make_async_copy(code_ref, codes, load_sem.at[2]),
        pltpu.make_async_copy(old_ref, field_b.at[pl.ds(1, CX), pl.ds(LOW, CY)], load_sem.at[1]),
    ]
    for load in loads:
        load.start()

    lane = lax.broadcasted_iota(jnp.int32, (CY, CZ), 1)
    zero_plane = jnp.zeros((CY, CZ), F32)

    UNROLL = 4

    def over_planes(body, init):
        def chunk(i, carry):
            return body([i * UNROLL + u for u in range(UNROLL)], carry)
        return lax.fori_loop(0, CX // UNROLL, chunk, init)

    def take_faces(step, xs, planes, carry):
        low, high = carry
        for x, plane in zip(xs, planes):
            low = jnp.where(lane == x, pltpu.roll(plane, x, 1), low)
            high = jnp.where(lane == x, pltpu.roll(plane, x + 1, 1), high)
        for x, plane in zip(xs, planes):
            ystage[step, 0, pl.ds(x, 1), :] = plane[0:1, :]
            ystage[step, 1, pl.ds(x, 1), :] = plane[CY - 1:CY, :]
        return low, high

    def halo_copy(step, axis, side):
        current = step % 2
        if axis == 0:
            source = fields[current].at[CX if side else 1, pl.ds(LOW, CY)]
            target = xrecv.at[step, 1 - side]
        elif axis == 1:
            source, target = ystage.at[step, side], yrecv.at[step, 1 - side]
        else:
            source, target = zstage.at[step, side], zrecv.at[step, 1 - side]
        return pltpu.make_async_remote_copy(
            src_ref=source, dst_ref=target,
            send_sem=halo_send.at[step, axis, side],
            recv_sem=halo_recv.at[step, axis, 1 - side],
            device_id=beside(axis, side), device_id_type=MESH,
        )

    def halo_start(step):
        for axis in range(3):
            for side in range(2):
                @pl.when(exists(axis, side))
                def _():
                    halo_copy(step, axis, side).start()

    def halo_wait_send(step, axes=(0, 1, 2)):
        for axis in axes:
            for side in range(2):
                @pl.when(exists(axis, side))
                def _():
                    halo_copy(step, axis, side).wait_send()

    def halo_wait_recv(step, axes):
        for axis in axes:
            buffer = (xrecv, yrecv, zrecv)[axis]
            for side in range(2):
                @pl.when(exists(axis, side))
                def _():
                    halo_copy(step, axis, 1 - side).wait_recv()
                @pl.when(jnp.logical_not(exists(axis, side)))
                def _():
                    buffer[step, side] = zero_plane

    dirs = dirs_ref[...]
    targets = jnp.concatenate(
        [dirs[k:k + 1, :] for k in range(K_DEV)]
        + [jnp.full((1, PB - ENTRIES), -1, jnp.int32)], axis=1)
    targets = jnp.where(targets >= 0, targets, TARGETS).astype(F32)
    by_lane = jnp.broadcast_to(targets, (PB, PB))
    by_row = by_lane.T
    lanes = lax.broadcasted_iota(jnp.int32, (PB, PB), 1).astype(F32)
    rows = lax.broadcasted_iota(jnp.int32, (PB, PB), 0).astype(F32)

    def count(mask, axis):
        return jnp.sum(jnp.where(mask, 1.0, 0.0), axis=axis, keepdims=True)

    def even(amount):
        return 2.0 * jnp.floor(0.5 * (amount + 1.0))

    member = by_row == lanes
    along_lanes = count(member, 0)
    along_rows = count(by_lane == rows, 1)
    first_lanes = jnp.sum(jnp.where(rows < lanes, even(along_rows), 0.0), axis=0, keepdims=True)
    first_rows = jnp.sum(jnp.where(lanes < rows, even(along_lanes), 0.0), axis=1, keepdims=True)
    before = count(jnp.logical_and(by_lane == by_row, lanes < rows), 1)
    slot = before + jnp.sum(jnp.where(member, first_lanes, 0.0), axis=1, keepdims=True)
    taken = jnp.logical_and(slot == lanes, by_row < TARGETS)
    sequence = ENTRIES + jnp.sum(jnp.where(taken, rows - ENTRIES, 0.0), axis=0, keepdims=True)
    ends = jnp.where(along_lanes > 0, 0.5 * (first_lanes + even(along_lanes)), 0.0)
    opens = count(
        jnp.logical_and(jnp.logical_and(0.5 * first_rows == lanes, along_rows > 0), rows < TARGETS), 0)
    table[0:1, :] = sequence.astype(jnp.int32)
    table[1:2, :] = ends.astype(jnp.int32)
    table[2:3, :] = opens.astype(jnp.int32)
    table[3:8, :] = jnp.zeros((5, PB), jnp.int32)
    order_load = pltpu.make_async_copy(table, order, load_sem.at[7])
    order_load.start()

    loads[0].wait()

    def first_faces(xs, carry):
        return take_faces(0, xs, [field_a[x + 1, LOW:HIGH, :] for x in xs], carry)

    low, high = over_planes(first_faces, (zero_plane, zero_plane))
    zstage[0, 0] = low
    zstage[0, 1] = high

    pl.semaphore_wait(barrier, expected)
    halo_start(0)

    def core_copy(half):
        return pltpu.make_async_remote_copy(
            src_ref=part.at[pl.ds(half * 4, 4), :, :, 1 - core],
            dst_ref=core_recv.at[pl.ds(half * 4, 4)],
            send_sem=core_ssem.at[half], recv_sem=core_rsem.at[half],
            device_id=sibling, device_id_type=MESH,
        )

    loads[1].wait()

    def widen(block, carry):
        signal[block, HOLD:, :] = jnp.zeros((TW + MAXOFF - HOLD, PB), F32)
        return carry

    lax.fori_loop(0, BLOCKS, widen, 0)
    for block in range(BLOCKS):
        signal[block, :HOLD, :] = hist[:, block * PB:(block + 1) * PB].astype(F32)
    trail[0] = jnp.zeros((TW, DB), F32)
    order_load.wait()
    loads[2].wait()

    wv[ENTRIES] = jnp.zeros((PB, DB), BF16)

    def far_pair(p):
        windows, blocks = [], []
        for u in range(2):
            entry = jnp.clip(order[0, 2 * p + u], 0, ENTRIES)
            k = jnp.minimum(lax.shift_right_logical(entry, 4), K_DEV - 1)
            block = jnp.bitwise_and(entry, BLOCKS - 1)
            windows.append(signal[block, pl.ds(delay_ref[k, block], TW), :].astype(BF16))
            blocks.append(wv[jnp.where(entry < ENTRIES, block * K_DEV + k, ENTRIES)])
        term = jnp.dot(
            jnp.concatenate(windows, axis=1), jnp.concatenate(blocks, axis=0),
            preferred_element_type=F32)
        trail[p + 1] = term + trail[jnp.where(order[2, p] > 0, 0, p)]

    def far_pairs(first, amount):
        def chunk(i, carry):
            for u in range(2):
                far_pair(first + i * 2 + u)
            return carry
        lax.fori_loop(0, amount // 2, chunk, 0)

    def far_collect():
        for j in range(TARGETS):
            end = jnp.clip(order[1, j], 0, PAIRS)
            for quarter in range(4):
                found = trail[end, quarter * 128:(quarter + 1) * 128, :]
                part[j, quarter] = found.reshape(4, 2, ROWS, DB)

    far_pairs(0, 28)

    loads[3].wait()

    def plane_coefficients(xs, carry):
        for x in xs:
            code = codes[x]
            for index, values in enumerate(COEFFICIENTS):
                coef[index, x] = jnp.where(
                    code == 0, values[0],
                    jnp.where(code == 1, values[1], jnp.where(code == 2, values[2], values[3])),
                ).astype(F32)
        return carry

    over_planes(plane_coefficients, 0)
    cell = surf_ref[...]
    cell_row = lax.shift_right_arithmetic(cell, 7)
    cell_lane = jnp.bitwise_and(cell, CZ - 1)

    def build_onehot(i, carry):
        rows = lax.broadcasted_iota(jnp.int32, (32, SLOT), 0) + i * 32
        onehot[pl.ds(pl.multiple_of(i * 32, 32), 32), :] = jnp.where(
            rows == cell_row, 1.0, 0.0).astype(BF16)
        return carry

    lax.fori_loop(0, CX * CY // 32, build_onehot, 0)
    samp_send[...] = jnp.zeros_like(samp_send)
    spad[...] = jnp.zeros_like(spad)
    loads[4].wait()

    def leap(step):
        here_ref, other_ref = fields[step % 2], fields[1 - step % 2]
        last = step == STEPS - 1
        halo_wait_recv(step, (1, 2))

        def y_rows(xs, carry):
            rows = [(yrecv[step, 0, pl.ds(x, 1), :], yrecv[step, 1, pl.ds(x, 1), :]) for x in xs]
            for x, (low, high) in zip(xs, rows):
                here_ref[x + 1, LOW - 1:LOW, :] = low
                here_ref[x + 1, HIGH:HIGH + 1, :] = high
            return carry

        over_planes(y_rows, 0)
        z_low, z_high = zrecv[step, 0], zrecv[step, 1]

        def plane_step(xs, carry):
            planes = []
            for x in xs:
                here = here_ref[x + 1, LOW:HIGH, :]
                around = here_ref[x, LOW:HIGH, :] + here_ref[x + 2, LOW:HIGH, :]
                around = around + (
                    here_ref[x + 1, LOW - 1:HIGH - 1, :] + here_ref[x + 1, LOW + 1:HIGH + 1, :])
                below = jnp.where(
                    lane == 0, pltpu.roll(z_low, lax.rem(CZ - x, CZ), 1), pltpu.roll(here, 1, 1))
                above = jnp.where(
                    lane == CZ - 1, pltpu.roll(z_high, CZ - 1 - x, 1), pltpu.roll(here, CZ - 1, 1))
                around = around + (below + above)
                before = other_ref[x + 1, LOW:HIGH, :]
                planes.append(coef[0, x] * here + coef[1, x] * before + coef[2, x] * around)
            for x, new in zip(xs, planes):
                other_ref[x + 1, LOW:HIGH, :] = new
                rounded[pl.ds(pl.multiple_of(x * CY, CY), CY), :] = new.astype(BF16)
            if last:
                return carry
            return take_faces(step + 1, xs, planes, carry)

        def inner(i, carry):
            return plane_step([1 + i * 5 + u for u in range(5)], carry)

        carry = lax.fori_loop(
            0, (CX - 2) // 5, inner, 0 if last else (zero_plane, zero_plane))
        halo_wait_recv(step, (0,))
        if step > 0:
            halo_wait_send(step - 1, (0,))
        here_ref[0, LOW:HIGH, :] = xrecv[step, 0]
        here_ref[CX + 1, LOW:HIGH, :] = xrecv[step, 1]
        carry = plane_step([0, CX - 1], carry)
        if not last:
            zstage[step + 1, 0], zstage[step + 1, 1] = carry
            halo_start(step + 1)

    def sample(step):
        picked = lax.dot_general(
            rounded[...], onehot[...], (((0,), (0,)), ((), ())), preferred_element_type=F32)
        level = lax.broadcasted_iota(jnp.int32, (CZ, SLOT), 0)
        values = jnp.sum(jnp.where(level == cell_lane, picked, 0.0), axis=0, keepdims=True)
        samp_send[4 + step:5 + step, :] = values

    axes = (("z", "y"), ("y", "z"))

    def index_on(axis):
        return z if axis == "z" else y

    def ring_copy(half, stage, kind, way):
        axis = axes[half][stage]
        place_now = index_on(axis)
        step_to = 1 if way == 0 else 3
        chunk = lax.rem(place_now + (2 if kind == 0 else step_to), 4)
        part = pl.ds(0 if (kind == 1) == (way == 1) else 2, 2)
        if stage == 0:
            source, target = sums.at[half, chunk, part], ring1.at[half, kind, way]
        else:
            source, target = totals.at[half, chunk, part], ring2.at[half, kind, way]
        return pltpu.make_async_remote_copy(
            src_ref=source, dst_ref=target,
            send_sem=ring_send.at[half, stage, kind, way],
            recv_sem=ring_recv.at[half, stage, kind, way],
            device_id=ring_neighbour(axis, step_to), device_id_type=MESH,
        )

    def core_finish(half):
        core_copy(half).wait_recv()

        def add(i, carry):
            yy, zz = i // 4, lax.rem(i, 4)
            total = part[half * 4:half * 4 + 4, yy, zz, core] + core_recv[half * 4:half * 4 + 4, yy, zz]
            if half == 0:
                sums[0, zz, yy] = total
            else:
                sums[1, yy, zz] = total
            return carry

        lax.fori_loop(0, 16, add, 0)

    def ring_begin(half, stage):
        for kind in (0, 1):
            for way in (0, 1):
                ring_copy(half, stage, kind, way).start()

    def ring_forward(half, stage):
        held = sums if stage == 0 else totals
        arrived = ring1 if stage == 0 else ring2
        place_now = index_on(axes[half][stage])
        for way in (0, 1):
            ring_copy(half, stage, 0, way).wait_recv()
            chunk = lax.rem(place_now + (1 if way == 0 else 3), 4)
            first = 0 if way == 0 else 2
            held[half, chunk, first:first + 2] = (
                held[half, chunk, first:first + 2] + arrived[half, 0, way])
            ring_copy(half, stage, 2, way).start()

    def ring_end(half, stage):
        held = sums if stage == 0 else totals
        arrived = ring1 if stage == 0 else ring2
        place_now = index_on(axes[half][stage])
        for kind in (1, 2):
            for way in (0, 1):
                ring_copy(half, stage, kind, way).wait_recv()
        first = held[half, place_now, 0:2] + (arrived[half, 2, 0] + arrived[half, 1, 1])
        second = held[half, place_now, 2:4] + (arrived[half, 1, 0] + arrived[half, 2, 1])
        return first, second

    leap(0)
    sample(0)
    far_pairs(28, PAIRS - 28)
    far_collect()
    for half in range(2):
        core_copy(half).start()
    leap(1)
    sample(1)
    for half in range(2):
        core_finish(half)
        ring_begin(half, 0)
    leap(2)
    save_prev = pltpu.make_async_copy(
        field_b.at[pl.ds(1, CX), pl.ds(LOW, CY)], prev_ref, load_sem.at[5])
    save_prev.start()
    sample(2)
    for half in range(2):
        ring_forward(half, 0)
    leap(3)
    save_next = pltpu.make_async_copy(
        field_a.at[pl.ds(1, CX), pl.ds(LOW, CY)], next_ref, load_sem.at[6])
    save_next.start()
    sample(3)

    def samp_copy(offset):
        return pltpu.make_async_remote_copy(
            src_ref=samp_send, dst_ref=samp_all.at[gy],
            send_sem=samp_ssem.at[offset - 1], recv_sem=samp_rsem.at[offset - 1],
            device_id=(gx, lax.rem(gy + offset, NY_DEV), gz), device_id_type=MESH,
        )

    def samp_arrival(offset):
        return pltpu.make_async_remote_copy(
            src_ref=samp_send, dst_ref=samp_all.at[lax.rem(gy + NY_DEV - offset, NY_DEV)],
            send_sem=samp_ssem.at[offset - 1], recv_sem=samp_rsem.at[offset - 1],
            device_id=(gx, lax.rem(gy + offset, NY_DEV), gz), device_id_type=MESH,
        )

    for offset in range(1, NY_DEV):
        samp_copy(offset).start()
    samp_all[gy] = samp_send[...]
    for half in range(2):
        first, second = ring_end(half, 0)
        totals[half, 0:2] = first
        totals[half, 2:4] = second
        ring_begin(half, 1)
    for offset in range(1, NY_DEV):
        samp_arrival(offset).wait_recv()
    for brick in range(NY_DEV):
        for i in range(SLOT // PB):
            spad[brick * (SLOT // PB) + i, 32:40, :] = samp_all[brick, :, i * PB:(i + 1) * PB]

    row = lax.broadcasted_iota(jnp.int32, (8, PB), 0)

    def entry_rows(block, carry):
        for entry in range(K_DEV):
            offset = delay_ref[entry, block]
            target = dir_ref[entry, block]
            early = spad[block, pl.ds(offset + 4, 8), :]
            late = spad[block, pl.ds(offset, 8), :]
            pair = jnp.where(row < 4, early, late)
            pieces = []
            for i in range(TARGETS // 2):
                wanted = jnp.where(row < 4, 2 * i, 2 * i + 1)
                pieces.append(jnp.where(wanted == target, pair, 0.0))
            lhs[:, pl.ds(pl.multiple_of((block * K_DEV + entry) * PB, PB), PB)] = (
                jnp.concatenate(pieces, axis=0).astype(BF16))
        return carry

    lax.fori_loop(0, BLOCKS, entry_rows, 0)
    for half in range(2):
        ring_forward(half, 1)
    flat_weights = wv[:ENTRIES].reshape(BLOCKS * K_DEV * PB, DB)
    correction = jnp.dot(lhs[...], flat_weights, preferred_element_type=F32)
    corr_out[...] = correction

    def corr_copy(member):
        return pltpu.make_async_remote_copy(
            src_ref=corr_out, dst_ref=corr_in.at[member],
            send_sem=corr_ssem, recv_sem=corr_rsem.at[member],
            device_id=owner, device_id_type=MESH,
        )

    @pl.when(jnp.logical_not(is_owner))
    def _():
        corr_copy(group).start()

    for half in range(2):
        first, second = ring_end(half, 1)
        for j in range(4):
            columns = slice((half * 4 + j) * DB, (half * 4 + j + 1) * DB)
            far_ref[:, columns] = first[j] if j < 2 else second[j - 2]

    @pl.when(is_owner)
    def _():
        def arrive(member, total):
            corr_copy(member).wait_recv()
            return total + corr_in[member]

        total = lax.fori_loop(0, OWNERS - 1, arrive, corr_out[...])
        for j in range(TARGETS):
            piece = total[(j // 2) * 8:(j // 2) * 8 + 8, :]
            if j % 2 == 0:
                piece = pltpu.roll(piece, 4, 0)
            columns = slice(j * DB, (j + 1) * DB)
            far_ref[8:16, columns] = far_ref[8:16, columns] + jnp.where(row >= 4, piece, 0.0)

    for step in range(STEPS):
        halo_wait_send(step, (0, 1, 2) if step == STEPS - 1 else (1, 2))
    for half in range(2):
        core_copy(half).wait_send()
        for stage in range(2):
            for kind in range(3):
                for way in range(2):
                    ring_copy(half, stage, kind, way).wait_send()
    for offset in range(1, NY_DEV):
        samp_copy(offset).wait_send()

    @pl.when(jnp.logical_not(is_owner))
    def _():
        corr_copy(group).wait_send()

    save_prev.wait()
    save_next.wait()


def hall(dirs, delays, surf_index, now, old, code, history, weights):
    any_space = pl.BlockSpec(memory_space=pl.ANY)
    smem = pl.BlockSpec(memory_space=pltpu.SMEM)
    vmem = pl.BlockSpec(memory_space=pltpu.VMEM)
    dma = pltpu.SemaphoreType.DMA
    brick = jax.ShapeDtypeStruct((CX, CY, CZ), F32)
    return pl.pallas_call(
        hall_kernel,
        out_shape=(brick, brick, jax.ShapeDtypeStruct((ROWS, TARGETS * DB), F32)),
        in_specs=[smem, smem, vmem, vmem] + [any_space] * 5,
        out_specs=(any_space, any_space, vmem),
        scratch_shapes=[
            pltpu.VMEM((CX + 2, PADROWS, CZ), F32),
            pltpu.VMEM((CX + 2, PADROWS, CZ), F32),
            pltpu.VMEM((CX, CY, CZ), jnp.int32),
            pltpu.VMEM((3, CX, CY, CZ), F32),
            pltpu.VMEM((STEPS, 2, CX, CZ), F32),
            pltpu.VMEM((STEPS, 2, CY, CZ), F32),
            pltpu.VMEM((STEPS, 2, CY, CZ), F32),
            pltpu.VMEM((STEPS, 2, CX, CZ), F32),
            pltpu.VMEM((STEPS, 2, CY, CZ), F32),
            pltpu.VMEM((CX * CY, SLOT), BF16),
            pltpu.VMEM((CX * CY, CZ), BF16),
            pltpu.VMEM((8, SLOT), F32),
            pltpu.VMEM((NY_DEV, 8, SLOT), F32),
            pltpu.VMEM((BLOCKS, 48, PB), F32),
            pltpu.VMEM((32, BLOCKS * K_DEV * PB), BF16),
            pltpu.VMEM((ENTRIES + 1, PB, DB), BF16),
            pltpu.VMEM((BLOCKS, TW + MAXOFF, PB), F32),
            pltpu.VMEM((PAIRS + 1, TW, DB), F32),
            pltpu.VMEM((8, PB), jnp.int32),
            pltpu.SMEM((8, PB), jnp.int32),
            pltpu.VMEM((HOLD, BLOCKS * PB), BF16),
            pltpu.VMEM((TARGETS, 4, 4, 2, ROWS, DB), F32),
            pltpu.VMEM((TARGETS, 4, 4, ROWS, DB), F32),
            pltpu.VMEM((2, 4, 4, 4, ROWS, DB), F32),
            pltpu.VMEM((2, 4, 4, ROWS, DB), F32),
            pltpu.VMEM((2, 3, 2, 2, 4, ROWS, DB), F32),
            pltpu.VMEM((2, 3, 2, 2, ROWS, DB), F32),
            pltpu.VMEM((32, DB), F32),
            pltpu.VMEM((OWNERS, 32, DB), F32),
            dma((8,)),
            dma((STEPS, 3, 2)), dma((STEPS, 3, 2)),
            dma((3,)), dma((3,)),
            dma((2,)), dma((2,)),
            dma((2, 2, 3, 2)), dma((2, 2, 3, 2)),
            dma, dma((OWNERS,)),
        ],
        compiler_params=pltpu.CompilerParams(
            collective_id=0, has_side_effects=True, vmem_limit_bytes=58 * 1024 * 1024),
    )(dirs, delays, dirs, surf_index, history, now, old, code, weights)


def save_kernel(*refs):
    sources, targets, held, sems = refs[:3], refs[3:6], refs[6:9], refs[9]
    arrivals = [pltpu.make_async_copy(sources[i], held[i], sems.at[0, i]) for i in range(3)]
    leaves = [pltpu.make_async_copy(held[i], targets[i], sems.at[1, i]) for i in range(3)]
    for copy in arrivals:
        copy.start()
    for arrival, leave in zip(arrivals, leaves):
        arrival.wait()
        leave.start()
    for copy in leaves:
        copy.wait()


def save(arrays):
    any_space = pl.BlockSpec(memory_space=pl.ANY)
    return pl.pallas_call(
        save_kernel,
        out_shape=tuple(jax.ShapeDtypeStruct(a.shape, a.dtype) for a in arrays),
        in_specs=[any_space] * 3,
        out_specs=(any_space,) * 3,
        scratch_shapes=[pltpu.VMEM(a.shape, a.dtype) for a in arrays]
        + [pltpu.SemaphoreType.DMA((2, 3))],
    )(*arrays)


def shards(pressure_now, pressure_old, cell_code, surf_index, history, dir_slot, delay, weights):
    flat_weights = weights.reshape(BLOCKS * K_DEV, PB, DB)
    return save(hall(
        dir_slot.T, delay.T, surf_index, pressure_now, pressure_old, cell_code, history,
        flat_weights))


def solution(mesh):
    return jax.shard_map(
        shards,
        mesh=mesh,
        in_specs=(
            P("gx", "gy", "gz"),
            P("gx", "gy", "gz"),
            P("gx", "gy", "gz"),
            P(("gx", "gz"), "gy"),
            P(None, ("gx", "gz")),
            P(("gx", "gz"), "gy"),
            P(("gx", "gz"), "gy"),
            P(("gx", "gz"), "gy", None, None),
        ),
        out_specs=(P("gx", "gy", "gz"), P("gx", "gy", "gz"), P(("gx", "gz"), "gy")),
        check_vma=False,
    )
```

```python
import functools

import jax
import jax.numpy as jnp
import numpy as np
from jax import lax
from jax.experimental import pallas as pl
from jax.experimental.pallas import tpu as pltpu
from jax.sharding import PartitionSpec as P

MESH = pl.DeviceIdType.MESH
F32 = jnp.float32
BF16 = jnp.bfloat16

STEPS = 4
CX, CY, CZ = 32, 32, 128
SLOT = 512
TW = 512
MAXOFF = 32
HOLD = 540
PB = 128
DB = 128
K_DEV = 6
BLOCKS = 16
ENTRIES = K_DEV * BLOCKS
PAIRS = ENTRIES // 2 + 4
TARGETS = 8
OWNERS = 32
ROWS = 16
NX_DEV, NY_DEV, NZ_DEV = 8, 4, 4
LOW, HIGH = 8, 40
PADROWS = 48


def coefficient_table():
    speeds = np.array([0.32, 0.26, 0.19, 0.11], np.float32).astype(np.float64)
    damping = np.array([0.0, 0.02, 0.08, 0.3], np.float32).astype(np.float64)
    here = (2.0 - 6.0 * speeds) / (1.0 + damping)
    before = -(1.0 - damping) / (1.0 + damping)
    around = speeds / (1.0 + damping)
    return [[float(np.float32(v)) for v in row] for row in (here, before, around)]


COEFFICIENTS = coefficient_table()


def hall_kernel(
    dir_ref, delay_ref, dirs_ref, surf_ref, hist_ref, now_ref, old_ref, code_ref, w_ref,
    next_ref, prev_ref, far_ref,
    field_a, field_b, codes, coef, ystage, zstage, xrecv, yrecv, zrecv,
    onehot, rounded, samp_send, samp_all, spad, lhs, wv,
    signal, trail, table, order, hist, part, core_recv, sums, totals, ring1, ring2, corr_out, corr_in,
    load_sem, halo_send, halo_recv, samp_ssem, samp_rsem,
    core_ssem, core_rsem, ring_send, ring_recv, corr_ssem, corr_rsem,
):
    fields = (field_a, field_b)
    gx, gy, gz = lax.axis_index("gx"), lax.axis_index("gy"), lax.axis_index("gz")
    y, z_hi = gx // 2, lax.rem(gx, 2)
    z_lo, core = gz // 2, lax.rem(gz, 2)
    z = z_hi * 2 + z_lo
    group = gx * 4 + gz
    is_owner = group == OWNERS - 1

    def place(yy, zz):
        return (yy * 2 + zz // 2, gy, lax.rem(zz, 2) * 2 + core)

    def ring_neighbour(axis, offset):
        if axis == "z":
            return place(y, lax.rem(z + offset, 4))
        return place(lax.rem(y + offset, 4), z)

    sibling = (gx, gy, z_lo * 2 + 1 - core)
    owner = (NX_DEV - 1, gy, NZ_DEV - 1)
    coords = (gx, gy, gz)
    extents = (NX_DEV, NY_DEV, NZ_DEV)

    def beside(axis, side):
        moved = list(coords)
        moved[axis] = coords[axis] + (1 if side else -1)
        return tuple(moved)

    def exists(axis, side):
        return coords[axis] < extents[axis] - 1 if side else coords[axis] > 0

    barrier = pltpu.get_barrier_semaphore()

    def greet(device):
        pl.semaphore_signal(barrier, inc=1, device_id=device, device_id_type=MESH)

    expected = jnp.int32(8)
    for axis in range(3):
        for side in range(2):
            @pl.when(exists(axis, side))
            def _():
                greet(beside(axis, side))
            expected = expected + exists(axis, side).astype(jnp.int32)
    greet(sibling)
    for axis in ("y", "z"):
        for offset in (1, 3):
            greet(ring_neighbour(axis, offset))
    for offset in range(1, NY_DEV):
        greet((gx, lax.rem(gy + offset, NY_DEV), gz))

    @pl.when(is_owner)
    def _():
        def greet_one(member, carry):
            greet((member // 4, gy, lax.rem(member, 4)))
            return carry
        lax.fori_loop(0, OWNERS - 1, greet_one, 0)

    expected = expected + jnp.where(is_owner, 0, 1)

    loads = [
        pltpu.make_async_copy(now_ref, field_a.at[pl.ds(1, CX), pl.ds(LOW, CY)], load_sem.at[0]),
        pltpu.make_async_copy(hist_ref, hist, load_sem.at[3]),
        pltpu.make_async_copy(w_ref, wv.at[pl.ds(0, ENTRIES)], load_sem.at[4]),
        pltpu.make_async_copy(code_ref, codes, load_sem.at[2]),
        pltpu.make_async_copy(old_ref, field_b.at[pl.ds(1, CX), pl.ds(LOW, CY)], load_sem.at[1]),
    ]
    for load in loads:
        load.start()

    lane = lax.broadcasted_iota(jnp.int32, (CY, CZ), 1)
    zero_plane = jnp.zeros((CY, CZ), F32)

    def over_planes(body, init, unroll=8):
        def chunk(i, carry):
            return body([i * unroll + u for u in range(unroll)], carry)
        return lax.fori_loop(0, CX // unroll, chunk, init)

    def take_faces(step, xs, planes, carry):
        low, high = carry
        for x, plane in zip(xs, planes):
            low = jnp.where(lane == x, pltpu.roll(plane, x, 1), low)
            high = jnp.where(lane == x, pltpu.roll(plane, x + 1, 1), high)
        for x, plane in zip(xs, planes):
            ystage[step, 0, pl.ds(x, 1), :] = plane[0:1, :]
            ystage[step, 1, pl.ds(x, 1), :] = plane[CY - 1:CY, :]
        return low, high

    def halo_copy(step, axis, side):
        current = step % 2
        if axis == 0:
            source = fields[current].at[CX if side else 1, pl.ds(LOW, CY)]
            target = xrecv.at[step, 1 - side]
        elif axis == 1:
            source, target = ystage.at[step, side], yrecv.at[step, 1 - side]
        else:
            source, target = zstage.at[step, side], zrecv.at[step, 1 - side]
        return pltpu.make_async_remote_copy(
            src_ref=source, dst_ref=target,
            send_sem=halo_send.at[step, axis, side],
            recv_sem=halo_recv.at[step, axis, 1 - side],
            device_id=beside(axis, side), device_id_type=MESH,
        )

    def halo_start(step):
        for axis in range(3):
            for side in range(2):
                @pl.when(exists(axis, side))
                def _():
                    halo_copy(step, axis, side).start()

    def halo_wait_send(step, axes=(0, 1, 2)):
        for axis in axes:
            for side in range(2):
                @pl.when(exists(axis, side))
                def _():
                    halo_copy(step, axis, side).wait_send()

    def halo_wait_recv(step, axes):
        for axis in axes:
            buffer = (xrecv, yrecv, zrecv)[axis]
            for side in range(2):
                @pl.when(exists(axis, side))
                def _():
                    halo_copy(step, axis, 1 - side).wait_recv()
                @pl.when(jnp.logical_not(exists(axis, side)))
                def _():
                    buffer[step, side] = zero_plane

    loads[0].wait()

    def first_faces(xs, carry):
        return take_faces(0, xs, [field_a[x + 1, LOW:HIGH, :] for x in xs], carry)

    low, high = over_planes(first_faces, (zero_plane, zero_plane))
    zstage[0, 0] = low
    zstage[0, 1] = high

    pl.semaphore_wait(barrier, expected)
    halo_start(0)

    dirs = dirs_ref[...]
    targets = jnp.concatenate(
        [dirs[k:k + 1, :] for k in range(K_DEV)]
        + [jnp.full((1, PB - ENTRIES), -1, jnp.int32)], axis=1)
    targets = jnp.where(targets >= 0, targets, TARGETS).astype(F32)
    by_lane = jnp.broadcast_to(targets, (PB, PB))
    by_row = by_lane.T
    lanes = lax.broadcasted_iota(jnp.int32, (PB, PB), 1).astype(F32)
    rows = lax.broadcasted_iota(jnp.int32, (PB, PB), 0).astype(F32)

    def count(mask, axis):
        return jnp.sum(jnp.where(mask, 1.0, 0.0), axis=axis, keepdims=True)

    def even(amount):
        return 2.0 * jnp.floor(0.5 * (amount + 1.0))

    member = by_row == lanes
    along_lanes = count(member, 0)
    along_rows = count(by_lane == rows, 1)
    first_lanes = jnp.sum(jnp.where(rows < lanes, even(along_rows), 0.0), axis=0, keepdims=True)
    first_rows = jnp.sum(jnp.where(lanes < rows, even(along_lanes), 0.0), axis=1, keepdims=True)
    before = count(jnp.logical_and(by_lane == by_row, lanes < rows), 1)
    slot = before + jnp.sum(jnp.where(member, first_lanes, 0.0), axis=1, keepdims=True)
    taken = jnp.logical_and(slot == lanes, by_row < TARGETS)
    sequence = ENTRIES + jnp.sum(jnp.where(taken, rows - ENTRIES, 0.0), axis=0, keepdims=True)
    ends = jnp.where(along_lanes > 0, 0.5 * (first_lanes + even(along_lanes)), 0.0)
    opens = count(
        jnp.logical_and(jnp.logical_and(0.5 * first_rows == lanes, along_rows > 0), rows < TARGETS), 0)
    table[0:1, :] = sequence.astype(jnp.int32)
    table[1:2, :] = ends.astype(jnp.int32)
    table[2:3, :] = opens.astype(jnp.int32)
    table[3:8, :] = jnp.zeros((5, PB), jnp.int32)
    order_load = pltpu.make_async_copy(table, order, load_sem.at[7])
    order_load.start()

    def core_copy(half):
        return pltpu.make_async_remote_copy(
            src_ref=part.at[pl.ds(half * 4, 4), :, :, 1 - core],
            dst_ref=core_recv.at[pl.ds(half * 4, 4)],
            send_sem=core_ssem.at[half], recv_sem=core_rsem.at[half],
            device_id=sibling, device_id_type=MESH,
        )

    loads[1].wait()

    def widen(block, carry):
        signal[block, HOLD:, :] = jnp.zeros((TW + MAXOFF - HOLD, PB), F32)
        return carry

    lax.fori_loop(0, BLOCKS, widen, 0)
    for block in range(BLOCKS):
        signal[block, :HOLD, :] = hist[:, block * PB:(block + 1) * PB].astype(F32)
    trail[0] = jnp.zeros((TW, DB), F32)
    order_load.wait()
    loads[2].wait()

    wv[ENTRIES] = jnp.zeros((PB, DB), BF16)

    def far_pair(p):
        windows, blocks = [], []
        for u in range(2):
            entry = jnp.clip(order[0, 2 * p + u], 0, ENTRIES)
            k = jnp.minimum(lax.shift_right_logical(entry, 4), K_DEV - 1)
            block = jnp.bitwise_and(entry, BLOCKS - 1)
            windows.append(signal[block, pl.ds(delay_ref[k, block], TW), :].astype(BF16))
            blocks.append(wv[jnp.where(entry < ENTRIES, block * K_DEV + k, ENTRIES)])
        term = jnp.dot(
            jnp.concatenate(windows, axis=1), jnp.concatenate(blocks, axis=0),
            preferred_element_type=F32)
        trail[p + 1] = term + trail[jnp.where(order[2, p] > 0, 0, p)]

    def far_pairs(first, amount, unroll):
        def chunk(i, carry):
            for u in range(unroll):
                far_pair(first + i * unroll + u)
            return carry
        lax.fori_loop(0, amount // unroll, chunk, 0)

    def far_collect():
        for j in range(TARGETS):
            end = jnp.clip(order[1, j], 0, PAIRS)
            for quarter in range(4):
                found = trail[end, quarter * 128:(quarter + 1) * 128, :]
                part[j, quarter] = found.reshape(4, 2, ROWS, DB)

    def core_start():
        far_collect()
        for half in range(2):
            core_copy(half).start()

    loads[3].wait()

    def plane_coefficients(xs, carry):
        for x in xs:
            code = codes[x]
            for index, values in enumerate(COEFFICIENTS):
                coef[index, x] = jnp.where(
                    code == 0, values[0],
                    jnp.where(code == 1, values[1], jnp.where(code == 2, values[2], values[3])),
                ).astype(F32)
        return carry

    over_planes(plane_coefficients, 0)
    cell = surf_ref[...]
    cell_row = lax.shift_right_arithmetic(cell, 7)
    cell_lane = jnp.bitwise_and(cell, CZ - 1)

    def build_onehot(i, carry):
        rows = lax.broadcasted_iota(jnp.int32, (128, SLOT), 0) + i * 128
        onehot[pl.ds(pl.multiple_of(i * 128, 128), 128), :] = jnp.where(
            rows == cell_row, 1.0, 0.0).astype(BF16)
        return carry

    lax.fori_loop(0, CX * CY // 128, build_onehot, 0)
    samp_send[...] = jnp.zeros_like(samp_send)
    spad[...] = jnp.zeros_like(spad)
    loads[4].wait()

    def leap(step):
        here_ref, other_ref = fields[step % 2], fields[1 - step % 2]
        last = step == STEPS - 1
        halo_wait_recv(step, (1, 2))

        def y_rows(xs, carry):
            rows = [(yrecv[step, 0, pl.ds(x, 1), :], yrecv[step, 1, pl.ds(x, 1), :]) for x in xs]
            for x, (low, high) in zip(xs, rows):
                here_ref[x + 1, LOW - 1:LOW, :] = low
                here_ref[x + 1, HIGH:HIGH + 1, :] = high
            return carry

        over_planes(y_rows, 0, 16)
        z_low, z_high = zrecv[step, 0], zrecv[step, 1]

        def plane_step(xs, carry):
            planes = []
            for x in xs:
                here = here_ref[x + 1, LOW:HIGH, :]
                around = here_ref[x, LOW:HIGH, :] + here_ref[x + 2, LOW:HIGH, :]
                around = around + (
                    here_ref[x + 1, LOW - 1:HIGH - 1, :] + here_ref[x + 1, LOW + 1:HIGH + 1, :])
                below = jnp.where(
                    lane == 0, pltpu.roll(z_low, lax.rem(CZ - x, CZ), 1), pltpu.roll(here, 1, 1))
                above = jnp.where(
                    lane == CZ - 1, pltpu.roll(z_high, CZ - 1 - x, 1), pltpu.roll(here, CZ - 1, 1))
                around = around + (below + above)
                before = other_ref[x + 1, LOW:HIGH, :]
                planes.append(coef[0, x] * here + coef[1, x] * before + coef[2, x] * around)
            for x, new in zip(xs, planes):
                other_ref[x + 1, LOW:HIGH, :] = new
                rounded[pl.ds(pl.multiple_of(x * CY, CY), CY), :] = new.astype(BF16)
            if last:
                return carry
            return take_faces(step + 1, xs, planes, carry)

        def inner(i, carry):
            return plane_step([1 + i * 10 + u for u in range(10)], carry)

        carry = lax.fori_loop(
            0, (CX - 2) // 10, inner, 0 if last else (zero_plane, zero_plane))
        halo_wait_recv(step, (0,))
        if step > 0:
            halo_wait_send(step - 1, (0,))
        here_ref[0, LOW:HIGH, :] = xrecv[step, 0]
        here_ref[CX + 1, LOW:HIGH, :] = xrecv[step, 1]
        carry = plane_step([0, CX - 1], carry)
        if not last:
            zstage[step + 1, 0], zstage[step + 1, 1] = carry
            halo_start(step + 1)

    def sample(step):
        picked = lax.dot_general(
            rounded[...], onehot[...], (((0,), (0,)), ((), ())), preferred_element_type=F32)
        level = lax.broadcasted_iota(jnp.int32, (CZ, SLOT), 0)
        values = jnp.sum(jnp.where(level == cell_lane, picked, 0.0), axis=0, keepdims=True)
        samp_send[4 + step:5 + step, :] = values

    axes = (("z", "y"), ("y", "z"))

    def index_on(axis):
        return z if axis == "z" else y

    def ring_copy(half, stage, kind, way):
        axis = axes[half][stage]
        place_now = index_on(axis)
        step_to = 1 if way == 0 else 3
        chunk = lax.rem(place_now + (2 if kind == 0 else step_to), 4)
        part = pl.ds(0 if (kind == 1) == (way == 1) else 2, 2)
        if stage == 0:
            source, target = sums.at[half, chunk, part], ring1.at[half, kind, way]
        else:
            source, target = totals.at[half, chunk, part], ring2.at[half, kind, way]
        return pltpu.make_async_remote_copy(
            src_ref=source, dst_ref=target,
            send_sem=ring_send.at[half, stage, kind, way],
            recv_sem=ring_recv.at[half, stage, kind, way],
            device_id=ring_neighbour(axis, step_to), device_id_type=MESH,
        )

    def core_finish(half):
        core_copy(half).wait_recv()

        for yy in range(4):
            for zz in range(4):
                total = (part[half * 4:half * 4 + 4, yy, zz, core]
                         + core_recv[half * 4:half * 4 + 4, yy, zz])
                if half == 0:
                    sums[0, zz, yy] = total
                else:
                    sums[1, yy, zz] = total

    def ring_begin(half, stage):
        for kind in (0, 1):
            for way in (0, 1):
                ring_copy(half, stage, kind, way).start()

    def ring_forward(half, stage):
        held = sums if stage == 0 else totals
        arrived = ring1 if stage == 0 else ring2
        place_now = index_on(axes[half][stage])
        for way in (0, 1):
            ring_copy(half, stage, 0, way).wait_recv()
            chunk = lax.rem(place_now + (1 if way == 0 else 3), 4)
            first = 0 if way == 0 else 2
            held[half, chunk, first:first + 2] = (
                held[half, chunk, first:first + 2] + arrived[half, 0, way])
            ring_copy(half, stage, 2, way).start()

    def ring_end(half, stage):
        held = sums if stage == 0 else totals
        arrived = ring1 if stage == 0 else ring2
        place_now = index_on(axes[half][stage])
        for kind in (1, 2):
            for way in (0, 1):
                ring_copy(half, stage, kind, way).wait_recv()
        first = held[half, place_now, 0:2] + (arrived[half, 2, 0] + arrived[half, 1, 1])
        second = held[half, place_now, 2:4] + (arrived[half, 1, 0] + arrived[half, 2, 1])
        return first, second

    far_pairs(0, 28, 14)
    leap(0)
    sample(0)
    far_pairs(28, PAIRS - 28, 12)
    core_start()
    leap(1)
    sample(1)
    for half in range(2):
        core_finish(half)
        ring_begin(half, 0)
    leap(2)
    save_prev = pltpu.make_async_copy(
        field_b.at[pl.ds(1, CX), pl.ds(LOW, CY)], prev_ref, load_sem.at[5])
    save_prev.start()
    sample(2)
    for half in range(2):
        ring_forward(half, 0)
    leap(3)
    save_next = pltpu.make_async_copy(
        field_a.at[pl.ds(1, CX), pl.ds(LOW, CY)], next_ref, load_sem.at[6])
    save_next.start()
    sample(3)

    def samp_copy(offset):
        return pltpu.make_async_remote_copy(
            src_ref=samp_send, dst_ref=samp_all.at[gy],
            send_sem=samp_ssem.at[offset - 1], recv_sem=samp_rsem.at[offset - 1],
            device_id=(gx, lax.rem(gy + offset, NY_DEV), gz), device_id_type=MESH,
        )

    def samp_arrival(offset):
        return pltpu.make_async_remote_copy(
            src_ref=samp_send, dst_ref=samp_all.at[lax.rem(gy + NY_DEV - offset, NY_DEV)],
            send_sem=samp_ssem.at[offset - 1], recv_sem=samp_rsem.at[offset - 1],
            device_id=(gx, lax.rem(gy + offset, NY_DEV), gz), device_id_type=MESH,
        )

    for offset in range(1, NY_DEV):
        samp_copy(offset).start()
    samp_all[gy] = samp_send[...]
    for half in range(2):
        first, second = ring_end(half, 0)
        totals[half, 0:2] = first
        totals[half, 2:4] = second
        ring_begin(half, 1)
    for offset in range(1, NY_DEV):
        samp_arrival(offset).wait_recv()
    for brick in range(NY_DEV):
        for i in range(SLOT // PB):
            spad[brick * (SLOT // PB) + i, 32:40, :] = samp_all[brick, :, i * PB:(i + 1) * PB]

    row = lax.broadcasted_iota(jnp.int32, (8, PB), 0)

    def entry_rows(i, carry):
        held = []
        for block in [i * 4 + u for u in range(4)]:
            for entry in range(K_DEV):
                offset = delay_ref[entry, block]
                target = dir_ref[entry, block]
                early = spad[block, pl.ds(offset + 4, 8), :]
                late = spad[block, pl.ds(offset, 8), :]
                pair = jnp.where(row < 4, early, late)
                pieces = []
                for k in range(TARGETS // 2):
                    wanted = jnp.where(row < 4, 2 * k, 2 * k + 1)
                    pieces.append(jnp.where(wanted == target, pair, 0.0))
                held.append(jnp.concatenate(pieces, axis=0).astype(BF16))
        width = 4 * K_DEV * PB
        lhs[:, pl.ds(pl.multiple_of(i * width, width), width)] = jnp.concatenate(held, axis=1)
        return carry

    lax.fori_loop(0, BLOCKS // 4, entry_rows, 0)
    for half in range(2):
        ring_forward(half, 1)
    flat_weights = wv[:ENTRIES].reshape(BLOCKS * K_DEV * PB, DB)
    correction = jnp.dot(lhs[...], flat_weights, preferred_element_type=F32)
    corr_out[...] = correction

    def corr_copy(member):
        return pltpu.make_async_remote_copy(
            src_ref=corr_out, dst_ref=corr_in.at[member],
            send_sem=corr_ssem, recv_sem=corr_rsem.at[member],
            device_id=owner, device_id_type=MESH,
        )

    @pl.when(jnp.logical_not(is_owner))
    def _():
        corr_copy(group).start()

    for half in range(2):
        first, second = ring_end(half, 1)
        for j in range(4):
            columns = slice((half * 4 + j) * DB, (half * 4 + j + 1) * DB)
            far_ref[:, columns] = first[j] if j < 2 else second[j - 2]

    @pl.when(is_owner)
    def _():
        def arrive(member, carry):
            corr_copy(member).wait_recv()
            return carry

        lax.fori_loop(0, OWNERS - 1, arrive, 0)
        total = corr_out[...]
        for member in range(OWNERS - 1):
            total = total + corr_in[member]
        for j in range(TARGETS):
            piece = total[(j // 2) * 8:(j // 2) * 8 + 8, :]
            if j % 2 == 0:
                piece = pltpu.roll(piece, 4, 0)
            columns = slice(j * DB, (j + 1) * DB)
            far_ref[8:16, columns] = far_ref[8:16, columns] + jnp.where(row >= 4, piece, 0.0)

    for step in range(STEPS):
        halo_wait_send(step, (0, 1, 2) if step == STEPS - 1 else (1, 2))
    for half in range(2):
        core_copy(half).wait_send()
        for stage in range(2):
            for kind in range(3):
                for way in range(2):
                    ring_copy(half, stage, kind, way).wait_send()
    for offset in range(1, NY_DEV):
        samp_copy(offset).wait_send()

    @pl.when(jnp.logical_not(is_owner))
    def _():
        corr_copy(group).wait_send()

    save_prev.wait()
    save_next.wait()


def hall(dirs, delays, surf_index, now, old, code, history, weights):
    any_space = pl.BlockSpec(memory_space=pl.ANY)
    smem = pl.BlockSpec(memory_space=pltpu.SMEM)
    vmem = pl.BlockSpec(memory_space=pltpu.VMEM)
    dma = pltpu.SemaphoreType.DMA
    brick = jax.ShapeDtypeStruct((CX, CY, CZ), F32)
    return pl.pallas_call(
        hall_kernel,
        out_shape=(brick, brick, jax.ShapeDtypeStruct((ROWS, TARGETS * DB), F32)),
        in_specs=[smem, smem, vmem, vmem] + [any_space] * 5,
        out_specs=(any_space, any_space, vmem),
        scratch_shapes=[
            pltpu.VMEM((CX + 2, PADROWS, CZ), F32),
            pltpu.VMEM((CX + 2, PADROWS, CZ), F32),
            pltpu.VMEM((CX, CY, CZ), jnp.int32),
            pltpu.VMEM((3, CX, CY, CZ), F32),
            pltpu.VMEM((STEPS, 2, CX, CZ), F32),
            pltpu.VMEM((STEPS, 2, CY, CZ), F32),
            pltpu.VMEM((STEPS, 2, CY, CZ), F32),
            pltpu.VMEM((STEPS, 2, CX, CZ), F32),
            pltpu.VMEM((STEPS, 2, CY, CZ), F32),
            pltpu.VMEM((CX * CY, SLOT), BF16),
            pltpu.VMEM((CX * CY, CZ), BF16),
            pltpu.VMEM((8, SLOT), F32),
            pltpu.VMEM((NY_DEV, 8, SLOT), F32),
            pltpu.VMEM((BLOCKS, 48, PB), F32),
            pltpu.VMEM((32, BLOCKS * K_DEV * PB), BF16),
            pltpu.VMEM((ENTRIES + 1, PB, DB), BF16),
            pltpu.VMEM((BLOCKS, TW + MAXOFF, PB), F32),
            pltpu.VMEM((PAIRS + 1, TW, DB), F32),
            pltpu.VMEM((8, PB), jnp.int32),
            pltpu.SMEM((8, PB), jnp.int32),
            pltpu.VMEM((HOLD, BLOCKS * PB), BF16),
            pltpu.VMEM((TARGETS, 4, 4, 2, ROWS, DB), F32),
            pltpu.VMEM((TARGETS, 4, 4, ROWS, DB), F32),
            pltpu.VMEM((2, 4, 4, 4, ROWS, DB), F32),
            pltpu.VMEM((2, 4, 4, ROWS, DB), F32),
            pltpu.VMEM((2, 3, 2, 2, 4, ROWS, DB), F32),
            pltpu.VMEM((2, 3, 2, 2, ROWS, DB), F32),
            pltpu.VMEM((32, DB), F32),
            pltpu.VMEM((OWNERS, 32, DB), F32),
            dma((8,)),
            dma((STEPS, 3, 2)), dma((STEPS, 3, 2)),
            dma((3,)), dma((3,)),
            dma((2,)), dma((2,)),
            dma((2, 2, 3, 2)), dma((2, 2, 3, 2)),
            dma, dma((OWNERS,)),
        ],
        compiler_params=pltpu.CompilerParams(
            collective_id=0, has_side_effects=True, vmem_limit_bytes=58 * 1024 * 1024),
    )(dirs, delays, dirs, surf_index, history, now, old, code, weights)


def save_kernel(*refs):
    sources, targets, held, sems = refs[:3], refs[3:6], refs[6:9], refs[9]
    arrivals = [pltpu.make_async_copy(sources[i], held[i], sems.at[0, i]) for i in range(3)]
    leaves = [pltpu.make_async_copy(held[i], targets[i], sems.at[1, i]) for i in range(3)]
    for copy in arrivals:
        copy.start()
    for arrival, leave in zip(arrivals, leaves):
        arrival.wait()
        leave.start()
    for copy in leaves:
        copy.wait()


def save(arrays):
    any_space = pl.BlockSpec(memory_space=pl.ANY)
    return pl.pallas_call(
        save_kernel,
        out_shape=tuple(jax.ShapeDtypeStruct(a.shape, a.dtype) for a in arrays),
        in_specs=[any_space] * 3,
        out_specs=(any_space,) * 3,
        scratch_shapes=[pltpu.VMEM(a.shape, a.dtype) for a in arrays]
        + [pltpu.SemaphoreType.DMA((2, 3))],
    )(*arrays)


def shards(pressure_now, pressure_old, cell_code, surf_index, history, dir_slot, delay, weights):
    flat_weights = weights.reshape(BLOCKS * K_DEV, PB, DB)
    return save(hall(
        dir_slot.T, delay.T, surf_index, pressure_now, pressure_old, cell_code, history,
        flat_weights))


def solution(mesh):
    return jax.shard_map(
        shards,
        mesh=mesh,
        in_specs=(
            P("gx", "gy", "gz"),
            P("gx", "gy", "gz"),
            P("gx", "gy", "gz"),
            P(("gx", "gz"), "gy"),
            P(None, ("gx", "gz")),
            P(("gx", "gz"), "gy"),
            P(("gx", "gz"), "gy"),
            P(("gx", "gz"), "gy", None, None),
        ),
        out_specs=(P("gx", "gy", "gz"), P("gx", "gy", "gz"), P(("gx", "gz"), "gy")),
        check_vma=False,
    )
```

```python
import functools

import jax
import jax.numpy as jnp
import numpy as np
from jax import lax
from jax.experimental import pallas as pl
from jax.experimental.pallas import tpu as pltpu
from jax.sharding import PartitionSpec as P

MESH = pl.DeviceIdType.MESH
F32 = jnp.float32
BF16 = jnp.bfloat16

STEPS = 4
CX, CY, CZ = 32, 32, 128
SLOT = 512
TW = 512
MAXOFF = 32
HOLD = 540
PB = 128
DB = 128
K_DEV = 6
BLOCKS = 16
ENTRIES = K_DEV * BLOCKS
PAIRS = ENTRIES // 2 + 4
TARGETS = 8
OWNERS = 32
ROWS = 16
NX_DEV, NY_DEV, NZ_DEV = 8, 4, 4
LOW, HIGH = 8, 40
PADROWS = 48


def coefficient_table():
    speeds = np.array([0.32, 0.26, 0.19, 0.11], np.float32).astype(np.float64)
    damping = np.array([0.0, 0.02, 0.08, 0.3], np.float32).astype(np.float64)
    here = (2.0 - 6.0 * speeds) / (1.0 + damping)
    before = -(1.0 - damping) / (1.0 + damping)
    around = speeds / (1.0 + damping)
    return [[float(np.float32(v)) for v in row] for row in (here, before, around)]


COEFFICIENTS = coefficient_table()


def hall_kernel(
    dir_ref, delay_ref, dirs_ref, surf_ref, hist_ref, now_ref, old_ref, code_ref, w_ref,
    next_ref, prev_ref, far_ref,
    field_a, field_b, codes, coef, ystage, zstage, xrecv, yrecv, zrecv,
    onehot, rounded, samp_send, samp_all, last_send, last_all, spad, lhs, last_lhs, wv,
    signal, trail, table, order, hist, part, core_recv, sums, totals, ring1, ring2, corr_out, corr_in, last_out, last_in,
    load_sem, halo_send, halo_recv, samp_ssem, samp_rsem,
    core_ssem, core_rsem, ring_send, ring_recv, corr_ssem, corr_rsem, last_ssem, last_rsem,
):
    fields = (field_a, field_b)
    gx, gy, gz = lax.axis_index("gx"), lax.axis_index("gy"), lax.axis_index("gz")
    y, z_hi = gx // 2, lax.rem(gx, 2)
    z_lo, core = gz // 2, lax.rem(gz, 2)
    z = z_hi * 2 + z_lo
    group = gx * 4 + gz
    is_owner = group == OWNERS - 1

    def place(yy, zz):
        return (yy * 2 + zz // 2, gy, lax.rem(zz, 2) * 2 + core)

    def ring_neighbour(axis, offset):
        if axis == "z":
            return place(y, lax.rem(z + offset, 4))
        return place(lax.rem(y + offset, 4), z)

    sibling = (gx, gy, z_lo * 2 + 1 - core)
    owner = (NX_DEV - 1, gy, NZ_DEV - 1)
    coords = (gx, gy, gz)
    extents = (NX_DEV, NY_DEV, NZ_DEV)

    def beside(axis, side):
        moved = list(coords)
        moved[axis] = coords[axis] + (1 if side else -1)
        return tuple(moved)

    def exists(axis, side):
        return coords[axis] < extents[axis] - 1 if side else coords[axis] > 0

    barrier = pltpu.get_barrier_semaphore()

    def greet(device):
        pl.semaphore_signal(barrier, inc=1, device_id=device, device_id_type=MESH)

    expected = jnp.int32(8)
    for axis in range(3):
        for side in range(2):
            @pl.when(exists(axis, side))
            def _():
                greet(beside(axis, side))
            expected = expected + exists(axis, side).astype(jnp.int32)
    greet(sibling)
    for axis in ("y", "z"):
        for offset in (1, 3):
            greet(ring_neighbour(axis, offset))
    for offset in range(1, NY_DEV):
        greet((gx, lax.rem(gy + offset, NY_DEV), gz))

    @pl.when(is_owner)
    def _():
        def greet_one(member, carry):
            greet((member // 4, gy, lax.rem(member, 4)))
            return carry
        lax.fori_loop(0, OWNERS - 1, greet_one, 0)

    expected = expected + jnp.where(is_owner, 0, 1)

    loads = [
        pltpu.make_async_copy(now_ref, field_a.at[pl.ds(1, CX), pl.ds(LOW, CY)], load_sem.at[0]),
        pltpu.make_async_copy(hist_ref, hist, load_sem.at[3]),
        pltpu.make_async_copy(w_ref, wv.at[pl.ds(0, ENTRIES)], load_sem.at[4]),
        pltpu.make_async_copy(code_ref, codes, load_sem.at[2]),
        pltpu.make_async_copy(old_ref, field_b.at[pl.ds(1, CX), pl.ds(LOW, CY)], load_sem.at[1]),
    ]
    for load in loads:
        load.start()

    lane = lax.broadcasted_iota(jnp.int32, (CY, CZ), 1)
    zero_plane = jnp.zeros((CY, CZ), F32)

    def over_planes(body, init, unroll=8):
        def chunk(i, carry):
            return body([i * unroll + u for u in range(unroll)], carry)
        return lax.fori_loop(0, CX // unroll, chunk, init)

    def take_faces(step, xs, planes, carry):
        low, high = carry
        for x, plane in zip(xs, planes):
            low = jnp.where(lane == x, pltpu.roll(plane, x, 1), low)
            high = jnp.where(lane == x, pltpu.roll(plane, x + 1, 1), high)
        for x, plane in zip(xs, planes):
            ystage[step, 0, pl.ds(x, 1), :] = plane[0:1, :]
            ystage[step, 1, pl.ds(x, 1), :] = plane[CY - 1:CY, :]
        return low, high

    def halo_copy(step, axis, side):
        current = step % 2
        if axis == 0:
            source = fields[current].at[CX if side else 1, pl.ds(LOW, CY)]
            target = xrecv.at[step, 1 - side]
        elif axis == 1:
            source, target = ystage.at[step, side], yrecv.at[step, 1 - side]
        else:
            source, target = zstage.at[step, side], zrecv.at[step, 1 - side]
        return pltpu.make_async_remote_copy(
            src_ref=source, dst_ref=target,
            send_sem=halo_send.at[step, axis, side],
            recv_sem=halo_recv.at[step, axis, 1 - side],
            device_id=beside(axis, side), device_id_type=MESH,
        )

    def halo_start(step):
        for axis in range(3):
            for side in range(2):
                @pl.when(exists(axis, side))
                def _():
                    halo_copy(step, axis, side).start()

    def halo_wait_send(step, axes=(0, 1, 2)):
        for axis in axes:
            for side in range(2):
                @pl.when(exists(axis, side))
                def _():
                    halo_copy(step, axis, side).wait_send()

    def halo_wait_recv(step, axes):
        for axis in axes:
            buffer = (xrecv, yrecv, zrecv)[axis]
            for side in range(2):
                @pl.when(exists(axis, side))
                def _():
                    halo_copy(step, axis, 1 - side).wait_recv()
                @pl.when(jnp.logical_not(exists(axis, side)))
                def _():
                    buffer[step, side] = zero_plane

    loads[0].wait()

    def first_faces(xs, carry):
        return take_faces(0, xs, [field_a[x + 1, LOW:HIGH, :] for x in xs], carry)

    low, high = over_planes(first_faces, (zero_plane, zero_plane))
    zstage[0, 0] = low
    zstage[0, 1] = high

    pl.semaphore_wait(barrier, expected)
    halo_start(0)

    dirs = dirs_ref[...]
    targets = jnp.concatenate(
        [dirs[k:k + 1, :] for k in range(K_DEV)]
        + [jnp.full((1, PB - ENTRIES), -1, jnp.int32)], axis=1)
    targets = jnp.where(targets >= 0, targets, TARGETS).astype(F32)
    by_lane = jnp.broadcast_to(targets, (PB, PB))
    by_row = by_lane.T
    lanes = lax.broadcasted_iota(jnp.int32, (PB, PB), 1).astype(F32)
    rows = lax.broadcasted_iota(jnp.int32, (PB, PB), 0).astype(F32)

    def count(mask, axis):
        return jnp.sum(jnp.where(mask, 1.0, 0.0), axis=axis, keepdims=True)

    def even(amount):
        return 2.0 * jnp.floor(0.5 * (amount + 1.0))

    member = by_row == lanes
    along_lanes = count(member, 0)
    along_rows = count(by_lane == rows, 1)
    first_lanes = jnp.sum(jnp.where(rows < lanes, even(along_rows), 0.0), axis=0, keepdims=True)
    first_rows = jnp.sum(jnp.where(lanes < rows, even(along_lanes), 0.0), axis=1, keepdims=True)
    before = count(jnp.logical_and(by_lane == by_row, lanes < rows), 1)
    slot = before + jnp.sum(jnp.where(member, first_lanes, 0.0), axis=1, keepdims=True)
    taken = jnp.logical_and(slot == lanes, by_row < TARGETS)
    sequence = ENTRIES + jnp.sum(jnp.where(taken, rows - ENTRIES, 0.0), axis=0, keepdims=True)
    ends = jnp.where(along_lanes > 0, 0.5 * (first_lanes + even(along_lanes)), 0.0)
    opens = count(
        jnp.logical_and(jnp.logical_and(0.5 * first_rows == lanes, along_rows > 0), rows < TARGETS), 0)
    table[0:1, :] = sequence.astype(jnp.int32)
    table[1:2, :] = ends.astype(jnp.int32)
    table[2:3, :] = opens.astype(jnp.int32)
    table[3:8, :] = jnp.zeros((5, PB), jnp.int32)
    order_load = pltpu.make_async_copy(table, order, load_sem.at[7])
    order_load.start()

    def core_copy(half):
        return pltpu.make_async_remote_copy(
            src_ref=part.at[pl.ds(half * 4, 4), :, :, 1 - core],
            dst_ref=core_recv.at[pl.ds(half * 4, 4)],
            send_sem=core_ssem.at[half], recv_sem=core_rsem.at[half],
            device_id=sibling, device_id_type=MESH,
        )

    loads[1].wait()

    def widen(block, carry):
        signal[block, HOLD:, :] = jnp.zeros((TW + MAXOFF - HOLD, PB), F32)
        return carry

    lax.fori_loop(0, BLOCKS, widen, 0)
    for block in range(BLOCKS):
        signal[block, :HOLD, :] = hist[:, block * PB:(block + 1) * PB].astype(F32)
    trail[0] = jnp.zeros((TW, DB), F32)
    order_load.wait()
    loads[2].wait()

    wv[ENTRIES] = jnp.zeros((PB, DB), BF16)

    def far_pair(p):
        windows, blocks = [], []
        for u in range(2):
            entry = jnp.clip(order[0, 2 * p + u], 0, ENTRIES)
            k = jnp.minimum(lax.shift_right_logical(entry, 4), K_DEV - 1)
            block = jnp.bitwise_and(entry, BLOCKS - 1)
            windows.append(signal[block, pl.ds(delay_ref[k, block], TW), :].astype(BF16))
            blocks.append(wv[jnp.where(entry < ENTRIES, block * K_DEV + k, ENTRIES)])
        term = jnp.dot(
            jnp.concatenate(windows, axis=1), jnp.concatenate(blocks, axis=0),
            preferred_element_type=F32)
        trail[p + 1] = term + trail[jnp.where(order[2, p] > 0, 0, p)]

    def far_pairs(first, amount, unroll):
        def chunk(i, carry):
            for u in range(unroll):
                far_pair(first + i * unroll + u)
            return carry
        lax.fori_loop(0, amount // unroll, chunk, 0)

    def far_collect():
        for j in range(TARGETS):
            end = jnp.clip(order[1, j], 0, PAIRS)
            for quarter in range(4):
                found = trail[end, quarter * 128:(quarter + 1) * 128, :]
                part[j, quarter] = found.reshape(4, 2, ROWS, DB)

    def core_start():
        far_collect()
        for half in range(2):
            core_copy(half).start()

    loads[3].wait()

    def plane_coefficients(xs, carry):
        for x in xs:
            code = codes[x]
            for index, values in enumerate(COEFFICIENTS):
                coef[index, x] = jnp.where(
                    code == 0, values[0],
                    jnp.where(code == 1, values[1], jnp.where(code == 2, values[2], values[3])),
                ).astype(F32)
        return carry

    over_planes(plane_coefficients, 0)
    cell = surf_ref[...]
    cell_row = lax.shift_right_arithmetic(cell, 7)
    cell_lane = jnp.bitwise_and(cell, CZ - 1)

    def build_onehot(i, carry):
        rows = lax.broadcasted_iota(jnp.int32, (128, SLOT), 0) + i * 128
        onehot[pl.ds(pl.multiple_of(i * 128, 128), 128), :] = jnp.where(
            rows == cell_row, 1.0, 0.0).astype(BF16)
        return carry

    lax.fori_loop(0, CX * CY // 128, build_onehot, 0)
    samp_send[...] = jnp.zeros_like(samp_send)
    spad[...] = jnp.zeros_like(spad)
    loads[4].wait()

    def leap(step):
        here_ref, other_ref = fields[step % 2], fields[1 - step % 2]
        last = step == STEPS - 1
        halo_wait_recv(step, (1, 2))

        def y_rows(xs, carry):
            rows = [(yrecv[step, 0, pl.ds(x, 1), :], yrecv[step, 1, pl.ds(x, 1), :]) for x in xs]
            for x, (low, high) in zip(xs, rows):
                here_ref[x + 1, LOW - 1:LOW, :] = low
                here_ref[x + 1, HIGH:HIGH + 1, :] = high
            return carry

        over_planes(y_rows, 0, 16)
        z_low, z_high = zrecv[step, 0], zrecv[step, 1]

        def plane_step(xs, carry):
            planes = []
            for x in xs:
                here = here_ref[x + 1, LOW:HIGH, :]
                around = here_ref[x, LOW:HIGH, :] + here_ref[x + 2, LOW:HIGH, :]
                around = around + (
                    here_ref[x + 1, LOW - 1:HIGH - 1, :] + here_ref[x + 1, LOW + 1:HIGH + 1, :])
                below = jnp.where(
                    lane == 0, pltpu.roll(z_low, lax.rem(CZ - x, CZ), 1), pltpu.roll(here, 1, 1))
                above = jnp.where(
                    lane == CZ - 1, pltpu.roll(z_high, CZ - 1 - x, 1), pltpu.roll(here, CZ - 1, 1))
                around = around + (below + above)
                before = other_ref[x + 1, LOW:HIGH, :]
                planes.append(coef[0, x] * here + coef[1, x] * before + coef[2, x] * around)
            for x, new in zip(xs, planes):
                other_ref[x + 1, LOW:HIGH, :] = new
                rounded[step % 2, pl.ds(x * CY if isinstance(x, int) else pl.multiple_of(x * CY, CY), CY), :] = new.astype(BF16)
            if last:
                return carry
            return take_faces(step + 1, xs, planes, carry)

        def inner(i, carry):
            return plane_step([1 + i * 10 + u for u in range(10)], carry)

        carry = lax.fori_loop(
            0, (CX - 2) // 10, inner, 0 if last else (zero_plane, zero_plane))
        halo_wait_recv(step, (0,))
        if step > 0:
            halo_wait_send(step - 1, (0,))
        here_ref[0, LOW:HIGH, :] = xrecv[step, 0]
        here_ref[CX + 1, LOW:HIGH, :] = xrecv[step, 1]
        carry = plane_step([0, CX - 1], carry)
        if not last:
            zstage[step + 1, 0], zstage[step + 1, 1] = carry
            halo_start(step + 1)

    def sample(step):
        picked = lax.dot_general(
            rounded[step % 2], onehot[...], (((0,), (0,)), ((), ())), preferred_element_type=F32)
        level = lax.broadcasted_iota(jnp.int32, (CZ, SLOT), 0)
        values = jnp.sum(jnp.where(level == cell_lane, picked, 0.0), axis=0, keepdims=True)
        if step < STEPS - 1:
            samp_send[4 + step:5 + step, :] = values
        else:
            last_send[...] = jnp.broadcast_to(values, (8, SLOT))

    axes = (("z", "y"), ("y", "z"))

    def index_on(axis):
        return z if axis == "z" else y

    def ring_copy(half, stage, kind, way):
        axis = axes[half][stage]
        place_now = index_on(axis)
        step_to = 1 if way == 0 else 3
        chunk = lax.rem(place_now + (2 if kind == 0 else step_to), 4)
        part = pl.ds(0 if (kind == 1) == (way == 1) else 2, 2)
        if stage == 0:
            source, target = sums.at[half, chunk, part], ring1.at[half, kind, way]
        else:
            source, target = totals.at[half, chunk, part], ring2.at[half, kind, way]
        return pltpu.make_async_remote_copy(
            src_ref=source, dst_ref=target,
            send_sem=ring_send.at[half, stage, kind, way],
            recv_sem=ring_recv.at[half, stage, kind, way],
            device_id=ring_neighbour(axis, step_to), device_id_type=MESH,
        )

    def core_finish(half):
        core_copy(half).wait_recv()

        for yy in range(4):
            for zz in range(4):
                total = (part[half * 4:half * 4 + 4, yy, zz, core]
                         + core_recv[half * 4:half * 4 + 4, yy, zz])
                if half == 0:
                    sums[0, zz, yy] = total
                else:
                    sums[1, yy, zz] = total

    def ring_begin(half, stage):
        for kind in (0, 1):
            for way in (0, 1):
                ring_copy(half, stage, kind, way).start()

    def ring_forward(half, stage):
        held = sums if stage == 0 else totals
        arrived = ring1 if stage == 0 else ring2
        place_now = index_on(axes[half][stage])
        for way in (0, 1):
            ring_copy(half, stage, 0, way).wait_recv()
            chunk = lax.rem(place_now + (1 if way == 0 else 3), 4)
            first = 0 if way == 0 else 2
            held[half, chunk, first:first + 2] = (
                held[half, chunk, first:first + 2] + arrived[half, 0, way])
            ring_copy(half, stage, 2, way).start()

    def ring_end(half, stage):
        held = sums if stage == 0 else totals
        arrived = ring1 if stage == 0 else ring2
        place_now = index_on(axes[half][stage])
        for kind in (1, 2):
            for way in (0, 1):
                ring_copy(half, stage, kind, way).wait_recv()
        first = held[half, place_now, 0:2] + (arrived[half, 2, 0] + arrived[half, 1, 1])
        second = held[half, place_now, 2:4] + (arrived[half, 1, 0] + arrived[half, 2, 1])
        return first, second

    def samp_copy(last, offset, arriving=False):
        source, target = (last_send, last_all) if last else (samp_send, samp_all)
        slot = lax.rem(gy + NY_DEV - offset, NY_DEV) if arriving else gy
        return pltpu.make_async_remote_copy(
            src_ref=source, dst_ref=target.at[slot],
            send_sem=samp_ssem.at[last, offset - 1], recv_sem=samp_rsem.at[last, offset - 1],
            device_id=(gx, lax.rem(gy + offset, NY_DEV), gz), device_id_type=MESH,
        )

    def samp_start(last):
        for offset in range(1, NY_DEV):
            samp_copy(last, offset).start()
        if last:
            last_all[gy] = last_send[...]
        else:
            samp_all[gy] = samp_send[...]

    def samp_wait(last):
        for offset in range(1, NY_DEV):
            samp_copy(last, offset, True).wait_recv()

    row = lax.broadcasted_iota(jnp.int32, (8, PB), 0)
    width = 4 * K_DEV * PB

    def entry_rows(i, carry):
        held = []
        for block in [i * 4 + u for u in range(4)]:
            for entry in range(K_DEV):
                offset = delay_ref[entry, block]
                target = dir_ref[entry, block]
                early = spad[block, pl.ds(offset + 4, 8), :]
                late = spad[block, pl.ds(offset, 8), :]
                pair = jnp.where(row < 4, early, late)
                pieces = []
                for k in range(TARGETS // 2):
                    wanted = jnp.where(row < 4, 2 * k, 2 * k + 1)
                    pieces.append(jnp.where(wanted == target, pair, 0.0))
                held.append(jnp.concatenate(pieces, axis=0).astype(BF16))
        lhs[:, pl.ds(pl.multiple_of(i * width, width), width)] = jnp.concatenate(held, axis=1)
        return carry

    def last_rows():
        for brick in range(NY_DEV):
            held = []
            for i in range(SLOT // PB):
                block = brick * (SLOT // PB) + i
                samples = last_all[brick, :, i * PB:(i + 1) * PB]
                for entry in range(K_DEV):
                    target = jnp.where(
                        delay_ref[entry, block] == MAXOFF, dir_ref[entry, block], -1)
                    held.append(jnp.where(row == target, samples, 0.0))
            picked = jnp.concatenate(held, axis=1)
            last_lhs[:, brick * width:(brick + 1) * width] = jnp.concatenate(
                [picked, jnp.zeros_like(picked)], axis=0).astype(BF16)

    def all_weights():
        return wv[:ENTRIES].reshape(ENTRIES * PB, DB)

    def corr_copy(last, member):
        source, target = (last_out, last_in) if last else (corr_out, corr_in)
        return pltpu.make_async_remote_copy(
            src_ref=source, dst_ref=target.at[member],
            send_sem=last_ssem if last else corr_ssem,
            recv_sem=(last_rsem if last else corr_rsem).at[member],
            device_id=owner, device_id_type=MESH,
        )

    def corr_start(last):
        @pl.when(jnp.logical_not(is_owner))
        def _():
            corr_copy(last, group).start()

    far_pairs(0, 28, 14)
    leap(0)
    far_pairs(28, PAIRS - 28, 12)
    core_start()
    leap(1)
    sample(0)
    sample(1)
    for half in range(2):
        core_finish(half)
        ring_begin(half, 0)
    leap(2)
    save_prev = pltpu.make_async_copy(
        field_b.at[pl.ds(1, CX), pl.ds(LOW, CY)], prev_ref, load_sem.at[5])
    save_prev.start()
    sample(2)
    samp_start(0)
    for half in range(2):
        ring_forward(half, 0)
    leap(3)
    sample(3)
    samp_start(1)
    save_next = pltpu.make_async_copy(
        field_a.at[pl.ds(1, CX), pl.ds(LOW, CY)], next_ref, load_sem.at[6])
    save_next.start()
    for half in range(2):
        first, second = ring_end(half, 0)
        totals[half, 0:2] = first
        totals[half, 2:4] = second
        ring_begin(half, 1)
    samp_wait(0)
    for brick in range(NY_DEV):
        for i in range(SLOT // PB):
            spad[brick * (SLOT // PB) + i, 32:40, :] = samp_all[brick, :, i * PB:(i + 1) * PB]
    lax.fori_loop(0, BLOCKS // 4, entry_rows, 0)
    corr_out[...] = jnp.dot(lhs[...], all_weights(), preferred_element_type=F32)
    corr_start(0)
    for half in range(2):
        ring_forward(half, 1)
    samp_wait(1)
    last_rows()
    last_out[...] = jnp.dot(
        last_lhs[...], all_weights(), preferred_element_type=F32)[:8]
    corr_start(1)
    for half in range(2):
        first, second = ring_end(half, 1)
        for j in range(4):
            columns = slice((half * 4 + j) * DB, (half * 4 + j + 1) * DB)
            far_ref[:, columns] = first[j] if j < 2 else second[j - 2]

    @pl.when(is_owner)
    def _():
        def arrivals(last):
            def one(member, carry):
                corr_copy(last, member).wait_recv()
                return carry
            lax.fori_loop(0, OWNERS - 1, one, 0)

        arrivals(0)
        total = corr_out[...]
        for member in range(OWNERS - 1):
            total = total + corr_in[member]
        for j in range(TARGETS):
            piece = total[(j // 2) * 8:(j // 2) * 8 + 8, :]
            if j % 2 == 0:
                piece = pltpu.roll(piece, 4, 0)
            columns = slice(j * DB, (j + 1) * DB)
            far_ref[8:16, columns] = far_ref[8:16, columns] + jnp.where(row >= 4, piece, 0.0)
        arrivals(1)
        total = last_out[...]
        for member in range(OWNERS - 1):
            total = total + last_in[member]
        for j in range(TARGETS):
            columns = slice(j * DB, (j + 1) * DB)
            far_ref[15:16, columns] = far_ref[15:16, columns] + total[j:j + 1, :]

    for step in range(STEPS):
        halo_wait_send(step, (0, 1, 2) if step == STEPS - 1 else (1, 2))
    for half in range(2):
        core_copy(half).wait_send()
        for stage in range(2):
            for kind in range(3):
                for way in range(2):
                    ring_copy(half, stage, kind, way).wait_send()
    for last in range(2):
        for offset in range(1, NY_DEV):
            samp_copy(last, offset).wait_send()

    @pl.when(jnp.logical_not(is_owner))
    def _():
        corr_copy(0, group).wait_send()
        corr_copy(1, group).wait_send()

    save_prev.wait()
    save_next.wait()


def hall(dirs, delays, surf_index, now, old, code, history, weights):
    any_space = pl.BlockSpec(memory_space=pl.ANY)
    smem = pl.BlockSpec(memory_space=pltpu.SMEM)
    vmem = pl.BlockSpec(memory_space=pltpu.VMEM)
    dma = pltpu.SemaphoreType.DMA
    brick = jax.ShapeDtypeStruct((CX, CY, CZ), F32)
    return pl.pallas_call(
        hall_kernel,
        out_shape=(brick, brick, jax.ShapeDtypeStruct((ROWS, TARGETS * DB), F32)),
        in_specs=[smem, smem, vmem, vmem] + [any_space] * 5,
        out_specs=(any_space, any_space, vmem),
        scratch_shapes=[
            pltpu.VMEM((CX + 2, PADROWS, CZ), F32),
            pltpu.VMEM((CX + 2, PADROWS, CZ), F32),
            pltpu.VMEM((CX, CY, CZ), jnp.int32),
            pltpu.VMEM((3, CX, CY, CZ), F32),
            pltpu.VMEM((STEPS, 2, CX, CZ), F32),
            pltpu.VMEM((STEPS, 2, CY, CZ), F32),
            pltpu.VMEM((STEPS, 2, CY, CZ), F32),
            pltpu.VMEM((STEPS, 2, CX, CZ), F32),
            pltpu.VMEM((STEPS, 2, CY, CZ), F32),
            pltpu.VMEM((CX * CY, SLOT), BF16),
            pltpu.VMEM((2, CX * CY, CZ), BF16),
            pltpu.VMEM((8, SLOT), F32),
            pltpu.VMEM((NY_DEV, 8, SLOT), F32),
            pltpu.VMEM((8, SLOT), F32),
            pltpu.VMEM((NY_DEV, 8, SLOT), F32),
            pltpu.VMEM((BLOCKS, 48, PB), F32),
            pltpu.VMEM((32, ENTRIES * PB), BF16),
            pltpu.VMEM((16, ENTRIES * PB), BF16),
            pltpu.VMEM((ENTRIES + 1, PB, DB), BF16),
            pltpu.VMEM((BLOCKS, TW + MAXOFF, PB), F32),
            pltpu.VMEM((PAIRS + 1, TW, DB), F32),
            pltpu.VMEM((8, PB), jnp.int32),
            pltpu.SMEM((8, PB), jnp.int32),
            pltpu.VMEM((HOLD, BLOCKS * PB), BF16),
            pltpu.VMEM((TARGETS, 4, 4, 2, ROWS, DB), F32),
            pltpu.VMEM((TARGETS, 4, 4, ROWS, DB), F32),
            pltpu.VMEM((2, 4, 4, 4, ROWS, DB), F32),
            pltpu.VMEM((2, 4, 4, ROWS, DB), F32),
            pltpu.VMEM((2, 3, 2, 2, 4, ROWS, DB), F32),
            pltpu.VMEM((2, 3, 2, 2, ROWS, DB), F32),
            pltpu.VMEM((32, DB), F32),
            pltpu.VMEM((OWNERS, 32, DB), F32),
            pltpu.VMEM((8, DB), F32),
            pltpu.VMEM((OWNERS, 8, DB), F32),
            dma((8,)),
            dma((STEPS, 3, 2)), dma((STEPS, 3, 2)),
            dma((2, 3)), dma((2, 3)),
            dma((2,)), dma((2,)),
            dma((2, 2, 3, 2)), dma((2, 2, 3, 2)),
            dma, dma((OWNERS,)), dma, dma((OWNERS,)),
        ],
        compiler_params=pltpu.CompilerParams(
            collective_id=0, has_side_effects=True, vmem_limit_bytes=58 * 1024 * 1024),
    )(dirs, delays, dirs, surf_index, history, now, old, code, weights)


def save_kernel(*refs):
    sources, targets, held, sems = refs[:3], refs[3:6], refs[6:9], refs[9]
    arrivals = [pltpu.make_async_copy(sources[i], held[i], sems.at[0, i]) for i in range(3)]
    leaves = [pltpu.make_async_copy(held[i], targets[i], sems.at[1, i]) for i in range(3)]
    for copy in arrivals:
        copy.start()
    for arrival, leave in zip(arrivals, leaves):
        arrival.wait()
        leave.start()
    for copy in leaves:
        copy.wait()


def save(arrays):
    any_space = pl.BlockSpec(memory_space=pl.ANY)
    return pl.pallas_call(
        save_kernel,
        out_shape=tuple(jax.ShapeDtypeStruct(a.shape, a.dtype) for a in arrays),
        in_specs=[any_space] * 3,
        out_specs=(any_space,) * 3,
        scratch_shapes=[pltpu.VMEM(a.shape, a.dtype) for a in arrays]
        + [pltpu.SemaphoreType.DMA((2, 3))],
    )(*arrays)


def shards(pressure_now, pressure_old, cell_code, surf_index, history, dir_slot, delay, weights):
    flat_weights = weights.reshape(BLOCKS * K_DEV, PB, DB)
    return save(hall(
        dir_slot.T, delay.T, surf_index, pressure_now, pressure_old, cell_code, history,
        flat_weights))


def solution(mesh):
    return jax.shard_map(
        shards,
        mesh=mesh,
        in_specs=(
            P("gx", "gy", "gz"),
            P("gx", "gy", "gz"),
            P("gx", "gy", "gz"),
            P(("gx", "gz"), "gy"),
            P(None, ("gx", "gz")),
            P(("gx", "gz"), "gy"),
            P(("gx", "gz"), "gy"),
            P(("gx", "gz"), "gy", None, None),
        ),
        out_specs=(P("gx", "gy", "gz"), P("gx", "gy", "gz"), P(("gx", "gz"), "gy")),
        check_vma=False,
    )
```

```python
import functools

import jax
import jax.numpy as jnp
import numpy as np
from jax import lax
from jax.experimental import pallas as pl
from jax.experimental.pallas import tpu as pltpu
from jax.sharding import PartitionSpec as P

MESH = pl.DeviceIdType.MESH
F32 = jnp.float32
BF16 = jnp.bfloat16

STEPS = 4
CX, CY, CZ = 32, 32, 128
SLOT = 512
TW = 512
MAXOFF = 32
HOLD = 540
PB = 128
DB = 128
K_DEV = 6
BLOCKS = 16
ENTRIES = K_DEV * BLOCKS
PAIRS = ENTRIES // 2 + 4
TARGETS = 8
OWNERS = 32
ROWS = 16
NX_DEV, NY_DEV, NZ_DEV = 8, 4, 4
LOW, HIGH = 8, 40
PADROWS = 48


def coefficient_table():
    speeds = np.array([0.32, 0.26, 0.19, 0.11], np.float32).astype(np.float64)
    damping = np.array([0.0, 0.02, 0.08, 0.3], np.float32).astype(np.float64)
    here = (2.0 - 6.0 * speeds) / (1.0 + damping)
    before = -(1.0 - damping) / (1.0 + damping)
    around = speeds / (1.0 + damping)
    return [[float(np.float32(v)) for v in row] for row in (here, before, around)]


COEFFICIENTS = coefficient_table()


def hall_kernel(
    dir_ref, delay_ref, dirs_ref, surf_ref, hist_ref, now_ref, old_ref, code_ref, w_ref,
    next_ref, prev_ref, far_ref,
    field_a, field_b, codes, coef, ystage, zstage, xrecv, yrecv, zrecv,
    onehot, rounded, samp_send, samp_all, last_send, last_all, spad, lhs, last_lhs, wv,
    signal, trail, table, order, hist, part, core_recv, sums, totals, ring1, ring2, corr_out, corr_in, last_out, last_in,
    load_sem, halo_send, halo_recv, samp_ssem, samp_rsem,
    core_ssem, core_rsem, ring_send, ring_recv, corr_ssem, corr_rsem, last_ssem, last_rsem,
):
    fields = (field_a, field_b)
    gx, gy, gz = lax.axis_index("gx"), lax.axis_index("gy"), lax.axis_index("gz")
    y, z_hi = gx // 2, lax.rem(gx, 2)
    z_lo, core = gz // 2, lax.rem(gz, 2)
    z = z_hi * 2 + z_lo
    group = gx * 4 + gz
    is_owner = group == OWNERS - 1

    def place(yy, zz):
        return (yy * 2 + zz // 2, gy, lax.rem(zz, 2) * 2 + core)

    def ring_neighbour(axis, offset):
        if axis == "z":
            return place(y, lax.rem(z + offset, 4))
        return place(lax.rem(y + offset, 4), z)

    sibling = (gx, gy, z_lo * 2 + 1 - core)
    owner = (NX_DEV - 1, gy, NZ_DEV - 1)
    coords = (gx, gy, gz)
    extents = (NX_DEV, NY_DEV, NZ_DEV)

    def beside(axis, side):
        moved = list(coords)
        moved[axis] = coords[axis] + (1 if side else -1)
        return tuple(moved)

    def exists(axis, side):
        return coords[axis] < extents[axis] - 1 if side else coords[axis] > 0

    barrier = pltpu.get_barrier_semaphore()

    def greet(device):
        pl.semaphore_signal(barrier, inc=1, device_id=device, device_id_type=MESH)

    expected = jnp.int32(8)
    for axis in range(3):
        for side in range(2):
            @pl.when(exists(axis, side))
            def _():
                greet(beside(axis, side))
            expected = expected + exists(axis, side).astype(jnp.int32)
    greet(sibling)
    for axis in ("y", "z"):
        for offset in (1, 3):
            greet(ring_neighbour(axis, offset))
    for offset in range(1, NY_DEV):
        greet((gx, lax.rem(gy + offset, NY_DEV), gz))

    @pl.when(is_owner)
    def _():
        def greet_one(member, carry):
            greet((member // 4, gy, lax.rem(member, 4)))
            return carry
        lax.fori_loop(0, OWNERS - 1, greet_one, 0)

    expected = expected + jnp.where(is_owner, 0, 1)

    loads = [
        pltpu.make_async_copy(now_ref, field_a.at[pl.ds(1, CX), pl.ds(LOW, CY)], load_sem.at[0]),
        pltpu.make_async_copy(hist_ref, hist, load_sem.at[3]),
        pltpu.make_async_copy(w_ref, wv.at[pl.ds(0, ENTRIES)], load_sem.at[4]),
        pltpu.make_async_copy(code_ref, codes, load_sem.at[2]),
        pltpu.make_async_copy(old_ref, field_b.at[pl.ds(1, CX), pl.ds(LOW, CY)], load_sem.at[1]),
    ]
    for load in loads:
        load.start()

    lane = lax.broadcasted_iota(jnp.int32, (CY, CZ), 1)
    zero_plane = jnp.zeros((CY, CZ), F32)

    def over_planes(body, init, unroll=8):
        def chunk(i, carry):
            return body([i * unroll + u for u in range(unroll)], carry)
        return lax.fori_loop(0, CX // unroll, chunk, init)

    def take_faces(step, xs, planes, carry):
        low, high = carry
        for x, plane in zip(xs, planes):
            low = jnp.where(lane == x, pltpu.roll(plane, x, 1), low)
            high = jnp.where(lane == x, pltpu.roll(plane, x + 1, 1), high)
        for x, plane in zip(xs, planes):
            ystage[step, 0, pl.ds(x, 1), :] = plane[0:1, :]
            ystage[step, 1, pl.ds(x, 1), :] = plane[CY - 1:CY, :]
        return low, high

    def halo_copy(step, axis, side):
        current = step % 2
        if axis == 0:
            source = fields[current].at[CX if side else 1, pl.ds(LOW, CY)]
            target = xrecv.at[step, 1 - side]
        elif axis == 1:
            source, target = ystage.at[step, side], yrecv.at[step, 1 - side]
        else:
            source, target = zstage.at[step, side], zrecv.at[step, 1 - side]
        return pltpu.make_async_remote_copy(
            src_ref=source, dst_ref=target,
            send_sem=halo_send.at[step, axis, side],
            recv_sem=halo_recv.at[step, axis, 1 - side],
            device_id=beside(axis, side), device_id_type=MESH,
        )

    def halo_start(step):
        for axis in range(3):
            for side in range(2):
                @pl.when(exists(axis, side))
                def _():
                    halo_copy(step, axis, side).start()

    def halo_wait_send(step, axes=(0, 1, 2)):
        for axis in axes:
            for side in range(2):
                @pl.when(exists(axis, side))
                def _():
                    halo_copy(step, axis, side).wait_send()

    def halo_wait_recv(step, axes):
        for axis in axes:
            buffer = (xrecv, yrecv, zrecv)[axis]
            for side in range(2):
                @pl.when(exists(axis, side))
                def _():
                    halo_copy(step, axis, 1 - side).wait_recv()
                @pl.when(jnp.logical_not(exists(axis, side)))
                def _():
                    buffer[step, side] = zero_plane

    loads[0].wait()

    def first_faces(xs, carry):
        return take_faces(0, xs, [field_a[x + 1, LOW:HIGH, :] for x in xs], carry)

    low, high = over_planes(first_faces, (zero_plane, zero_plane))
    zstage[0, 0] = low
    zstage[0, 1] = high

    pl.semaphore_wait(barrier, expected)
    halo_start(0)

    dirs = dirs_ref[...]
    targets = jnp.concatenate(
        [dirs[k:k + 1, :] for k in range(K_DEV)]
        + [jnp.full((1, PB - ENTRIES), -1, jnp.int32)], axis=1)
    targets = jnp.where(targets >= 0, targets, TARGETS).astype(F32)
    by_lane = jnp.broadcast_to(targets, (PB, PB))
    by_row = by_lane.T
    lanes = lax.broadcasted_iota(jnp.int32, (PB, PB), 1).astype(F32)
    rows = lax.broadcasted_iota(jnp.int32, (PB, PB), 0).astype(F32)

    def count(mask, axis):
        return jnp.sum(jnp.where(mask, 1.0, 0.0), axis=axis, keepdims=True)

    def even(amount):
        return 2.0 * jnp.floor(0.5 * (amount + 1.0))

    member = by_row == lanes
    along_lanes = count(member, 0)
    along_rows = count(by_lane == rows, 1)
    first_lanes = jnp.sum(jnp.where(rows < lanes, even(along_rows), 0.0), axis=0, keepdims=True)
    first_rows = jnp.sum(jnp.where(lanes < rows, even(along_lanes), 0.0), axis=1, keepdims=True)
    before = count(jnp.logical_and(by_lane == by_row, lanes < rows), 1)
    slot = before + jnp.sum(jnp.where(member, first_lanes, 0.0), axis=1, keepdims=True)
    taken = jnp.logical_and(slot == lanes, by_row < TARGETS)
    sequence = ENTRIES + jnp.sum(jnp.where(taken, rows - ENTRIES, 0.0), axis=0, keepdims=True)
    ends = jnp.where(along_lanes > 0, 0.5 * (first_lanes + even(along_lanes)), 0.0)
    opens = count(
        jnp.logical_and(jnp.logical_and(0.5 * first_rows == lanes, along_rows > 0), rows < TARGETS), 0)
    table[0:1, :] = sequence.astype(jnp.int32)
    table[1:2, :] = ends.astype(jnp.int32)
    table[2:3, :] = opens.astype(jnp.int32)
    table[3:8, :] = jnp.zeros((5, PB), jnp.int32)
    order_load = pltpu.make_async_copy(table, order, load_sem.at[7])
    order_load.start()

    def core_copy(half):
        return pltpu.make_async_remote_copy(
            src_ref=part.at[pl.ds(half * 4, 4), :, :, 1 - core],
            dst_ref=core_recv.at[pl.ds(half * 4, 4)],
            send_sem=core_ssem.at[half], recv_sem=core_rsem.at[half],
            device_id=sibling, device_id_type=MESH,
        )

    loads[1].wait()

    def widen(block, carry):
        signal[block, HOLD:, :] = jnp.zeros((TW + MAXOFF - HOLD, PB), F32)
        return carry

    lax.fori_loop(0, BLOCKS, widen, 0)
    for block in range(BLOCKS):
        signal[block, :HOLD, :] = hist[:, block * PB:(block + 1) * PB].astype(F32)
    trail[0] = jnp.zeros((TW, DB), F32)
    order_load.wait()
    loads[2].wait()

    wv[ENTRIES] = jnp.zeros((PB, DB), BF16)

    def far_pair(p):
        windows, blocks = [], []
        for u in range(2):
            entry = jnp.clip(order[0, 2 * p + u], 0, ENTRIES)
            k = jnp.minimum(lax.shift_right_logical(entry, 4), K_DEV - 1)
            block = jnp.bitwise_and(entry, BLOCKS - 1)
            windows.append(signal[block, pl.ds(delay_ref[k, block], TW), :].astype(BF16))
            blocks.append(wv[jnp.where(entry < ENTRIES, block * K_DEV + k, ENTRIES)])
        term = jnp.dot(
            jnp.concatenate(windows, axis=1), jnp.concatenate(blocks, axis=0),
            preferred_element_type=F32)
        trail[p + 1] = term + trail[jnp.where(order[2, p] > 0, 0, p)]

    def far_pairs(first, amount, unroll):
        def chunk(i, carry):
            for u in range(unroll):
                far_pair(first + i * unroll + u)
            return carry
        lax.fori_loop(0, amount // unroll, chunk, 0)

    def far_collect():
        for j in range(TARGETS):
            end = jnp.clip(order[1, j], 0, PAIRS)
            for quarter in range(4):
                found = trail[end, quarter * 128:(quarter + 1) * 128, :]
                part[j, quarter] = found.reshape(4, 2, ROWS, DB)

    def core_start():
        far_collect()
        for half in range(2):
            core_copy(half).start()

    loads[3].wait()

    def plane_coefficients(xs, carry):
        for x in xs:
            code = codes[x]
            for index, values in enumerate(COEFFICIENTS):
                coef[index, x] = jnp.where(
                    code == 0, values[0],
                    jnp.where(code == 1, values[1], jnp.where(code == 2, values[2], values[3])),
                ).astype(F32)
        return carry

    over_planes(plane_coefficients, 0)
    cell = surf_ref[...]
    cell_row = lax.shift_right_arithmetic(cell, 7)
    cell_lane = jnp.bitwise_and(cell, CZ - 1)

    def build_onehot(i, carry):
        rows = lax.broadcasted_iota(jnp.int32, (128, SLOT), 0) + i * 128
        onehot[pl.ds(pl.multiple_of(i * 128, 128), 128), :] = jnp.where(
            rows == cell_row, 1.0, 0.0).astype(BF16)
        return carry

    lax.fori_loop(0, CX * CY // 128, build_onehot, 0)
    samp_send[...] = jnp.zeros_like(samp_send)
    spad[...] = jnp.zeros_like(spad)
    loads[4].wait()

    def leap(step, between=None):
        here_ref, other_ref = fields[step % 2], fields[1 - step % 2]
        last = step == STEPS - 1
        halo_wait_recv(step, (1, 2))

        def y_rows(xs, carry):
            rows = [(yrecv[step, 0, pl.ds(x, 1), :], yrecv[step, 1, pl.ds(x, 1), :]) for x in xs]
            for x, (low, high) in zip(xs, rows):
                here_ref[x + 1, LOW - 1:LOW, :] = low
                here_ref[x + 1, HIGH:HIGH + 1, :] = high
            return carry

        over_planes(y_rows, 0, 16)
        z_low, z_high = zrecv[step, 0], zrecv[step, 1]

        def plane_step(xs, carry):
            planes = []
            for x in xs:
                here = here_ref[x + 1, LOW:HIGH, :]
                around = here_ref[x, LOW:HIGH, :] + here_ref[x + 2, LOW:HIGH, :]
                around = around + (
                    here_ref[x + 1, LOW - 1:HIGH - 1, :] + here_ref[x + 1, LOW + 1:HIGH + 1, :])
                below = jnp.where(
                    lane == 0, pltpu.roll(z_low, lax.rem(CZ - x, CZ), 1), pltpu.roll(here, 1, 1))
                above = jnp.where(
                    lane == CZ - 1, pltpu.roll(z_high, CZ - 1 - x, 1), pltpu.roll(here, CZ - 1, 1))
                around = around + (below + above)
                before = other_ref[x + 1, LOW:HIGH, :]
                planes.append(coef[0, x] * here + coef[1, x] * before + coef[2, x] * around)
            for x, new in zip(xs, planes):
                other_ref[x + 1, LOW:HIGH, :] = new
                rounded[step % 2, pl.ds(x * CY if isinstance(x, int) else pl.multiple_of(x * CY, CY), CY), :] = new.astype(BF16)
            if last:
                return carry
            return take_faces(step + 1, xs, planes, carry)

        def inner(i, carry):
            return plane_step([1 + i * 10 + u for u in range(10)], carry)

        carry = lax.fori_loop(
            0, (CX - 2) // 10, inner, 0 if last else (zero_plane, zero_plane))
        if between is not None:
            between()
        halo_wait_recv(step, (0,))
        if step > 0:
            halo_wait_send(step - 1, (0,))
        here_ref[0, LOW:HIGH, :] = xrecv[step, 0]
        here_ref[CX + 1, LOW:HIGH, :] = xrecv[step, 1]
        carry = plane_step([0, CX - 1], carry)
        if not last:
            zstage[step + 1, 0], zstage[step + 1, 1] = carry
            halo_start(step + 1)

    def sample(step):
        picked = lax.dot_general(
            rounded[step % 2], onehot[...], (((0,), (0,)), ((), ())), preferred_element_type=F32)
        level = lax.broadcasted_iota(jnp.int32, (CZ, SLOT), 0)
        values = jnp.sum(jnp.where(level == cell_lane, picked, 0.0), axis=0, keepdims=True)
        if step < STEPS - 1:
            samp_send[4 + step:5 + step, :] = values
        else:
            last_send[...] = jnp.broadcast_to(values, (8, SLOT))

    axes = (("z", "y"), ("y", "z"))

    def index_on(axis):
        return z if axis == "z" else y

    def ring_copy(half, stage, kind, way):
        axis = axes[half][stage]
        place_now = index_on(axis)
        step_to = 1 if way == 0 else 3
        chunk = lax.rem(place_now + (2 if kind == 0 else step_to), 4)
        part = pl.ds(0 if (kind == 1) == (way == 1) else 2, 2)
        if stage == 0:
            source, target = sums.at[half, chunk, part], ring1.at[half, kind, way]
        else:
            source, target = totals.at[half, chunk, part], ring2.at[half, kind, way]
        return pltpu.make_async_remote_copy(
            src_ref=source, dst_ref=target,
            send_sem=ring_send.at[half, stage, kind, way],
            recv_sem=ring_recv.at[half, stage, kind, way],
            device_id=ring_neighbour(axis, step_to), device_id_type=MESH,
        )

    def core_finish(half):
        core_copy(half).wait_recv()

        for yy in range(4):
            for zz in range(4):
                total = (part[half * 4:half * 4 + 4, yy, zz, core]
                         + core_recv[half * 4:half * 4 + 4, yy, zz])
                if half == 0:
                    sums[0, zz, yy] = total
                else:
                    sums[1, yy, zz] = total

    def ring_begin(half, stage):
        for kind in (0, 1):
            for way in (0, 1):
                ring_copy(half, stage, kind, way).start()

    def ring_forward(half, stage):
        held = sums if stage == 0 else totals
        arrived = ring1 if stage == 0 else ring2
        place_now = index_on(axes[half][stage])
        for way in (0, 1):
            ring_copy(half, stage, 0, way).wait_recv()
            chunk = lax.rem(place_now + (1 if way == 0 else 3), 4)
            first = 0 if way == 0 else 2
            held[half, chunk, first:first + 2] = (
                held[half, chunk, first:first + 2] + arrived[half, 0, way])
            ring_copy(half, stage, 2, way).start()

    def ring_end(half, stage):
        held = sums if stage == 0 else totals
        arrived = ring1 if stage == 0 else ring2
        place_now = index_on(axes[half][stage])
        for kind in (1, 2):
            for way in (0, 1):
                ring_copy(half, stage, kind, way).wait_recv()
        first = held[half, place_now, 0:2] + (arrived[half, 2, 0] + arrived[half, 1, 1])
        second = held[half, place_now, 2:4] + (arrived[half, 1, 0] + arrived[half, 2, 1])
        return first, second

    def samp_copy(last, offset, arriving=False):
        source, target = (last_send, last_all) if last else (samp_send, samp_all)
        slot = lax.rem(gy + NY_DEV - offset, NY_DEV) if arriving else gy
        return pltpu.make_async_remote_copy(
            src_ref=source, dst_ref=target.at[slot],
            send_sem=samp_ssem.at[last, offset - 1], recv_sem=samp_rsem.at[last, offset - 1],
            device_id=(gx, lax.rem(gy + offset, NY_DEV), gz), device_id_type=MESH,
        )

    def samp_start(last):
        for offset in range(1, NY_DEV):
            samp_copy(last, offset).start()
        if last:
            last_all[gy] = last_send[...]
        else:
            samp_all[gy] = samp_send[...]

    def samp_wait(last):
        for offset in range(1, NY_DEV):
            samp_copy(last, offset, True).wait_recv()

    row = lax.broadcasted_iota(jnp.int32, (8, PB), 0)
    width = 4 * K_DEV * PB

    def entry_rows(i, carry):
        held = []
        for block in [i * 4 + u for u in range(4)]:
            for entry in range(K_DEV):
                offset = delay_ref[entry, block]
                target = dir_ref[entry, block]
                early = spad[block, pl.ds(offset + 4, 8), :]
                late = spad[block, pl.ds(offset, 8), :]
                pair = jnp.where(row < 4, early, late)
                pieces = []
                for k in range(TARGETS // 2):
                    wanted = jnp.where(row < 4, 2 * k, 2 * k + 1)
                    pieces.append(jnp.where(wanted == target, pair, 0.0))
                held.append(jnp.concatenate(pieces, axis=0).astype(BF16))
        lhs[:, pl.ds(pl.multiple_of(i * width, width), width)] = jnp.concatenate(held, axis=1)
        return carry

    def last_rows():
        for brick in range(NY_DEV):
            held = []
            for i in range(SLOT // PB):
                block = brick * (SLOT // PB) + i
                samples = last_all[brick, :, i * PB:(i + 1) * PB]
                for entry in range(K_DEV):
                    target = jnp.where(
                        delay_ref[entry, block] == MAXOFF, dir_ref[entry, block], -1)
                    held.append(jnp.where(row == target, samples, 0.0))
            picked = jnp.concatenate(held, axis=1)
            last_lhs[:, brick * width:(brick + 1) * width] = jnp.concatenate(
                [picked, jnp.zeros_like(picked)], axis=0).astype(BF16)

    def all_weights():
        return wv[:ENTRIES].reshape(ENTRIES * PB, DB)

    def corr_copy(last, member):
        source, target = (last_out, last_in) if last else (corr_out, corr_in)
        return pltpu.make_async_remote_copy(
            src_ref=source, dst_ref=target.at[member],
            send_sem=last_ssem if last else corr_ssem,
            recv_sem=(last_rsem if last else corr_rsem).at[member],
            device_id=owner, device_id_type=MESH,
        )

    def corr_start(last):
        @pl.when(jnp.logical_not(is_owner))
        def _():
            corr_copy(last, group).start()

    far_pairs(0, 28, 14)
    leap(0)
    far_pairs(28, PAIRS - 28, 12)
    core_start()
    leap(1)
    for half in range(2):
        core_finish(half)
        ring_begin(half, 0)
    sample(0)
    sample(1)
    leap(2)
    save_prev = pltpu.make_async_copy(
        field_b.at[pl.ds(1, CX), pl.ds(LOW, CY)], prev_ref, load_sem.at[5])
    save_prev.start()
    for half in range(2):
        ring_forward(half, 0)
    sample(2)
    samp_start(0)

    def second_ring():
        for half in range(2):
            first, second = ring_end(half, 0)
            totals[half, 0:2] = first
            totals[half, 2:4] = second
            ring_begin(half, 1)

    leap(3, second_ring)
    sample(3)
    samp_start(1)
    save_next = pltpu.make_async_copy(
        field_a.at[pl.ds(1, CX), pl.ds(LOW, CY)], next_ref, load_sem.at[6])
    save_next.start()
    samp_wait(0)
    for brick in range(NY_DEV):
        for i in range(SLOT // PB):
            spad[brick * (SLOT // PB) + i, 32:40, :] = samp_all[brick, :, i * PB:(i + 1) * PB]
    lax.fori_loop(0, BLOCKS // 4, entry_rows, 0)
    for half in range(2):
        ring_forward(half, 1)
    corr_out[...] = jnp.dot(lhs[...], all_weights(), preferred_element_type=F32)
    corr_start(0)
    for half in range(2):
        first, second = ring_end(half, 1)
        for j in range(4):
            columns = slice((half * 4 + j) * DB, (half * 4 + j + 1) * DB)
            far_ref[:, columns] = first[j] if j < 2 else second[j - 2]
    samp_wait(1)
    last_rows()
    last_out[...] = jnp.dot(
        last_lhs[...], all_weights(), preferred_element_type=F32)[:8]
    corr_start(1)

    @pl.when(is_owner)
    def _():
        def arrivals(last):
            def one(member, carry):
                corr_copy(last, member).wait_recv()
                return carry
            lax.fori_loop(0, OWNERS - 1, one, 0)

        arrivals(0)
        total = corr_out[...]
        for member in range(OWNERS - 1):
            total = total + corr_in[member]
        for j in range(TARGETS):
            piece = total[(j // 2) * 8:(j // 2) * 8 + 8, :]
            if j % 2 == 0:
                piece = pltpu.roll(piece, 4, 0)
            columns = slice(j * DB, (j + 1) * DB)
            far_ref[8:16, columns] = far_ref[8:16, columns] + jnp.where(row >= 4, piece, 0.0)
        arrivals(1)
        total = last_out[...]
        for member in range(OWNERS - 1):
            total = total + last_in[member]
        for j in range(TARGETS):
            columns = slice(j * DB, (j + 1) * DB)
            far_ref[15:16, columns] = far_ref[15:16, columns] + total[j:j + 1, :]

    for step in range(STEPS):
        halo_wait_send(step, (0, 1, 2) if step == STEPS - 1 else (1, 2))
    for half in range(2):
        core_copy(half).wait_send()
        for stage in range(2):
            for kind in range(3):
                for way in range(2):
                    ring_copy(half, stage, kind, way).wait_send()
    for last in range(2):
        for offset in range(1, NY_DEV):
            samp_copy(last, offset).wait_send()

    @pl.when(jnp.logical_not(is_owner))
    def _():
        corr_copy(0, group).wait_send()
        corr_copy(1, group).wait_send()

    save_prev.wait()
    save_next.wait()


def hall(dirs, delays, surf_index, now, old, code, history, weights):
    any_space = pl.BlockSpec(memory_space=pl.ANY)
    smem = pl.BlockSpec(memory_space=pltpu.SMEM)
    vmem = pl.BlockSpec(memory_space=pltpu.VMEM)
    dma = pltpu.SemaphoreType.DMA
    brick = jax.ShapeDtypeStruct((CX, CY, CZ), F32)
    return pl.pallas_call(
        hall_kernel,
        out_shape=(brick, brick, jax.ShapeDtypeStruct((ROWS, TARGETS * DB), F32)),
        in_specs=[smem, smem, vmem, vmem] + [any_space] * 5,
        out_specs=(any_space, any_space, vmem),
        scratch_shapes=[
            pltpu.VMEM((CX + 2, PADROWS, CZ), F32),
            pltpu.VMEM((CX + 2, PADROWS, CZ), F32),
            pltpu.VMEM((CX, CY, CZ), jnp.int32),
            pltpu.VMEM((3, CX, CY, CZ), F32),
            pltpu.VMEM((STEPS, 2, CX, CZ), F32),
            pltpu.VMEM((STEPS, 2, CY, CZ), F32),
            pltpu.VMEM((STEPS, 2, CY, CZ), F32),
            pltpu.VMEM((STEPS, 2, CX, CZ), F32),
            pltpu.VMEM((STEPS, 2, CY, CZ), F32),
            pltpu.VMEM((CX * CY, SLOT), BF16),
            pltpu.VMEM((2, CX * CY, CZ), BF16),
            pltpu.VMEM((8, SLOT), F32),
            pltpu.VMEM((NY_DEV, 8, SLOT), F32),
            pltpu.VMEM((8, SLOT), F32),
            pltpu.VMEM((NY_DEV, 8, SLOT), F32),
            pltpu.VMEM((BLOCKS, 48, PB), F32),
            pltpu.VMEM((32, ENTRIES * PB), BF16),
            pltpu.VMEM((16, ENTRIES * PB), BF16),
            pltpu.VMEM((ENTRIES + 1, PB, DB), BF16),
            pltpu.VMEM((BLOCKS, TW + MAXOFF, PB), F32),
            pltpu.VMEM((PAIRS + 1, TW, DB), F32),
            pltpu.VMEM((8, PB), jnp.int32),
            pltpu.SMEM((8, PB), jnp.int32),
            pltpu.VMEM((HOLD, BLOCKS * PB), BF16),
            pltpu.VMEM((TARGETS, 4, 4, 2, ROWS, DB), F32),
            pltpu.VMEM((TARGETS, 4, 4, ROWS, DB), F32),
            pltpu.VMEM((2, 4, 4, 4, ROWS, DB), F32),
            pltpu.VMEM((2, 4, 4, ROWS, DB), F32),
            pltpu.VMEM((2, 3, 2, 2, 4, ROWS, DB), F32),
            pltpu.VMEM((2, 3, 2, 2, ROWS, DB), F32),
            pltpu.VMEM((32, DB), F32),
            pltpu.VMEM((OWNERS, 32, DB), F32),
            pltpu.VMEM((8, DB), F32),
            pltpu.VMEM((OWNERS, 8, DB), F32),
            dma((8,)),
            dma((STEPS, 3, 2)), dma((STEPS, 3, 2)),
            dma((2, 3)), dma((2, 3)),
            dma((2,)), dma((2,)),
            dma((2, 2, 3, 2)), dma((2, 2, 3, 2)),
            dma, dma((OWNERS,)), dma, dma((OWNERS,)),
        ],
        compiler_params=pltpu.CompilerParams(
            collective_id=0, has_side_effects=True, vmem_limit_bytes=58 * 1024 * 1024),
    )(dirs, delays, dirs, surf_index, history, now, old, code, weights)


def save_kernel(*refs):
    sources, targets, held, sems = refs[:3], refs[3:6], refs[6:9], refs[9]
    arrivals = [pltpu.make_async_copy(sources[i], held[i], sems.at[0, i]) for i in range(3)]
    leaves = [pltpu.make_async_copy(held[i], targets[i], sems.at[1, i]) for i in range(3)]
    for copy in arrivals:
        copy.start()
    for arrival, leave in zip(arrivals, leaves):
        arrival.wait()
        leave.start()
    for copy in leaves:
        copy.wait()


def save(arrays):
    any_space = pl.BlockSpec(memory_space=pl.ANY)
    return pl.pallas_call(
        save_kernel,
        out_shape=tuple(jax.ShapeDtypeStruct(a.shape, a.dtype) for a in arrays),
        in_specs=[any_space] * 3,
        out_specs=(any_space,) * 3,
        scratch_shapes=[pltpu.VMEM(a.shape, a.dtype) for a in arrays]
        + [pltpu.SemaphoreType.DMA((2, 3))],
    )(*arrays)


def shards(pressure_now, pressure_old, cell_code, surf_index, history, dir_slot, delay, weights):
    flat_weights = weights.reshape(BLOCKS * K_DEV, PB, DB)
    return save(hall(
        dir_slot.T, delay.T, surf_index, pressure_now, pressure_old, cell_code, history,
        flat_weights))


def solution(mesh):
    return jax.shard_map(
        shards,
        mesh=mesh,
        in_specs=(
            P("gx", "gy", "gz"),
            P("gx", "gy", "gz"),
            P("gx", "gy", "gz"),
            P(("gx", "gz"), "gy"),
            P(None, ("gx", "gz")),
            P(("gx", "gz"), "gy"),
            P(("gx", "gz"), "gy"),
            P(("gx", "gz"), "gy", None, None),
        ),
        out_specs=(P("gx", "gy", "gz"), P("gx", "gy", "gz"), P(("gx", "gz"), "gy")),
        check_vma=False,
    )
```

```python
import functools

import jax
import jax.numpy as jnp
import numpy as np
from jax import lax
from jax.experimental import pallas as pl
from jax.experimental.pallas import tpu as pltpu
from jax.sharding import PartitionSpec as P

MESH = pl.DeviceIdType.MESH
F32 = jnp.float32
BF16 = jnp.bfloat16

STEPS = 4
CX, CY, CZ = 32, 32, 128
SLOT = 512
TW = 512
MAXOFF = 32
HOLD = 540
PB = 128
DB = 128
K_DEV = 6
BLOCKS = 16
ENTRIES = K_DEV * BLOCKS
PAIRS = ENTRIES // 2 + 4
TARGETS = 8
OWNERS = 32
ROWS = 16
NX_DEV, NY_DEV, NZ_DEV = 8, 4, 4
LOW, HIGH = 16, 48
WIDE_LOW, WIDE_HIGH = 8, 56
PADROWS = 64
ROUNDS = 2
EDGES = [(a, i, b, j) for a, b in ((0, 1), (0, 2), (1, 2)) for i in (0, 1) for j in (0, 1)]


def coefficient_table():
    speeds = np.array([0.32, 0.26, 0.19, 0.11], np.float32).astype(np.float64)
    damping = np.array([0.0, 0.02, 0.08, 0.3], np.float32).astype(np.float64)
    here = (2.0 - 6.0 * speeds) / (1.0 + damping)
    before = -(1.0 - damping) / (1.0 + damping)
    around = speeds / (1.0 + damping)
    return [[float(np.float32(v)) for v in row] for row in (here, before, around)]


COEFFICIENTS = coefficient_table()


def hall_kernel(
    dir_ref, delay_ref, dirs_ref, surf_ref, hist_ref, now_ref, old_ref, code_ref, w_ref,
    next_ref, prev_ref, far_ref,
    field_a, field_b, codes, coef, stage, land, edges, zlayer, zkeep, zcoef,
    onehot, rounded, samp_send, samp_all, last_send, last_all, spad, lhs, last_lhs, wv,
    signal, trail, table, order, hist, part, core_recv, sums, totals, ring1, ring2, corr_out, corr_in, last_out, last_in,
    load_sem, halo_send, halo_recv, edge_send, edge_recv, samp_ssem, samp_rsem,
    core_ssem, core_rsem, ring_send, ring_recv, corr_ssem, corr_rsem, last_ssem, last_rsem,
):
    gx, gy, gz = lax.axis_index("gx"), lax.axis_index("gy"), lax.axis_index("gz")
    y, z_hi = gx // 2, lax.rem(gx, 2)
    z_lo, core = gz // 2, lax.rem(gz, 2)
    z = z_hi * 2 + z_lo
    group = gx * 4 + gz
    is_owner = group == OWNERS - 1

    def place(yy, zz):
        return (yy * 2 + zz // 2, gy, lax.rem(zz, 2) * 2 + core)

    def ring_neighbour(axis, offset):
        if axis == "z":
            return place(y, lax.rem(z + offset, 4))
        return place(lax.rem(y + offset, 4), z)

    sibling = (gx, gy, z_lo * 2 + 1 - core)
    owner = (NX_DEV - 1, gy, NZ_DEV - 1)
    coords = (gx, gy, gz)
    extents = (NX_DEV, NY_DEV, NZ_DEV)

    def beside(axis, side):
        moved = list(coords)
        moved[axis] = coords[axis] + (1 if side else -1)
        return tuple(moved)

    def exists(axis, side):
        return coords[axis] < extents[axis] - 1 if side else coords[axis] > 0

    def across(edge):
        moved = list(coords)
        for axis, side in (edge[:2], edge[2:]):
            moved[axis] = coords[axis] + (1 if side else -1)
        return tuple(moved)

    def edge_exists(edge):
        return jnp.logical_and(exists(edge[0], edge[1]), exists(edge[2], edge[3]))

    barrier = pltpu.get_barrier_semaphore()

    def greet(device):
        pl.semaphore_signal(barrier, inc=1, device_id=device, device_id_type=MESH)

    expected = jnp.int32(8)
    for axis in range(3):
        for side in range(2):
            @pl.when(exists(axis, side))
            def _():
                greet(beside(axis, side))
            expected = expected + exists(axis, side).astype(jnp.int32)
    for first, i, second, j in EDGES:
        there = edge_exists((first, i, second, j))
        @pl.when(there)
        def _():
            greet(across((first, i, second, j)))
        expected = expected + there.astype(jnp.int32)
    greet(sibling)
    for axis in ("y", "z"):
        for offset in (1, 3):
            greet(ring_neighbour(axis, offset))
    for offset in range(1, NY_DEV):
        greet((gx, lax.rem(gy + offset, NY_DEV), gz))

    @pl.when(is_owner)
    def _():
        def greet_one(member, carry):
            greet((member // 4, gy, lax.rem(member, 4)))
            return carry
        lax.fori_loop(0, OWNERS - 1, greet_one, 0)

    expected = expected + jnp.where(is_owner, 0, 1)

    loads = [
        pltpu.make_async_copy(now_ref, field_a.at[pl.ds(2, CX), pl.ds(LOW, CY)], load_sem.at[0]),
        pltpu.make_async_copy(old_ref, field_b.at[pl.ds(2, CX), pl.ds(LOW, CY)], load_sem.at[1]),
        pltpu.make_async_copy(code_ref, codes, load_sem.at[2]),
        pltpu.make_async_copy(hist_ref, hist, load_sem.at[3]),
        pltpu.make_async_copy(w_ref, wv.at[pl.ds(0, ENTRIES)], load_sem.at[4]),
    ]
    for load in loads:
        load.start()

    lane = lax.broadcasted_iota(jnp.int32, (CY, CZ), 1)
    zero_plane = jnp.zeros((CY, CZ), F32)

    def over_planes(body, init, unroll=8):
        def chunk(i, carry):
            return body([i * unroll + u for u in range(unroll)], carry)
        return lax.fori_loop(0, CX // unroll, chunk, init)

    def pack_z(xs, planes, shifts, carry):
        for x, plane in zip(xs, planes):
            carry = [
                jnp.where(lane == x, pltpu.roll(plane[k], lax.rem(x + shift, CZ), 1), held)
                for held, (k, shift) in zip(carry, shifts)]
        return carry

    def pack_now(turn, xs, planes, carry):
        carry = pack_z(
            xs, [(p,) for p in planes], ((0, 0), (0, CZ - 1), (0, 1), (0, 2)), carry)
        for x, plane in zip(xs, planes):
            for side, layer, y in ((0, 0, 0), (0, 1, 1), (1, 0, CY - 1), (1, 1, CY - 2)):
                stage[turn, 1, side, layer, pl.ds(x, 1), :] = plane[y:y + 1, :]
        return carry

    def pack_now_end(turn, carry):
        for value, (side, layer) in zip(carry, ((0, 0), (0, 1), (1, 0), (1, 1))):
            stage[turn, 2, side, layer] = value
        for side, layer, x in ((0, 0, 0), (0, 1, 1), (1, 0, CX - 1), (1, 1, CX - 2)):
            stage[turn, 0, side, layer] = field_a[x + 2, LOW:HIGH, :]

    def pack_rest(xs, carry):
        planes = [(field_b[x + 2, LOW:HIGH, :], codes[x].astype(F32)) for x in xs]
        carry = pack_z(xs, planes, ((0, 0), (1, 0), (0, 1), (1, 1)), carry)
        for x, plane in zip(xs, planes):
            for side, y in ((0, 0), (1, CY - 1)):
                for k in range(2):
                    stage[0, 1, side, 2 + k, pl.ds(x, 1), :] = plane[k][y:y + 1, :]
        return carry

    def pack_rest_end(carry):
        for value, (side, layer) in zip(carry, ((0, 2), (0, 3), (1, 2), (1, 3))):
            stage[0, 2, side, layer] = value
        for side, x in ((0, 0), (1, CX - 1)):
            stage[0, 0, side, 2] = field_b[x + 2, LOW:HIGH, :]
            stage[0, 0, side, 3] = codes[x].astype(F32)

    def halo_copy(turn, piece, axis, side):
        layers = pl.ds(2 * piece, 2)
        return pltpu.make_async_remote_copy(
            src_ref=stage.at[turn, axis, side, layers],
            dst_ref=land.at[turn, axis, 1 - side, layers],
            send_sem=halo_send.at[turn, piece, axis, side],
            recv_sem=halo_recv.at[turn, piece, axis, 1 - side],
            device_id=beside(axis, side), device_id_type=MESH,
        )

    def edge_copy(turn, edge):
        a, i, b, j = edge
        number, opposite = EDGES.index(edge), EDGES.index((a, 1 - i, b, 1 - j))
        source, target = stage.at[turn, b, j, 0], edges.at[turn, opposite]
        if (a, b) != (0, 2):
            source, target = source.at[pl.ds(24 * i, 8)], target.at[pl.ds(0, 8)]
        return pltpu.make_async_remote_copy(
            src_ref=source, dst_ref=target,
            send_sem=edge_send.at[turn, number], recv_sem=edge_recv.at[turn, opposite],
            device_id=across(edge), device_id_type=MESH,
        )

    def for_faces(act):
        for axis in range(3):
            for side in range(2):
                @pl.when(exists(axis, side))
                def _():
                    act(axis, side)

    def for_edges(act):
        for edge in EDGES:
            @pl.when(edge_exists(edge))
            def _():
                act(edge)

    def halo_start(turn, piece):
        for_faces(lambda axis, side: halo_copy(turn, piece, axis, side).start())
        if piece == 0:
            for_edges(lambda edge: edge_copy(turn, edge).start())

    def halo_wait_recv(turn, piece):
        for_faces(lambda axis, side: halo_copy(turn, piece, axis, 1 - side).wait_recv())
        if piece == 0:
            for_edges(lambda edge: edge_copy(
                turn, (edge[0], 1 - edge[1], edge[2], 1 - edge[3])).wait_recv())

    def halo_wait_send(turn, piece):
        for_faces(lambda axis, side: halo_copy(turn, piece, axis, side).wait_send())
        if piece == 0:
            for_edges(lambda edge: edge_copy(turn, edge).wait_send())

    loads[0].wait()
    four = [zero_plane] * 4

    def first_faces(xs, carry):
        return pack_now(0, xs, [field_a[x + 2, LOW:HIGH, :] for x in xs], carry)

    pack_now_end(0, over_planes(first_faces, four))
    pl.semaphore_wait(barrier, expected)
    halo_start(0, 0)
    loads[1].wait()
    loads[2].wait()
    pack_rest_end(over_planes(pack_rest, four))
    halo_start(0, 1)

    for axis in range(3):
        for side in range(2):
            @pl.when(jnp.logical_not(exists(axis, side)))
            def _():
                land[0, axis, side, 0:3] = jnp.zeros((3, CY, CZ), F32)
                land[0, axis, side, 3] = jnp.full((CY, CZ), 9.0, F32)
                land[1, axis, side, 0:2] = jnp.zeros((2, CY, CZ), F32)
    for number, edge in enumerate(EDGES):
        @pl.when(jnp.logical_not(edge_exists(edge)))
        def _():
            for turn in range(ROUNDS):
                edges[turn, number] = zero_plane

    for ref in (field_a, field_b):
        for x in (0, 1, CX + 2, CX + 3):
            ref[x] = jnp.zeros((PADROWS, CZ), F32)
        ref[2:CX + 2, 0:LOW, :] = jnp.zeros((CX, LOW, CZ), F32)
        ref[2:CX + 2, HIGH:, :] = jnp.zeros((CX, PADROWS - HIGH, CZ), F32)
    zlayer[...] = jnp.zeros_like(zlayer)
    for index in range(3):
        for x in (0, CX + 1):
            coef[index, x] = jnp.zeros((WIDE_HIGH - WIDE_LOW, CZ), F32)
        coef[index, 1:CX + 1, 0:8, :] = jnp.zeros((CX, 8, CZ), F32)
        coef[index, 1:CX + 1, 40:48, :] = jnp.zeros((CX, 8, CZ), F32)

    dirs = dirs_ref[...]
    targets = jnp.concatenate(
        [dirs[k:k + 1, :] for k in range(K_DEV)]
        + [jnp.full((1, PB - ENTRIES), -1, jnp.int32)], axis=1)
    targets = jnp.where(targets >= 0, targets, TARGETS).astype(F32)
    by_lane = jnp.broadcast_to(targets, (PB, PB))
    by_row = by_lane.T
    lanes = lax.broadcasted_iota(jnp.int32, (PB, PB), 1).astype(F32)
    rows = lax.broadcasted_iota(jnp.int32, (PB, PB), 0).astype(F32)

    def count(mask, axis):
        return jnp.sum(jnp.where(mask, 1.0, 0.0), axis=axis, keepdims=True)

    def even(amount):
        return 2.0 * jnp.floor(0.5 * (amount + 1.0))

    member = by_row == lanes
    along_lanes = count(member, 0)
    along_rows = count(by_lane == rows, 1)
    first_lanes = jnp.sum(jnp.where(rows < lanes, even(along_rows), 0.0), axis=0, keepdims=True)
    first_rows = jnp.sum(jnp.where(lanes < rows, even(along_lanes), 0.0), axis=1, keepdims=True)
    before = count(jnp.logical_and(by_lane == by_row, lanes < rows), 1)
    slot = before + jnp.sum(jnp.where(member, first_lanes, 0.0), axis=1, keepdims=True)
    taken = jnp.logical_and(slot == lanes, by_row < TARGETS)
    sequence = ENTRIES + jnp.sum(jnp.where(taken, rows - ENTRIES, 0.0), axis=0, keepdims=True)
    ends = jnp.where(along_lanes > 0, 0.5 * (first_lanes + even(along_lanes)), 0.0)
    opens = count(
        jnp.logical_and(jnp.logical_and(0.5 * first_rows == lanes, along_rows > 0), rows < TARGETS), 0)
    table[0:1, :] = sequence.astype(jnp.int32)
    table[1:2, :] = ends.astype(jnp.int32)
    table[2:3, :] = opens.astype(jnp.int32)
    table[3:8, :] = jnp.zeros((5, PB), jnp.int32)
    order_load = pltpu.make_async_copy(table, order, load_sem.at[7])
    order_load.start()

    def core_copy(half):
        return pltpu.make_async_remote_copy(
            src_ref=part.at[pl.ds(half * 4, 4), :, :, 1 - core],
            dst_ref=core_recv.at[pl.ds(half * 4, 4)],
            send_sem=core_ssem.at[half], recv_sem=core_rsem.at[half],
            device_id=sibling, device_id_type=MESH,
        )

    loads[3].wait()

    def widen(block, carry):
        signal[block, HOLD:, :] = jnp.zeros((TW + MAXOFF - HOLD, PB), F32)
        return carry

    lax.fori_loop(0, BLOCKS, widen, 0)
    for block in range(BLOCKS):
        signal[block, :HOLD, :] = hist[:, block * PB:(block + 1) * PB].astype(F32)
    trail[0] = jnp.zeros((TW, DB), F32)
    order_load.wait()
    loads[4].wait()

    wv[ENTRIES] = jnp.zeros((PB, DB), BF16)

    def far_pair(p):
        windows, blocks = [], []
        for u in range(2):
            entry = jnp.clip(order[0, 2 * p + u], 0, ENTRIES)
            k = jnp.minimum(lax.shift_right_logical(entry, 4), K_DEV - 1)
            block = jnp.bitwise_and(entry, BLOCKS - 1)
            windows.append(signal[block, pl.ds(delay_ref[k, block], TW), :].astype(BF16))
            blocks.append(wv[jnp.where(entry < ENTRIES, block * K_DEV + k, ENTRIES)])
        term = jnp.dot(
            jnp.concatenate(windows, axis=1), jnp.concatenate(blocks, axis=0),
            preferred_element_type=F32)
        trail[p + 1] = term + trail[jnp.where(order[2, p] > 0, 0, p)]

    def far_pairs(first, amount, unroll):
        def chunk(i, carry):
            for u in range(unroll):
                far_pair(first + i * unroll + u)
            return carry
        lax.fori_loop(0, amount // unroll, chunk, 0)

    def far_collect():
        for j in range(TARGETS):
            end = jnp.clip(order[1, j], 0, PAIRS)
            for quarter in range(4):
                found = trail[end, quarter * 128:(quarter + 1) * 128, :]
                part[j, quarter] = found.reshape(4, 2, ROWS, DB)

    def core_start():
        far_collect()
        for half in range(2):
            core_copy(half).start()

    def plane_coefficients(xs, carry):
        for x in xs:
            code = codes[x]
            for index, values in enumerate(COEFFICIENTS):
                coef[index, x + 1, 8:40, :] = jnp.where(
                    code == 0, values[0],
                    jnp.where(code == 1, values[1], jnp.where(code == 2, values[2], values[3])),
                ).astype(F32)
        return carry

    over_planes(plane_coefficients, 0)
    cell = surf_ref[...]
    cell_row = lax.shift_right_arithmetic(cell, 7)
    cell_lane = jnp.bitwise_and(cell, CZ - 1)

    def build_onehot(i, carry):
        rows = lax.broadcasted_iota(jnp.int32, (128, SLOT), 0) + i * 128
        onehot[pl.ds(pl.multiple_of(i * 128, 128), 128), :] = jnp.where(
            rows == cell_row, 1.0, 0.0).astype(BF16)
        return carry

    lax.fori_loop(0, CX * CY // 128, build_onehot, 0)
    samp_send[...] = jnp.zeros_like(samp_send)
    spad[...] = jnp.zeros_like(spad)

    def layer_coefficients(code):
        found = []
        for values in COEFFICIENTS:
            value = jnp.zeros_like(code)
            for number in range(4):
                value = jnp.where(code == float(number), values[number], value)
            found.append(value)
        return found

    def place_rest():
        halo_wait_recv(0, 1)
        for side in range(2):
            x = 1 if side == 0 else CX + 2
            y = LOW - 1 if side == 0 else HIGH
            field_b[x, LOW:HIGH, :] = land[0, 0, side, 2]
            along_x = layer_coefficients(land[0, 0, side, 3])
            along_y = layer_coefficients(land[0, 1, side, 3])
            along_z = layer_coefficients(land[0, 2, side, 3])
            olds = land[0, 1, side, 2]
            for index in range(3):
                coef[index, x - 1, 8:40, :] = along_x[index]
                zcoef[side, index] = along_z[index]
            for plane in range(CX):
                field_b[plane + 2, y:y + 1, :] = olds[plane:plane + 1, :]
                for index in range(3):
                    coef[index, plane + 1, y - WIDE_LOW:y - WIDE_LOW + 1, :] = (
                        along_y[index][plane:plane + 1, :])

    def place_now(turn):
        halo_wait_recv(turn, 0)
        for side in range(2):
            for layer in range(2):
                x = 1 - layer if side == 0 else CX + 2 + layer
                field_a[x, LOW:HIGH, :] = land[turn, 0, side, layer]

        def rows(xs, carry):
            held = [
                [land[turn, 1, side, layer, pl.ds(x, 1), :] for side in (0, 1) for layer in (0, 1)]
                for x in xs]
            for x, values in zip(xs, held):
                for y, value in zip((LOW - 1, LOW - 2, HIGH, HIGH + 1), values):
                    field_a[x + 2, y:y + 1, :] = value
            return carry

        over_planes(rows, 0)
        for i in range(2):
            for j in range(2):
                number = EDGES.index((0, i, 1, j))
                x, y = (CX + 2 if i else 1), (HIGH if j else LOW - 1)
                row = 0 if i else 7
                field_a[x, y:y + 1, :] = edges[turn, number, row:row + 1, :]
        for side in range(2):
            face = land[turn, 2, side, 0]
            below = edges[turn, EDGES.index((0, 0, 2, side))]
            above = edges[turn, EDGES.index((0, 1, 2, side))]
            face = jnp.where(lane == CZ - 1, pltpu.roll(below, CZ - CX, 1), face)
            face = jnp.where(lane == CX, pltpu.roll(above, CX, 1), face)
            zlayer[side, 8:40, :] = face
            zlayer[side, 7:8, :] = edges[turn, EDGES.index((1, 0, 2, side)), 7:8, :]
            zlayer[side, 40:41, :] = edges[turn, EDGES.index((1, 1, 2, side)), 0:1, :]

    def z_neighbours(here, low, high, x):
        lanes = lax.broadcasted_iota(jnp.int32, here.shape, 1)
        below = jnp.where(
            lanes == 0, pltpu.roll(low, lax.rem(CZ - x, CZ), 1), pltpu.roll(here, 1, 1))
        above = jnp.where(
            lanes == CZ - 1, pltpu.roll(high, lax.rem(2 * CZ - 1 - x, CZ), 1),
            pltpu.roll(here, CZ - 1, 1))
        return below + above

    def keep_rounded(slot, x, values):
        first = x * CY if isinstance(x, int) else pl.multiple_of(x * CY, CY)
        rounded[slot, pl.ds(first, CY), :] = values.astype(BF16)

    def wide_step(turn):
        for side in range(2):
            here = zlayer[side, 8:40, :]
            around = pltpu.roll(here, 1, 1) + pltpu.roll(here, CZ - 1, 1)
            around = around + (zlayer[side, 7:39, :] + zlayer[side, 9:41, :])
            around = around + (land[turn, 2, side, 1] + stage[turn, 2, side, 0])
            before = land[0, 2, side, 2] if turn == 0 else zkeep[side]
            zkeep[side] = (
                zcoef[side, 0] * here + zcoef[side, 1] * before + zcoef[side, 2] * around)
        low, high = zlayer[0], zlayer[1]

        def planes(xs):
            found = []
            for x in xs:
                here = field_a[x + 2, WIDE_LOW:WIDE_HIGH, :]
                around = (field_a[x + 1, WIDE_LOW:WIDE_HIGH, :]
                          + field_a[x + 3, WIDE_LOW:WIDE_HIGH, :])
                around = around + (field_a[x + 2, WIDE_LOW - 1:WIDE_HIGH - 1, :]
                                   + field_a[x + 2, WIDE_LOW + 1:WIDE_HIGH + 1, :])
                around = around + z_neighbours(here, low, high, x)
                before = field_b[x + 2, WIDE_LOW:WIDE_HIGH, :]
                found.append(
                    coef[0, x + 1] * here + coef[1, x + 1] * before + coef[2, x + 1] * around)
            for x, new in zip(xs, found):
                field_b[x + 2, WIDE_LOW:WIDE_HIGH, :] = new
            return found

        def inner(xs, carry):
            for x, new in zip(xs, planes(xs)):
                keep_rounded(0, x, new[8:40, :])
            return carry

        over_planes(inner, 0)
        planes([-1, CX])

    def close_step(turn):
        low, high = zkeep[0], zkeep[1]

        def planes(xs, carry):
            found = []
            for x in xs:
                here = field_b[x + 2, LOW:HIGH, :]
                around = field_b[x + 1, LOW:HIGH, :] + field_b[x + 3, LOW:HIGH, :]
                around = around + (
                    field_b[x + 2, LOW - 1:HIGH - 1, :] + field_b[x + 2, LOW + 1:HIGH + 1, :])
                around = around + z_neighbours(here, low, high, x)
                before = field_a[x + 2, LOW:HIGH, :]
                found.append(
                    coef[0, x + 1, 8:40] * here + coef[1, x + 1, 8:40] * before
                    + coef[2, x + 1, 8:40] * around)
            for x, new in zip(xs, found):
                field_a[x + 2, LOW:HIGH, :] = new
                keep_rounded(1, x, new)
            return carry if turn else pack_now(1, xs, found, carry)

        carry = over_planes(planes, 0 if turn else four)
        if turn == 0:
            pack_now_end(1, carry)
            halo_start(1, 0)

    def sample(step):
        picked = lax.dot_general(
            rounded[step % 2], onehot[...], (((0,), (0,)), ((), ())), preferred_element_type=F32)
        level = lax.broadcasted_iota(jnp.int32, (CZ, SLOT), 0)
        values = jnp.sum(jnp.where(level == cell_lane, picked, 0.0), axis=0, keepdims=True)
        if step < STEPS - 1:
            samp_send[4 + step:5 + step, :] = values
        else:
            last_send[...] = jnp.broadcast_to(values, (8, SLOT))

    axes = (("z", "y"), ("y", "z"))

    def index_on(axis):
        return z if axis == "z" else y

    def ring_copy(half, stage, kind, way):
        axis = axes[half][stage]
        place_now = index_on(axis)
        step_to = 1 if way == 0 else 3
        chunk = lax.rem(place_now + (2 if kind == 0 else step_to), 4)
        part = pl.ds(0 if (kind == 1) == (way == 1) else 2, 2)
        if stage == 0:
            source, target = sums.at[half, chunk, part], ring1.at[half, kind, way]
        else:
            source, target = totals.at[half, chunk, part], ring2.at[half, kind, way]
        return pltpu.make_async_remote_copy(
            src_ref=source, dst_ref=target,
            send_sem=ring_send.at[half, stage, kind, way],
            recv_sem=ring_recv.at[half, stage, kind, way],
            device_id=ring_neighbour(axis, step_to), device_id_type=MESH,
        )

    def core_finish(half):
        core_copy(half).wait_recv()

        for yy in range(4):
            for zz in range(4):
                total = (part[half * 4:half * 4 + 4, yy, zz, core]
                         + core_recv[half * 4:half * 4 + 4, yy, zz])
                if half == 0:
                    sums[0, zz, yy] = total
                else:
                    sums[1, yy, zz] = total

    def ring_begin(half, stage):
        for kind in (0, 1):
            for way in (0, 1):
                ring_copy(half, stage, kind, way).start()

    def ring_forward(half, stage):
        held = sums if stage == 0 else totals
        arrived = ring1 if stage == 0 else ring2
        place_now = index_on(axes[half][stage])
        for way in (0, 1):
            ring_copy(half, stage, 0, way).wait_recv()
            chunk = lax.rem(place_now + (1 if way == 0 else 3), 4)
            first = 0 if way == 0 else 2
            held[half, chunk, first:first + 2] = (
                held[half, chunk, first:first + 2] + arrived[half, 0, way])
            ring_copy(half, stage, 2, way).start()

    def ring_end(half, stage):
        held = sums if stage == 0 else totals
        arrived = ring1 if stage == 0 else ring2
        place_now = index_on(axes[half][stage])
        for kind in (1, 2):
            for way in (0, 1):
                ring_copy(half, stage, kind, way).wait_recv()
        first = held[half, place_now, 0:2] + (arrived[half, 2, 0] + arrived[half, 1, 1])
        second = held[half, place_now, 2:4] + (arrived[half, 1, 0] + arrived[half, 2, 1])
        return first, second

    def samp_copy(last, offset, arriving=False):
        source, target = (last_send, last_all) if last else (samp_send, samp_all)
        slot = lax.rem(gy + NY_DEV - offset, NY_DEV) if arriving else gy
        return pltpu.make_async_remote_copy(
            src_ref=source, dst_ref=target.at[slot],
            send_sem=samp_ssem.at[last, offset - 1], recv_sem=samp_rsem.at[last, offset - 1],
            device_id=(gx, lax.rem(gy + offset, NY_DEV), gz), device_id_type=MESH,
        )

    def samp_start(last):
        for offset in range(1, NY_DEV):
            samp_copy(last, offset).start()
        if last:
            last_all[gy] = last_send[...]
        else:
            samp_all[gy] = samp_send[...]

    def samp_wait(last):
        for offset in range(1, NY_DEV):
            samp_copy(last, offset, True).wait_recv()

    row = lax.broadcasted_iota(jnp.int32, (8, PB), 0)
    width = 4 * K_DEV * PB

    def entry_rows(i, carry):
        held = []
        for block in [i * 4 + u for u in range(4)]:
            for entry in range(K_DEV):
                offset = delay_ref[entry, block]
                target = dir_ref[entry, block]
                early = spad[block, pl.ds(offset + 4, 8), :]
                late = spad[block, pl.ds(offset, 8), :]
                pair = jnp.where(row < 4, early, late)
                pieces = []
                for k in range(TARGETS // 2):
                    wanted = jnp.where(row < 4, 2 * k, 2 * k + 1)
                    pieces.append(jnp.where(wanted == target, pair, 0.0))
                held.append(jnp.concatenate(pieces, axis=0).astype(BF16))
        lhs[:, pl.ds(pl.multiple_of(i * width, width), width)] = jnp.concatenate(held, axis=1)
        return carry

    def last_rows():
        for brick in range(NY_DEV):
            held = []
            for i in range(SLOT // PB):
                block = brick * (SLOT // PB) + i
                samples = last_all[brick, :, i * PB:(i + 1) * PB]
                for entry in range(K_DEV):
                    target = jnp.where(
                        delay_ref[entry, block] == MAXOFF, dir_ref[entry, block], -1)
                    held.append(jnp.where(row == target, samples, 0.0))
            picked = jnp.concatenate(held, axis=1)
            last_lhs[:, brick * width:(brick + 1) * width] = jnp.concatenate(
                [picked, jnp.zeros_like(picked)], axis=0).astype(BF16)

    def all_weights():
        return wv[:ENTRIES].reshape(ENTRIES * PB, DB)

    def corr_copy(last, member):
        source, target = (last_out, last_in) if last else (corr_out, corr_in)
        return pltpu.make_async_remote_copy(
            src_ref=source, dst_ref=target.at[member],
            send_sem=last_ssem if last else corr_ssem,
            recv_sem=(last_rsem if last else corr_rsem).at[member],
            device_id=owner, device_id_type=MESH,
        )

    def corr_start(last):
        @pl.when(jnp.logical_not(is_owner))
        def _():
            corr_copy(last, group).start()

    far_pairs(0, PAIRS, 13)
    core_start()
    place_rest()
    place_now(0)
    wide_step(0)
    close_step(0)
    sample(0)
    sample(1)
    for half in range(2):
        core_finish(half)
        ring_begin(half, 0)
    place_now(1)
    wide_step(1)
    save_prev = pltpu.make_async_copy(
        field_b.at[pl.ds(2, CX), pl.ds(LOW, CY)], prev_ref, load_sem.at[5])
    save_prev.start()
    close_step(1)
    sample(3)
    samp_start(1)
    sample(2)
    samp_start(0)
    save_next = pltpu.make_async_copy(
        field_a.at[pl.ds(2, CX), pl.ds(LOW, CY)], next_ref, load_sem.at[6])
    save_next.start()
    for half in range(2):
        ring_forward(half, 0)
    samp_wait(0)
    for brick in range(NY_DEV):
        for i in range(SLOT // PB):
            spad[brick * (SLOT // PB) + i, 32:40, :] = samp_all[brick, :, i * PB:(i + 1) * PB]
    lax.fori_loop(0, BLOCKS // 4, entry_rows, 0)
    corr_out[...] = jnp.dot(lhs[...], all_weights(), preferred_element_type=F32)
    corr_start(0)
    for half in range(2):
        first, second = ring_end(half, 0)
        totals[half, 0:2] = first
        totals[half, 2:4] = second
        ring_begin(half, 1)
    samp_wait(1)
    last_rows()
    last_out[...] = jnp.dot(
        last_lhs[...], all_weights(), preferred_element_type=F32)[:8]
    corr_start(1)
    for half in range(2):
        ring_forward(half, 1)
    for half in range(2):
        first, second = ring_end(half, 1)
        for j in range(4):
            columns = slice((half * 4 + j) * DB, (half * 4 + j + 1) * DB)
            far_ref[:, columns] = first[j] if j < 2 else second[j - 2]

    @pl.when(is_owner)
    def _():
        def arrivals(last):
            def one(member, carry):
                corr_copy(last, member).wait_recv()
                return carry
            lax.fori_loop(0, OWNERS - 1, one, 0)

        arrivals(0)
        total = corr_out[...]
        for member in range(OWNERS - 1):
            total = total + corr_in[member]
        for j in range(TARGETS):
            piece = total[(j // 2) * 8:(j // 2) * 8 + 8, :]
            if j % 2 == 0:
                piece = pltpu.roll(piece, 4, 0)
            columns = slice(j * DB, (j + 1) * DB)
            far_ref[8:16, columns] = far_ref[8:16, columns] + jnp.where(row >= 4, piece, 0.0)
        arrivals(1)
        total = last_out[...]
        for member in range(OWNERS - 1):
            total = total + last_in[member]
        for j in range(TARGETS):
            columns = slice(j * DB, (j + 1) * DB)
            far_ref[15:16, columns] = far_ref[15:16, columns] + total[j:j + 1, :]

    for turn, piece in ((0, 0), (0, 1), (1, 0)):
        halo_wait_send(turn, piece)
    for half in range(2):
        core_copy(half).wait_send()
        for stage in range(2):
            for kind in range(3):
                for way in range(2):
                    ring_copy(half, stage, kind, way).wait_send()
    for last in range(2):
        for offset in range(1, NY_DEV):
            samp_copy(last, offset).wait_send()

    @pl.when(jnp.logical_not(is_owner))
    def _():
        corr_copy(0, group).wait_send()
        corr_copy(1, group).wait_send()

    save_prev.wait()
    save_next.wait()


def hall(dirs, delays, surf_index, now, old, code, history, weights):
    any_space = pl.BlockSpec(memory_space=pl.ANY)
    smem = pl.BlockSpec(memory_space=pltpu.SMEM)
    vmem = pl.BlockSpec(memory_space=pltpu.VMEM)
    dma = pltpu.SemaphoreType.DMA
    brick = jax.ShapeDtypeStruct((CX, CY, CZ), F32)
    return pl.pallas_call(
        hall_kernel,
        out_shape=(brick, brick, jax.ShapeDtypeStruct((ROWS, TARGETS * DB), F32)),
        in_specs=[smem, smem, vmem, vmem] + [any_space] * 5,
        out_specs=(any_space, any_space, vmem),
        scratch_shapes=[
            pltpu.VMEM((CX + 4, PADROWS, CZ), F32),
            pltpu.VMEM((CX + 4, PADROWS, CZ), F32),
            pltpu.VMEM((CX, CY, CZ), jnp.int32),
            pltpu.VMEM((3, CX + 2, WIDE_HIGH - WIDE_LOW, CZ), F32),
            pltpu.VMEM((ROUNDS, 3, 2, 4, CY, CZ), F32),
            pltpu.VMEM((ROUNDS, 3, 2, 4, CY, CZ), F32),
            pltpu.VMEM((ROUNDS, len(EDGES), CY, CZ), F32),
            pltpu.VMEM((2, 48, CZ), F32),
            pltpu.VMEM((2, CY, CZ), F32),
            pltpu.VMEM((2, 3, CY, CZ), F32),
            pltpu.VMEM((CX * CY, SLOT), BF16),
            pltpu.VMEM((2, CX * CY, CZ), BF16),
            pltpu.VMEM((8, SLOT), F32),
            pltpu.VMEM((NY_DEV, 8, SLOT), F32),
            pltpu.VMEM((8, SLOT), F32),
            pltpu.VMEM((NY_DEV, 8, SLOT), F32),
            pltpu.VMEM((BLOCKS, 48, PB), F32),
            pltpu.VMEM((32, ENTRIES * PB), BF16),
            pltpu.VMEM((16, ENTRIES * PB), BF16),
            pltpu.VMEM((ENTRIES + 1, PB, DB), BF16),
            pltpu.VMEM((BLOCKS, TW + MAXOFF, PB), F32),
            pltpu.VMEM((PAIRS + 1, TW, DB), F32),
            pltpu.VMEM((8, PB), jnp.int32),
            pltpu.SMEM((8, PB), jnp.int32),
            pltpu.VMEM((HOLD, BLOCKS * PB), BF16),
            pltpu.VMEM((TARGETS, 4, 4, 2, ROWS, DB), F32),
            pltpu.VMEM((TARGETS, 4, 4, ROWS, DB), F32),
            pltpu.VMEM((2, 4, 4, 4, ROWS, DB), F32),
            pltpu.VMEM((2, 4, 4, ROWS, DB), F32),
            pltpu.VMEM((2, 3, 2, 2, 4, ROWS, DB), F32),
            pltpu.VMEM((2, 3, 2, 2, ROWS, DB), F32),
            pltpu.VMEM((32, DB), F32),
            pltpu.VMEM((OWNERS, 32, DB), F32),
            pltpu.VMEM((8, DB), F32),
            pltpu.VMEM((OWNERS, 8, DB), F32),
            dma((8,)),
            dma((ROUNDS, 2, 3, 2)), dma((ROUNDS, 2, 3, 2)),
            dma((ROUNDS, len(EDGES))), dma((ROUNDS, len(EDGES))),
            dma((2, 3)), dma((2, 3)),
            dma((2,)), dma((2,)),
            dma((2, 2, 3, 2)), dma((2, 2, 3, 2)),
            dma, dma((OWNERS,)), dma, dma((OWNERS,)),
        ],
        compiler_params=pltpu.CompilerParams(
            collective_id=0, has_side_effects=True, vmem_limit_bytes=58 * 1024 * 1024),
    )(dirs, delays, dirs, surf_index, history, now, old, code, weights)


def save_kernel(*refs):
    sources, targets, held, sems = refs[:3], refs[3:6], refs[6:9], refs[9]
    arrivals = [pltpu.make_async_copy(sources[i], held[i], sems.at[0, i]) for i in range(3)]
    leaves = [pltpu.make_async_copy(held[i], targets[i], sems.at[1, i]) for i in range(3)]
    for copy in arrivals:
        copy.start()
    for arrival, leave in zip(arrivals, leaves):
        arrival.wait()
        leave.start()
    for copy in leaves:
        copy.wait()


def save(arrays):
    any_space = pl.BlockSpec(memory_space=pl.ANY)
    return pl.pallas_call(
        save_kernel,
        out_shape=tuple(jax.ShapeDtypeStruct(a.shape, a.dtype) for a in arrays),
        in_specs=[any_space] * 3,
        out_specs=(any_space,) * 3,
        scratch_shapes=[pltpu.VMEM(a.shape, a.dtype) for a in arrays]
        + [pltpu.SemaphoreType.DMA((2, 3))],
    )(*arrays)


def shards(pressure_now, pressure_old, cell_code, surf_index, history, dir_slot, delay, weights):
    flat_weights = weights.reshape(BLOCKS * K_DEV, PB, DB)
    return save(hall(
        dir_slot.T, delay.T, surf_index, pressure_now, pressure_old, cell_code, history,
        flat_weights))


def solution(mesh):
    return jax.shard_map(
        shards,
        mesh=mesh,
        in_specs=(
            P("gx", "gy", "gz"),
            P("gx", "gy", "gz"),
            P("gx", "gy", "gz"),
            P(("gx", "gz"), "gy"),
            P(None, ("gx", "gz")),
            P(("gx", "gz"), "gy"),
            P(("gx", "gz"), "gy"),
            P(("gx", "gz"), "gy", None, None),
        ),
        out_specs=(P("gx", "gy", "gz"), P("gx", "gy", "gz"), P(("gx", "gz"), "gy")),
        check_vma=False,
    )
```

```python
import functools

import jax
import jax.numpy as jnp
import numpy as np
from jax import lax
from jax.experimental import pallas as pl
from jax.experimental.pallas import tpu as pltpu
from jax.sharding import PartitionSpec as P

MESH = pl.DeviceIdType.MESH
F32 = jnp.float32
BF16 = jnp.bfloat16

STEPS = 4
CX, CY, CZ = 32, 32, 128
SLOT = 512
TW = 512
MAXOFF = 32
HOLD = 540
PB = 128
DB = 128
K_DEV = 6
BLOCKS = 16
ENTRIES = K_DEV * BLOCKS
PAIRS = ENTRIES // 2 + 4
TARGETS = 8
OWNERS = 32
ROWS = 16
NX_DEV, NY_DEV, NZ_DEV = 8, 4, 4
LOW, HIGH = 8, 40
PADROWS = 48


def coefficient_table():
    speeds = np.array([0.32, 0.26, 0.19, 0.11], np.float32).astype(np.float64)
    damping = np.array([0.0, 0.02, 0.08, 0.3], np.float32).astype(np.float64)
    here = (2.0 - 6.0 * speeds) / (1.0 + damping)
    before = -(1.0 - damping) / (1.0 + damping)
    around = speeds / (1.0 + damping)
    return [[float(np.float32(v)) for v in row] for row in (here, before, around)]


COEFFICIENTS = coefficient_table()


def hall_kernel(
    dir_ref, delay_ref, dirs_ref, surf_ref, hist_ref, now_ref, old_ref, code_ref, w_ref,
    next_ref, prev_ref, far_ref,
    field_a, field_b, codes, coef, ystage, zstage, xrecv, yrecv, zrecv,
    onehot, cellmask, rounded, samp_send, samp_all, last_send, last_all, spad, lhs, last_lhs, wv,
    signal, trail, table, order, hist, part, core_recv, sums, totals, ring1, ring2, corr_out, corr_in, last_out, last_in,
    load_sem, halo_send, halo_recv, samp_ssem, samp_rsem,
    core_ssem, core_rsem, ring_send, ring_recv, direct_send, direct_recv, corr_ssem, corr_rsem, last_ssem, last_rsem,
):
    fields = (field_a, field_b)
    gx, gy, gz = lax.axis_index("gx"), lax.axis_index("gy"), lax.axis_index("gz")
    y, z_hi = gx // 2, lax.rem(gx, 2)
    z_lo, core = gz // 2, lax.rem(gz, 2)
    z = z_hi * 2 + z_lo
    group = gx * 4 + gz
    is_owner = group == OWNERS - 1

    def place(yy, zz):
        return (yy * 2 + zz // 2, gy, lax.rem(zz, 2) * 2 + core)

    def ring_neighbour(axis, offset):
        if axis == "z":
            return place(y, lax.rem(z + offset, 4))
        return place(lax.rem(y + offset, 4), z)

    sibling = (gx, gy, z_lo * 2 + 1 - core)
    owner = (NX_DEV - 1, gy, NZ_DEV - 1)
    coords = (gx, gy, gz)
    extents = (NX_DEV, NY_DEV, NZ_DEV)

    def beside(axis, side):
        moved = list(coords)
        moved[axis] = coords[axis] + (1 if side else -1)
        return tuple(moved)

    def exists(axis, side):
        return coords[axis] < extents[axis] - 1 if side else coords[axis] > 0

    barrier = pltpu.get_barrier_semaphore()

    def greet(device):
        pl.semaphore_signal(barrier, inc=1, device_id=device, device_id_type=MESH)

    expected = jnp.int32(10)
    for axis in range(3):
        for side in range(2):
            @pl.when(exists(axis, side))
            def _():
                greet(beside(axis, side))
            expected = expected + exists(axis, side).astype(jnp.int32)
    greet(sibling)
    for axis in ("y", "z"):
        for offset in (1, 2, 3):
            greet(ring_neighbour(axis, offset))
    for offset in range(1, NY_DEV):
        greet((gx, lax.rem(gy + offset, NY_DEV), gz))

    @pl.when(is_owner)
    def _():
        def greet_one(member, carry):
            greet((member // 4, gy, lax.rem(member, 4)))
            return carry
        lax.fori_loop(0, OWNERS - 1, greet_one, 0)

    expected = expected + jnp.where(is_owner, 0, 1)

    loads = [
        pltpu.make_async_copy(now_ref, field_a.at[pl.ds(1, CX), pl.ds(LOW, CY)], load_sem.at[0]),
        pltpu.make_async_copy(hist_ref, hist, load_sem.at[3]),
        pltpu.make_async_copy(w_ref, wv.at[pl.ds(0, ENTRIES)], load_sem.at[4]),
        pltpu.make_async_copy(code_ref, codes, load_sem.at[2]),
        pltpu.make_async_copy(old_ref, field_b.at[pl.ds(1, CX), pl.ds(LOW, CY)], load_sem.at[1]),
    ]
    for load in loads:
        load.start()

    lane = lax.broadcasted_iota(jnp.int32, (CY, CZ), 1)
    zero_plane = jnp.zeros((CY, CZ), F32)

    def over_planes(body, init, unroll=8):
        def chunk(i, carry):
            return body([i * unroll + u for u in range(unroll)], carry)
        return lax.fori_loop(0, CX // unroll, chunk, init)

    def take_faces(step, xs, planes, held):
        for x, plane in zip(xs, planes):
            mine = jnp.logical_or(lane == 2 * x, lane == lax.rem(2 * x + CZ - 1, CZ))
            held = jnp.where(mine, pltpu.roll(plane, 2 * x, 1), held)
        for x, plane in zip(xs, planes):
            ystage[step, 0, pl.ds(x, 1), :] = plane[0:1, :]
            ystage[step, 1, pl.ds(x, 1), :] = plane[CY - 1:CY, :]
        return held

    def halo_copy(step, axis, side):
        current = step % 2
        if axis == 0:
            source = fields[current].at[CX if side else 1, pl.ds(LOW, CY)]
            target = xrecv.at[step, 1 - side]
        elif axis == 1:
            source, target = ystage.at[step, side], yrecv.at[step, 1 - side]
        else:
            source, target = zstage.at[step], zrecv.at[step, 1 - side]
        return pltpu.make_async_remote_copy(
            src_ref=source, dst_ref=target,
            send_sem=halo_send.at[step, axis, side],
            recv_sem=halo_recv.at[step, axis, 1 - side],
            device_id=beside(axis, side), device_id_type=MESH,
        )

    def halo_start(step):
        for axis in range(3):
            for side in range(2):
                @pl.when(exists(axis, side))
                def _():
                    halo_copy(step, axis, side).start()

    def halo_wait_send(step, axes=(0, 1, 2)):
        for axis in axes:
            for side in range(2):
                @pl.when(exists(axis, side))
                def _():
                    halo_copy(step, axis, side).wait_send()

    def halo_wait_recv(step, axes):
        for axis in axes:
            buffer = (xrecv, yrecv, zrecv)[axis]
            for side in range(2):
                @pl.when(exists(axis, side))
                def _():
                    halo_copy(step, axis, 1 - side).wait_recv()
                @pl.when(jnp.logical_not(exists(axis, side)))
                def _():
                    buffer[step, side] = zero_plane

    loads[0].wait()

    def first_faces(xs, carry):
        return take_faces(0, xs, [field_a[x + 1, LOW:HIGH, :] for x in xs], carry)

    zstage[0] = over_planes(first_faces, zero_plane)

    pl.semaphore_wait(barrier, expected)
    halo_start(0)

    dirs = dirs_ref[...]
    targets = jnp.concatenate(
        [dirs[k:k + 1, :] for k in range(K_DEV)]
        + [jnp.full((1, PB - ENTRIES), -1, jnp.int32)], axis=1)
    targets = jnp.where(targets >= 0, targets, TARGETS).astype(F32)
    by_lane = jnp.broadcast_to(targets, (PB, PB))
    by_row = by_lane.T
    lanes = lax.broadcasted_iota(jnp.int32, (PB, PB), 1).astype(F32)
    rows = lax.broadcasted_iota(jnp.int32, (PB, PB), 0).astype(F32)

    def count(mask, axis):
        return jnp.sum(jnp.where(mask, 1.0, 0.0), axis=axis, keepdims=True)

    def even(amount):
        return 2.0 * jnp.floor(0.5 * (amount + 1.0))

    member = by_row == lanes
    along_lanes = count(member, 0)
    along_rows = count(by_lane == rows, 1)
    first_lanes = jnp.sum(jnp.where(rows < lanes, even(along_rows), 0.0), axis=0, keepdims=True)
    first_rows = jnp.sum(jnp.where(lanes < rows, even(along_lanes), 0.0), axis=1, keepdims=True)
    before = count(jnp.logical_and(by_lane == by_row, lanes < rows), 1)
    slot = before + jnp.sum(jnp.where(member, first_lanes, 0.0), axis=1, keepdims=True)
    taken = jnp.logical_and(slot == lanes, by_row < TARGETS)
    sequence = ENTRIES + jnp.sum(jnp.where(taken, rows - ENTRIES, 0.0), axis=0, keepdims=True)
    ends = jnp.where(along_lanes > 0, 0.5 * (first_lanes + even(along_lanes)), 0.0)
    opens = count(
        jnp.logical_and(jnp.logical_and(0.5 * first_rows == lanes, along_rows > 0), rows < TARGETS), 0)
    table[0:1, :] = sequence.astype(jnp.int32)
    table[1:2, :] = ends.astype(jnp.int32)
    table[2:3, :] = opens.astype(jnp.int32)
    table[3:8, :] = jnp.zeros((5, PB), jnp.int32)
    order_load = pltpu.make_async_copy(table, order, load_sem.at[7])
    order_load.start()

    def core_copy(half):
        return pltpu.make_async_remote_copy(
            src_ref=part.at[pl.ds(half * 4, 4), :, :, 1 - core],
            dst_ref=core_recv.at[pl.ds(half * 4, 4)],
            send_sem=core_ssem.at[half], recv_sem=core_rsem.at[half],
            device_id=sibling, device_id_type=MESH,
        )

    loads[1].wait()

    def widen(block, carry):
        signal[block, HOLD:, :] = jnp.zeros((TW + MAXOFF - HOLD, PB), F32)
        return carry

    lax.fori_loop(0, BLOCKS, widen, 0)
    for block in range(BLOCKS):
        signal[block, :HOLD, :] = hist[:, block * PB:(block + 1) * PB].astype(F32)
    trail[0] = jnp.zeros((TW, DB), F32)
    order_load.wait()
    loads[2].wait()

    wv[ENTRIES] = jnp.zeros((PB, DB), BF16)

    def far_pair(p):
        windows, blocks = [], []
        for u in range(2):
            entry = jnp.clip(order[0, 2 * p + u], 0, ENTRIES)
            k = jnp.minimum(lax.shift_right_logical(entry, 4), K_DEV - 1)
            block = jnp.bitwise_and(entry, BLOCKS - 1)
            windows.append(signal[block, pl.ds(delay_ref[k, block], TW), :].astype(BF16))
            blocks.append(wv[jnp.where(entry < ENTRIES, block * K_DEV + k, ENTRIES)])
        term = jnp.dot(
            jnp.concatenate(windows, axis=1), jnp.concatenate(blocks, axis=0),
            preferred_element_type=F32)
        trail[p + 1] = term + trail[jnp.where(order[2, p] > 0, 0, p)]

    def far_pairs(first, amount, unroll):
        def chunk(i, carry):
            for u in range(unroll):
                far_pair(first + i * unroll + u)
            return carry
        lax.fori_loop(0, amount // unroll, chunk, 0)

    def far_collect():
        for j in range(TARGETS):
            end = jnp.clip(order[1, j], 0, PAIRS)
            for quarter in range(4):
                found = trail[end, quarter * 128:(quarter + 1) * 128, :]
                part[j, quarter] = found.reshape(4, 2, ROWS, DB)

    def core_start():
        far_collect()
        for half in range(2):
            core_copy(half).start()

    loads[3].wait()

    def plane_coefficients(xs, carry):
        for x in xs:
            code = codes[x]
            for index, values in enumerate(COEFFICIENTS):
                coef[index, x] = jnp.where(
                    code == 0, values[0],
                    jnp.where(code == 1, values[1], jnp.where(code == 2, values[2], values[3])),
                ).astype(F32)
        return carry

    over_planes(plane_coefficients, 0)
    slot_lane = lax.broadcasted_iota(jnp.int32, (PB, PB), 1)
    for i in range(SLOT // PB):
        slots = slice(i * PB, (i + 1) * PB)
        cell = jnp.broadcast_to(surf_ref[:, slots].astype(F32), (PB, PB)).T.astype(jnp.int32)
        cell_row = lax.shift_right_arithmetic(cell, 7)
        cellmask[slots, :] = jnp.where(
            slot_lane == jnp.bitwise_and(cell, CZ - 1), 1.0, 0.0)
        for q in range(CX * CY // PB):
            onehot[slots, q * PB:(q + 1) * PB] = jnp.where(
                slot_lane + q * PB == cell_row, 1.0, 0.0).astype(BF16)
    samp_send[...] = jnp.zeros_like(samp_send)
    spad[...] = jnp.zeros_like(spad)
    loads[4].wait()

    def leap(step):
        here_ref, other_ref = fields[step % 2], fields[1 - step % 2]
        last = step == STEPS - 1
        halo_wait_recv(step, (1, 2))

        def y_rows(xs, carry):
            rows = [(yrecv[step, 0, pl.ds(x, 1), :], yrecv[step, 1, pl.ds(x, 1), :]) for x in xs]
            for x, (low, high) in zip(xs, rows):
                here_ref[x + 1, LOW - 1:LOW, :] = low
                here_ref[x + 1, HIGH:HIGH + 1, :] = high
            return carry

        over_planes(y_rows, 0, 16)
        z_halo = jnp.where(
            jnp.bitwise_and(lane, 1) == 0,
            pltpu.roll(zrecv[step, 0], 1, 1), pltpu.roll(zrecv[step, 1], CZ - 1, 1))
        ends = jnp.logical_or(lane == 0, lane == CZ - 1)

        def plane_step(xs, carry):
            planes = []
            for x in xs:
                here = here_ref[x + 1, LOW:HIGH, :]
                around = here_ref[x, LOW:HIGH, :] + here_ref[x + 2, LOW:HIGH, :]
                around = around + (
                    here_ref[x + 1, LOW - 1:HIGH - 1, :] + here_ref[x + 1, LOW + 1:HIGH + 1, :])
                beside_z = (jnp.where(lane == 0, 0.0, pltpu.roll(here, 1, 1))
                            + jnp.where(lane == CZ - 1, 0.0, pltpu.roll(here, CZ - 1, 1)))
                outside = pltpu.roll(z_halo, lax.rem(2 * (CZ - x), CZ), 1)
                around = around + (beside_z + jnp.where(ends, outside, 0.0))
                before = other_ref[x + 1, LOW:HIGH, :]
                planes.append(coef[0, x] * here + coef[1, x] * before + coef[2, x] * around)
            for x, new in zip(xs, planes):
                other_ref[x + 1, LOW:HIGH, :] = new
                rounded[step % 2, pl.ds(x * CY if isinstance(x, int) else pl.multiple_of(x * CY, CY), CY), :] = new.astype(BF16)
            if last:
                return carry
            return take_faces(step + 1, xs, planes, carry)

        def inner(i, carry):
            return plane_step([1 + i * 10 + u for u in range(10)], carry)

        carry = lax.fori_loop(
            0, (CX - 2) // 10, inner, 0 if last else zero_plane)
        halo_wait_recv(step, (0,))
        if step > 0:
            halo_wait_send(step - 1, (0,))
        here_ref[0, LOW:HIGH, :] = xrecv[step, 0]
        here_ref[CX + 1, LOW:HIGH, :] = xrecv[step, 1]
        carry = plane_step([0, CX - 1], carry)
        if not last:
            zstage[step + 1] = carry
            halo_start(step + 1)

    def sample(step):
        picked = jnp.dot(onehot[...], rounded[step % 2], preferred_element_type=F32)
        values = lax.dot_general(
            jnp.ones((8, CZ), BF16), (picked * cellmask[...]).astype(BF16),
            (((1,), (1,)), ((), ())), preferred_element_type=F32)
        if step < STEPS - 1:
            samp_send[4 + step:5 + step, :] = values[0:1, :]
        else:
            last_send[...] = values

    axes = (("z", "y"), ("y", "z"))

    def index_on(axis):
        return z if axis == "z" else y

    def ring_copy(half, kind, way):
        axis = axes[half][0]
        place_now = index_on(axis)
        step_to = 1 if way == 0 else 3
        chunk = lax.rem(place_now + (2 if kind == 0 else step_to), 4)
        part_now = pl.ds(0 if (kind == 1) == (way == 1) else 2, 2)
        return pltpu.make_async_remote_copy(
            src_ref=sums.at[half, chunk, part_now], dst_ref=ring1.at[half, kind, way],
            send_sem=ring_send.at[half, kind, way],
            recv_sem=ring_recv.at[half, kind, way],
            device_id=ring_neighbour(axis, step_to), device_id_type=MESH,
        )

    def direct_copy(half, offset):
        axis = axes[half][1]
        return pltpu.make_async_remote_copy(
            src_ref=totals.at[half, lax.rem(index_on(axis) + offset, 4)],
            dst_ref=ring2.at[half, offset - 1],
            send_sem=direct_send.at[half, offset - 1],
            recv_sem=direct_recv.at[half, offset - 1],
            device_id=ring_neighbour(axis, offset), device_id_type=MESH,
        )

    def core_finish(half):
        core_copy(half).wait_recv()

        for yy in range(4):
            for zz in range(4):
                total = (part[half * 4:half * 4 + 4, yy, zz, core]
                         + core_recv[half * 4:half * 4 + 4, yy, zz])
                if half == 0:
                    sums[0, zz, yy] = total
                else:
                    sums[1, yy, zz] = total

    def ring_begin(half):
        for kind in (0, 1):
            for way in (0, 1):
                ring_copy(half, kind, way).start()

    def ring_forward(half):
        place_now = index_on(axes[half][0])
        for way in (0, 1):
            ring_copy(half, 0, way).wait_recv()
            chunk = lax.rem(place_now + (1 if way == 0 else 3), 4)
            first = 0 if way == 0 else 2
            sums[half, chunk, first:first + 2] = (
                sums[half, chunk, first:first + 2] + ring1[half, 0, way])
            ring_copy(half, 2, way).start()

    def ring_end(half):
        place_now = index_on(axes[half][0])
        for kind in (1, 2):
            for way in (0, 1):
                ring_copy(half, kind, way).wait_recv()
        totals[half, 0:2] = sums[half, place_now, 0:2] + (ring1[half, 2, 0] + ring1[half, 1, 1])
        totals[half, 2:4] = sums[half, place_now, 2:4] + (ring1[half, 1, 0] + ring1[half, 2, 1])
        for offset in (2, 1, 3):
            direct_copy(half, offset).start()

    def direct_end(half):
        for offset in (1, 2, 3):
            direct_copy(half, offset).wait_recv()
        result = totals[half, index_on(axes[half][1])]
        result = result + (ring2[half, 0] + (ring2[half, 1] + ring2[half, 2]))
        for j in range(4):
            columns = slice((half * 4 + j) * DB, (half * 4 + j + 1) * DB)
            far_ref[:, columns] = result[j]

    def samp_copy(last, offset, arriving=False):
        source, target = (last_send, last_all) if last else (samp_send, samp_all)
        slot = lax.rem(gy + NY_DEV - offset, NY_DEV) if arriving else gy
        return pltpu.make_async_remote_copy(
            src_ref=source, dst_ref=target.at[slot],
            send_sem=samp_ssem.at[last, offset - 1], recv_sem=samp_rsem.at[last, offset - 1],
            device_id=(gx, lax.rem(gy + offset, NY_DEV), gz), device_id_type=MESH,
        )

    def samp_start(last):
        for offset in range(1, NY_DEV):
            samp_copy(last, offset).start()
        if last:
            last_all[gy] = last_send[...]
        else:
            samp_all[gy] = samp_send[...]

    def samp_wait(last):
        for offset in range(1, NY_DEV):
            samp_copy(last, offset, True).wait_recv()

    row = lax.broadcasted_iota(jnp.int32, (8, PB), 0)
    width = 4 * K_DEV * PB

    def entry_rows(i, carry):
        held = []
        for block in [i * 4 + u for u in range(4)]:
            for entry in range(K_DEV):
                offset = delay_ref[entry, block]
                target = dir_ref[entry, block]
                early = spad[block, pl.ds(offset + 4, 8), :]
                late = spad[block, pl.ds(offset, 8), :]
                pair = jnp.where(row < 4, early, late)
                pieces = []
                for k in range(TARGETS // 2):
                    wanted = jnp.where(row < 4, 2 * k, 2 * k + 1)
                    pieces.append(jnp.where(wanted == target, pair, 0.0))
                held.append(jnp.concatenate(pieces, axis=0).astype(BF16))
        lhs[:, pl.ds(pl.multiple_of(i * width, width), width)] = jnp.concatenate(held, axis=1)
        return carry

    def last_rows():
        for brick in range(NY_DEV):
            held = []
            for i in range(SLOT // PB):
                block = brick * (SLOT // PB) + i
                samples = last_all[brick, :, i * PB:(i + 1) * PB]
                for entry in range(K_DEV):
                    target = jnp.where(
                        delay_ref[entry, block] == MAXOFF, dir_ref[entry, block], -1)
                    held.append(jnp.where(row == target, samples, 0.0))
            picked = jnp.concatenate(held, axis=1)
            last_lhs[:, brick * width:(brick + 1) * width] = jnp.concatenate(
                [picked, jnp.zeros_like(picked)], axis=0).astype(BF16)

    def all_weights():
        return wv[:ENTRIES].reshape(ENTRIES * PB, DB)

    def corr_copy(last, member):
        source, target = (last_out, last_in) if last else (corr_out, corr_in)
        return pltpu.make_async_remote_copy(
            src_ref=source, dst_ref=target.at[member],
            send_sem=last_ssem if last else corr_ssem,
            recv_sem=(last_rsem if last else corr_rsem).at[member],
            device_id=owner, device_id_type=MESH,
        )

    def corr_start(last):
        @pl.when(jnp.logical_not(is_owner))
        def _():
            corr_copy(last, group).start()

    far_pairs(0, 28, 14)
    leap(0)
    far_pairs(28, PAIRS - 28, 12)
    core_start()
    leap(1)
    sample(0)
    sample(1)
    for half in range(2):
        core_finish(half)
        ring_begin(half)
    leap(2)
    save_prev = pltpu.make_async_copy(
        field_b.at[pl.ds(1, CX), pl.ds(LOW, CY)], prev_ref, load_sem.at[5])
    save_prev.start()
    sample(2)
    samp_start(0)
    for half in range(2):
        ring_forward(half)
    leap(3)
    sample(3)
    samp_start(1)
    save_next = pltpu.make_async_copy(
        field_a.at[pl.ds(1, CX), pl.ds(LOW, CY)], next_ref, load_sem.at[6])
    save_next.start()
    for half in range(2):
        ring_end(half)
    samp_wait(0)
    for brick in range(NY_DEV):
        for i in range(SLOT // PB):
            spad[brick * (SLOT // PB) + i, 32:40, :] = samp_all[brick, :, i * PB:(i + 1) * PB]
    lax.fori_loop(0, BLOCKS // 4, entry_rows, 0)
    corr_out[...] = jnp.dot(lhs[...], all_weights(), preferred_element_type=F32)
    corr_start(0)
    samp_wait(1)
    last_rows()
    last_out[...] = jnp.dot(
        last_lhs[...], all_weights(), preferred_element_type=F32)[:8]
    corr_start(1)
    for half in range(2):
        direct_end(half)

    @pl.when(is_owner)
    def _():
        def arrivals(last):
            def one(member, carry):
                corr_copy(last, member).wait_recv()
                return carry
            lax.fori_loop(0, OWNERS - 1, one, 0)

        arrivals(0)
        total = corr_out[...]
        for member in range(OWNERS - 1):
            total = total + corr_in[member]
        for j in range(TARGETS):
            piece = total[(j // 2) * 8:(j // 2) * 8 + 8, :]
            if j % 2 == 0:
                piece = pltpu.roll(piece, 4, 0)
            columns = slice(j * DB, (j + 1) * DB)
            far_ref[8:16, columns] = far_ref[8:16, columns] + jnp.where(row >= 4, piece, 0.0)
        arrivals(1)
        total = last_out[...]
        for member in range(OWNERS - 1):
            total = total + last_in[member]
        for j in range(TARGETS):
            columns = slice(j * DB, (j + 1) * DB)
            far_ref[15:16, columns] = far_ref[15:16, columns] + total[j:j + 1, :]

    for step in range(STEPS):
        halo_wait_send(step, (0, 1, 2) if step == STEPS - 1 else (1, 2))
    for half in range(2):
        core_copy(half).wait_send()
        for kind in range(3):
            for way in range(2):
                ring_copy(half, kind, way).wait_send()
        for offset in (1, 2, 3):
            direct_copy(half, offset).wait_send()
    for last in range(2):
        for offset in range(1, NY_DEV):
            samp_copy(last, offset).wait_send()

    @pl.when(jnp.logical_not(is_owner))
    def _():
        corr_copy(0, group).wait_send()
        corr_copy(1, group).wait_send()

    save_prev.wait()
    save_next.wait()


def hall(dirs, delays, surf_index, now, old, code, history, weights):
    any_space = pl.BlockSpec(memory_space=pl.ANY)
    smem = pl.BlockSpec(memory_space=pltpu.SMEM)
    vmem = pl.BlockSpec(memory_space=pltpu.VMEM)
    dma = pltpu.SemaphoreType.DMA
    brick = jax.ShapeDtypeStruct((CX, CY, CZ), F32)
    return pl.pallas_call(
        hall_kernel,
        out_shape=(brick, brick, jax.ShapeDtypeStruct((ROWS, TARGETS * DB), F32)),
        in_specs=[smem, smem, vmem, vmem] + [any_space] * 5,
        out_specs=(any_space, any_space, vmem),
        scratch_shapes=[
            pltpu.VMEM((CX + 2, PADROWS, CZ), F32),
            pltpu.VMEM((CX + 2, PADROWS, CZ), F32),
            pltpu.VMEM((CX, CY, CZ), jnp.int32),
            pltpu.VMEM((3, CX, CY, CZ), F32),
            pltpu.VMEM((STEPS, 2, CX, CZ), F32),
            pltpu.VMEM((STEPS, CY, CZ), F32),
            pltpu.VMEM((STEPS, 2, CY, CZ), F32),
            pltpu.VMEM((STEPS, 2, CX, CZ), F32),
            pltpu.VMEM((STEPS, 2, CY, CZ), F32),
            pltpu.VMEM((SLOT, CX * CY), BF16),
            pltpu.VMEM((SLOT, CZ), F32),
            pltpu.VMEM((2, CX * CY, CZ), BF16),
            pltpu.VMEM((8, SLOT), F32),
            pltpu.VMEM((NY_DEV, 8, SLOT), F32),
            pltpu.VMEM((8, SLOT), F32),
            pltpu.VMEM((NY_DEV, 8, SLOT), F32),
            pltpu.VMEM((BLOCKS, 48, PB), F32),
            pltpu.VMEM((32, ENTRIES * PB), BF16),
            pltpu.VMEM((16, ENTRIES * PB), BF16),
            pltpu.VMEM((ENTRIES + 1, PB, DB), BF16),
            pltpu.VMEM((BLOCKS, TW + MAXOFF, PB), F32),
            pltpu.VMEM((PAIRS + 1, TW, DB), F32),
            pltpu.VMEM((8, PB), jnp.int32),
            pltpu.SMEM((8, PB), jnp.int32),
            pltpu.VMEM((HOLD, BLOCKS * PB), BF16),
            pltpu.VMEM((TARGETS, 4, 4, 2, ROWS, DB), F32),
            pltpu.VMEM((TARGETS, 4, 4, ROWS, DB), F32),
            pltpu.VMEM((2, 4, 4, 4, ROWS, DB), F32),
            pltpu.VMEM((2, 4, 4, ROWS, DB), F32),
            pltpu.VMEM((2, 3, 2, 2, 4, ROWS, DB), F32),
            pltpu.VMEM((2, 3, 4, ROWS, DB), F32),
            pltpu.VMEM((32, DB), F32),
            pltpu.VMEM((OWNERS, 32, DB), F32),
            pltpu.VMEM((8, DB), F32),
            pltpu.VMEM((OWNERS, 8, DB), F32),
            dma((8,)),
            dma((STEPS, 3, 2)), dma((STEPS, 3, 2)),
            dma((2, 3)), dma((2, 3)),
            dma((2,)), dma((2,)),
            dma((2, 3, 2)), dma((2, 3, 2)), dma((2, 3)), dma((2, 3)),
            dma, dma((OWNERS,)), dma, dma((OWNERS,)),
        ],
        compiler_params=pltpu.CompilerParams(
            collective_id=0, has_side_effects=True, vmem_limit_bytes=58 * 1024 * 1024),
    )(dirs, delays, dirs, surf_index, history, now, old, code, weights)


def save_kernel(*refs):
    sources, targets, held, sems = refs[:3], refs[3:6], refs[6:9], refs[9]
    arrivals = [pltpu.make_async_copy(sources[i], held[i], sems.at[0, i]) for i in range(3)]
    leaves = [pltpu.make_async_copy(held[i], targets[i], sems.at[1, i]) for i in range(3)]
    for copy in arrivals:
        copy.start()
    for arrival, leave in zip(arrivals, leaves):
        arrival.wait()
        leave.start()
    for copy in leaves:
        copy.wait()


def save(arrays):
    any_space = pl.BlockSpec(memory_space=pl.ANY)
    return pl.pallas_call(
        save_kernel,
        out_shape=tuple(jax.ShapeDtypeStruct(a.shape, a.dtype) for a in arrays),
        in_specs=[any_space] * 3,
        out_specs=(any_space,) * 3,
        scratch_shapes=[pltpu.VMEM(a.shape, a.dtype) for a in arrays]
        + [pltpu.SemaphoreType.DMA((2, 3))],
    )(*arrays)


def shards(pressure_now, pressure_old, cell_code, surf_index, history, dir_slot, delay, weights):
    flat_weights = weights.reshape(BLOCKS * K_DEV, PB, DB)
    return save(hall(
        dir_slot.T, delay.T, surf_index, pressure_now, pressure_old, cell_code, history,
        flat_weights))


def solution(mesh):
    return jax.shard_map(
        shards,
        mesh=mesh,
        in_specs=(
            P("gx", "gy", "gz"),
            P("gx", "gy", "gz"),
            P("gx", "gy", "gz"),
            P(("gx", "gz"), "gy"),
            P(None, ("gx", "gz")),
            P(("gx", "gz"), "gy"),
            P(("gx", "gz"), "gy"),
            P(("gx", "gz"), "gy", None, None),
        ),
        out_specs=(P("gx", "gy", "gz"), P("gx", "gy", "gz"), P(("gx", "gz"), "gy")),
        check_vma=False,
    )
```

```python
import functools

import jax
import jax.numpy as jnp
import numpy as np
from jax import lax
from jax.experimental import pallas as pl
from jax.experimental.pallas import tpu as pltpu
from jax.sharding import PartitionSpec as P

MESH = pl.DeviceIdType.MESH
F32 = jnp.float32
BF16 = jnp.bfloat16

STEPS = 4
CX, CY, CZ = 32, 32, 128
SLOT = 512
TW = 512
MAXOFF = 32
HOLD = 540
PB = 128
DB = 128
K_DEV = 6
BLOCKS = 16
ENTRIES = K_DEV * BLOCKS
PAIRS = ENTRIES // 2 + 4
TARGETS = 8
OWNERS = 32
ROWS = 16
NX_DEV, NY_DEV, NZ_DEV = 8, 4, 4
LOW, HIGH = 8, 40
PADROWS = 48


def coefficient_table():
    speeds = np.array([0.32, 0.26, 0.19, 0.11], np.float32).astype(np.float64)
    damping = np.array([0.0, 0.02, 0.08, 0.3], np.float32).astype(np.float64)
    here = (2.0 - 6.0 * speeds) / (1.0 + damping)
    before = -(1.0 - damping) / (1.0 + damping)
    around = speeds / (1.0 + damping)
    return [[float(np.float32(v)) for v in row] for row in (here, before, around)]


COEFFICIENTS = coefficient_table()


def hall_kernel(
    dir_ref, delay_ref, dirs_ref, surf_ref, hist_ref, now_ref, old_ref, code_ref, w_ref,
    next_ref, prev_ref, far_ref,
    field_a, field_b, codes, coef, ystage, zstage, xrecv, yrecv, zrecv,
    onehot, cellmask, rounded, samp_send, samp_all, last_send, last_all, spad, lhs, last_lhs, wv,
    signal, trail, table, order, hist, part, core_recv, sums, totals, ring1, ring2, corr_out, corr_in, last_out, last_in,
    load_sem, halo_send, halo_recv, samp_ssem, samp_rsem,
    core_ssem, core_rsem, ring_send, ring_recv, direct_send, direct_recv, corr_ssem, corr_rsem, last_ssem, last_rsem,
):
    fields = (field_a, field_b)
    gx, gy, gz = lax.axis_index("gx"), lax.axis_index("gy"), lax.axis_index("gz")
    y, z_hi = gx // 2, lax.rem(gx, 2)
    z_lo, core = gz // 2, lax.rem(gz, 2)
    z = z_hi * 2 + z_lo
    group = gx * 4 + gz
    is_owner = group == OWNERS - 1

    def place(yy, zz):
        return (yy * 2 + zz // 2, gy, lax.rem(zz, 2) * 2 + core)

    def ring_neighbour(axis, offset):
        if axis == "z":
            return place(y, lax.rem(z + offset, 4))
        return place(lax.rem(y + offset, 4), z)

    sibling = (gx, gy, z_lo * 2 + 1 - core)
    owner = (NX_DEV - 1, gy, NZ_DEV - 1)
    coords = (gx, gy, gz)
    extents = (NX_DEV, NY_DEV, NZ_DEV)

    def beside(axis, side):
        moved = list(coords)
        moved[axis] = coords[axis] + (1 if side else -1)
        return tuple(moved)

    def exists(axis, side):
        return coords[axis] < extents[axis] - 1 if side else coords[axis] > 0

    barrier = pltpu.get_barrier_semaphore()

    def greet(device):
        pl.semaphore_signal(barrier, inc=1, device_id=device, device_id_type=MESH)

    expected = jnp.int32(10)
    for axis in range(3):
        for side in range(2):
            @pl.when(exists(axis, side))
            def _():
                greet(beside(axis, side))
            expected = expected + exists(axis, side).astype(jnp.int32)
    greet(sibling)
    for axis in ("y", "z"):
        for offset in (1, 2, 3):
            greet(ring_neighbour(axis, offset))
    for offset in range(1, NY_DEV):
        greet((gx, lax.rem(gy + offset, NY_DEV), gz))

    @pl.when(is_owner)
    def _():
        def greet_one(member, carry):
            greet((member // 4, gy, lax.rem(member, 4)))
            return carry
        lax.fori_loop(0, OWNERS - 1, greet_one, 0)

    expected = expected + jnp.where(is_owner, 0, 1)

    loads = [
        pltpu.make_async_copy(now_ref, field_a.at[pl.ds(1, CX), pl.ds(LOW, CY)], load_sem.at[0]),
        pltpu.make_async_copy(hist_ref, hist, load_sem.at[3]),
        pltpu.make_async_copy(w_ref, wv.at[pl.ds(0, ENTRIES)], load_sem.at[4]),
        pltpu.make_async_copy(code_ref, codes, load_sem.at[2]),
        pltpu.make_async_copy(old_ref, field_b.at[pl.ds(1, CX), pl.ds(LOW, CY)], load_sem.at[1]),
    ]
    for load in loads:
        load.start()

    lane = lax.broadcasted_iota(jnp.int32, (CY, CZ), 1)
    zero_plane = jnp.zeros((CY, CZ), F32)

    def over_planes(body, init, unroll=8):
        def chunk(i, carry):
            return body([i * unroll + u for u in range(unroll)], carry)
        return lax.fori_loop(0, CX // unroll, chunk, init)

    def take_faces(step, xs, planes, held):
        for x, plane in zip(xs, planes):
            mine = jnp.logical_or(lane == 2 * x, lane == lax.rem(2 * x + CZ - 1, CZ))
            held = jnp.where(mine, pltpu.roll(plane, 2 * x, 1), held)
        for x, plane in zip(xs, planes):
            ystage[step, 0, pl.ds(x, 1), :] = plane[0:1, :]
            ystage[step, 1, pl.ds(x, 1), :] = plane[CY - 1:CY, :]
        return held

    def halo_copy(step, axis, side):
        current = step % 2
        if axis == 0:
            source = fields[current].at[CX if side else 1, pl.ds(LOW, CY)]
            target = xrecv.at[step, 1 - side]
        elif axis == 1:
            source, target = ystage.at[step, side], yrecv.at[step, 1 - side]
        else:
            source, target = zstage.at[step], zrecv.at[step, 1 - side]
        return pltpu.make_async_remote_copy(
            src_ref=source, dst_ref=target,
            send_sem=halo_send.at[step, axis, side],
            recv_sem=halo_recv.at[step, axis, 1 - side],
            device_id=beside(axis, side), device_id_type=MESH,
        )

    def halo_start(step):
        for axis in range(3):
            for side in range(2):
                @pl.when(exists(axis, side))
                def _():
                    halo_copy(step, axis, side).start()

    def halo_wait_send(step, axes=(0, 1, 2)):
        for axis in axes:
            for side in range(2):
                @pl.when(exists(axis, side))
                def _():
                    halo_copy(step, axis, side).wait_send()

    def halo_wait_recv(step, axes):
        for axis in axes:
            buffer = (xrecv, yrecv, zrecv)[axis]
            for side in range(2):
                @pl.when(exists(axis, side))
                def _():
                    halo_copy(step, axis, 1 - side).wait_recv()
                @pl.when(jnp.logical_not(exists(axis, side)))
                def _():
                    buffer[step, side] = zero_plane

    loads[0].wait()

    def first_faces(xs, carry):
        return take_faces(0, xs, [field_a[x + 1, LOW:HIGH, :] for x in xs], carry)

    zstage[0] = over_planes(first_faces, zero_plane)

    pl.semaphore_wait(barrier, expected)
    halo_start(0)

    dirs = dirs_ref[...]
    targets = jnp.concatenate(
        [dirs[k:k + 1, :] for k in range(K_DEV)]
        + [jnp.full((1, PB - ENTRIES), -1, jnp.int32)], axis=1)
    targets = jnp.where(targets >= 0, targets, TARGETS).astype(F32)
    by_lane = jnp.broadcast_to(targets, (PB, PB))
    by_row = by_lane.T
    lanes = lax.broadcasted_iota(jnp.int32, (PB, PB), 1).astype(F32)
    rows = lax.broadcasted_iota(jnp.int32, (PB, PB), 0).astype(F32)

    def count(mask, axis):
        return jnp.sum(jnp.where(mask, 1.0, 0.0), axis=axis, keepdims=True)

    def even(amount):
        return 2.0 * jnp.floor(0.5 * (amount + 1.0))

    member = by_row == lanes
    along_lanes = count(member, 0)
    along_rows = count(by_lane == rows, 1)
    first_lanes = jnp.sum(jnp.where(rows < lanes, even(along_rows), 0.0), axis=0, keepdims=True)
    first_rows = jnp.sum(jnp.where(lanes < rows, even(along_lanes), 0.0), axis=1, keepdims=True)
    before = count(jnp.logical_and(by_lane == by_row, lanes < rows), 1)
    slot = before + jnp.sum(jnp.where(member, first_lanes, 0.0), axis=1, keepdims=True)
    taken = jnp.logical_and(slot == lanes, by_row < TARGETS)
    sequence = ENTRIES + jnp.sum(jnp.where(taken, rows - ENTRIES, 0.0), axis=0, keepdims=True)
    ends = jnp.where(along_lanes > 0, 0.5 * (first_lanes + even(along_lanes)), 0.0)
    opens = count(
        jnp.logical_and(jnp.logical_and(0.5 * first_rows == lanes, along_rows > 0), rows < TARGETS), 0)
    table[0:1, :] = sequence.astype(jnp.int32)
    table[1:2, :] = ends.astype(jnp.int32)
    table[2:3, :] = opens.astype(jnp.int32)
    table[3:8, :] = jnp.zeros((5, PB), jnp.int32)
    order_load = pltpu.make_async_copy(table, order, load_sem.at[7])
    order_load.start()

    def core_copy(half):
        return pltpu.make_async_remote_copy(
            src_ref=part.at[pl.ds(half * 4, 4), :, :, 1 - core],
            dst_ref=core_recv.at[pl.ds(half * 4, 4)],
            send_sem=core_ssem.at[half], recv_sem=core_rsem.at[half],
            device_id=sibling, device_id_type=MESH,
        )

    loads[1].wait()

    def widen(block, carry):
        signal[block, HOLD:, :] = jnp.zeros((TW + MAXOFF - HOLD, PB), F32)
        return carry

    lax.fori_loop(0, BLOCKS, widen, 0)
    for block in range(BLOCKS):
        signal[block, :HOLD, :] = hist[:, block * PB:(block + 1) * PB].astype(F32)
    trail[0] = jnp.zeros((TW, DB), F32)
    order_load.wait()
    loads[2].wait()

    wv[ENTRIES] = jnp.zeros((PB, DB), BF16)

    def far_pair(p):
        windows, blocks = [], []
        for u in range(2):
            entry = jnp.clip(order[0, 2 * p + u], 0, ENTRIES)
            k = jnp.minimum(lax.shift_right_logical(entry, 4), K_DEV - 1)
            block = jnp.bitwise_and(entry, BLOCKS - 1)
            windows.append(signal[block, pl.ds(delay_ref[k, block], TW), :].astype(BF16))
            blocks.append(wv[jnp.where(entry < ENTRIES, block * K_DEV + k, ENTRIES)])
        term = jnp.dot(
            jnp.concatenate(windows, axis=1), jnp.concatenate(blocks, axis=0),
            preferred_element_type=F32)
        trail[p + 1] = term + trail[jnp.where(order[2, p] > 0, 0, p)]

    def far_pairs(first, amount, unroll):
        def chunk(i, carry):
            for u in range(unroll):
                far_pair(first + i * unroll + u)
            return carry
        lax.fori_loop(0, amount // unroll, chunk, 0)

    def far_collect():
        for j in range(TARGETS):
            end = jnp.clip(order[1, j], 0, PAIRS)
            for quarter in range(4):
                found = trail[end, quarter * 128:(quarter + 1) * 128, :]
                part[j, quarter] = found.reshape(4, 2, ROWS, DB)

    def core_start():
        far_collect()
        for half in range(2):
            core_copy(half).start()

    loads[3].wait()

    def plane_coefficients(xs, carry):
        for x in xs:
            code = codes[x]
            for index, values in enumerate(COEFFICIENTS):
                coef[index, x] = jnp.where(
                    code == 0, values[0],
                    jnp.where(code == 1, values[1], jnp.where(code == 2, values[2], values[3])),
                ).astype(F32)
        return carry

    over_planes(plane_coefficients, 0)
    loads[4].wait()

    def leap(step):
        here_ref, other_ref = fields[step % 2], fields[1 - step % 2]
        last = step == STEPS - 1
        halo_wait_recv(step, (1, 2))

        def y_rows(xs, carry):
            rows = [(yrecv[step, 0, pl.ds(x, 1), :], yrecv[step, 1, pl.ds(x, 1), :]) for x in xs]
            for x, (low, high) in zip(xs, rows):
                here_ref[x + 1, LOW - 1:LOW, :] = low
                here_ref[x + 1, HIGH:HIGH + 1, :] = high
            return carry

        over_planes(y_rows, 0, 16)
        z_halo = jnp.where(
            jnp.bitwise_and(lane, 1) == 0,
            pltpu.roll(zrecv[step, 0], 1, 1), pltpu.roll(zrecv[step, 1], CZ - 1, 1))
        ends = jnp.logical_or(lane == 0, lane == CZ - 1)

        def plane_step(xs, carry):
            planes = []
            for x in xs:
                here = here_ref[x + 1, LOW:HIGH, :]
                around = here_ref[x, LOW:HIGH, :] + here_ref[x + 2, LOW:HIGH, :]
                around = around + (
                    here_ref[x + 1, LOW - 1:HIGH - 1, :] + here_ref[x + 1, LOW + 1:HIGH + 1, :])
                beside_z = (jnp.where(lane == 0, 0.0, pltpu.roll(here, 1, 1))
                            + jnp.where(lane == CZ - 1, 0.0, pltpu.roll(here, CZ - 1, 1)))
                outside = pltpu.roll(z_halo, lax.rem(2 * (CZ - x), CZ), 1)
                around = around + (beside_z + jnp.where(ends, outside, 0.0))
                before = other_ref[x + 1, LOW:HIGH, :]
                planes.append(coef[0, x] * here + coef[1, x] * before + coef[2, x] * around)
            for x, new in zip(xs, planes):
                other_ref[x + 1, LOW:HIGH, :] = new
                rounded[step % 2, pl.ds(x * CY if isinstance(x, int) else pl.multiple_of(x * CY, CY), CY), :] = new.astype(BF16)
            if last:
                return carry
            return take_faces(step + 1, xs, planes, carry)

        def inner(i, carry):
            return plane_step([1 + i * 10 + u for u in range(10)], carry)

        carry = lax.fori_loop(
            0, (CX - 2) // 10, inner, 0 if last else zero_plane)
        halo_wait_recv(step, (0,))
        if step > 0:
            halo_wait_send(step - 1, (0,))
        here_ref[0, LOW:HIGH, :] = xrecv[step, 0]
        here_ref[CX + 1, LOW:HIGH, :] = xrecv[step, 1]
        carry = plane_step([0, CX - 1], carry)
        if not last:
            zstage[step + 1] = carry
            halo_start(step + 1)

    def sample(step):
        picked = jnp.dot(onehot[...], rounded[step % 2], preferred_element_type=F32)
        values = lax.dot_general(
            jnp.ones((8, CZ), BF16), (picked * cellmask[...]).astype(BF16),
            (((1,), (1,)), ((), ())), preferred_element_type=F32)
        if step < STEPS - 1:
            samp_send[4 + step:5 + step, :] = values[0:1, :]
        else:
            last_send[...] = values

    axes = (("z", "y"), ("y", "z"))

    def index_on(axis):
        return z if axis == "z" else y

    def ring_copy(half, kind, way):
        axis = axes[half][0]
        place_now = index_on(axis)
        step_to = 1 if way == 0 else 3
        chunk = lax.rem(place_now + (2 if kind == 0 else step_to), 4)
        part_now = pl.ds(0 if (kind == 1) == (way == 1) else 2, 2)
        return pltpu.make_async_remote_copy(
            src_ref=sums.at[half, chunk, part_now], dst_ref=ring1.at[half, kind, way],
            send_sem=ring_send.at[half, kind, way],
            recv_sem=ring_recv.at[half, kind, way],
            device_id=ring_neighbour(axis, step_to), device_id_type=MESH,
        )

    def direct_copy(half, offset):
        axis = axes[half][1]
        return pltpu.make_async_remote_copy(
            src_ref=totals.at[half, lax.rem(index_on(axis) + offset, 4)],
            dst_ref=ring2.at[half, offset - 1],
            send_sem=direct_send.at[half, offset - 1],
            recv_sem=direct_recv.at[half, offset - 1],
            device_id=ring_neighbour(axis, offset), device_id_type=MESH,
        )

    def core_finish(half):
        core_copy(half).wait_recv()

        for yy in range(4):
            for zz in range(4):
                total = (part[half * 4:half * 4 + 4, yy, zz, core]
                         + core_recv[half * 4:half * 4 + 4, yy, zz])
                if half == 0:
                    sums[0, zz, yy] = total
                else:
                    sums[1, yy, zz] = total

    def ring_begin(half):
        for kind in (0, 1):
            for way in (0, 1):
                ring_copy(half, kind, way).start()

    def ring_forward(half):
        place_now = index_on(axes[half][0])
        for way in (0, 1):
            ring_copy(half, 0, way).wait_recv()
            chunk = lax.rem(place_now + (1 if way == 0 else 3), 4)
            first = 0 if way == 0 else 2
            sums[half, chunk, first:first + 2] = (
                sums[half, chunk, first:first + 2] + ring1[half, 0, way])
            ring_copy(half, 2, way).start()

    def ring_end(half):
        place_now = index_on(axes[half][0])
        for kind in (1, 2):
            for way in (0, 1):
                ring_copy(half, kind, way).wait_recv()
        totals[half, 0:2] = sums[half, place_now, 0:2] + (ring1[half, 2, 0] + ring1[half, 1, 1])
        totals[half, 2:4] = sums[half, place_now, 2:4] + (ring1[half, 1, 0] + ring1[half, 2, 1])
        for offset in (2, 1, 3):
            direct_copy(half, offset).start()

    def direct_end(half):
        for offset in (1, 2, 3):
            direct_copy(half, offset).wait_recv()
        result = totals[half, index_on(axes[half][1])]
        result = result + (ring2[half, 0] + (ring2[half, 1] + ring2[half, 2]))
        for j in range(4):
            columns = slice((half * 4 + j) * DB, (half * 4 + j + 1) * DB)
            far_ref[:, columns] = result[j]

    def samp_copy(last, offset, arriving=False):
        source, target = (last_send, last_all) if last else (samp_send, samp_all)
        slot = lax.rem(gy + NY_DEV - offset, NY_DEV) if arriving else gy
        return pltpu.make_async_remote_copy(
            src_ref=source, dst_ref=target.at[slot],
            send_sem=samp_ssem.at[last, offset - 1], recv_sem=samp_rsem.at[last, offset - 1],
            device_id=(gx, lax.rem(gy + offset, NY_DEV), gz), device_id_type=MESH,
        )

    def samp_start(last):
        for offset in range(1, NY_DEV):
            samp_copy(last, offset).start()
        if last:
            last_all[gy] = last_send[...]
        else:
            samp_all[gy] = samp_send[...]

    def samp_wait(last):
        for offset in range(1, NY_DEV):
            samp_copy(last, offset, True).wait_recv()

    row = lax.broadcasted_iota(jnp.int32, (8, PB), 0)
    width = 4 * K_DEV * PB

    def entry_rows(i, carry):
        held = []
        for block in [i * 4 + u for u in range(4)]:
            for entry in range(K_DEV):
                offset = delay_ref[entry, block]
                target = dir_ref[entry, block]
                early = spad[block, pl.ds(offset + 4, 8), :]
                late = spad[block, pl.ds(offset, 8), :]
                pair = jnp.where(row < 4, early, late)
                pieces = []
                for k in range(TARGETS // 2):
                    wanted = jnp.where(row < 4, 2 * k, 2 * k + 1)
                    pieces.append(jnp.where(wanted == target, pair, 0.0))
                held.append(jnp.concatenate(pieces, axis=0).astype(BF16))
        lhs[:, pl.ds(pl.multiple_of(i * width, width), width)] = jnp.concatenate(held, axis=1)
        return carry

    def last_rows():
        for brick in range(NY_DEV):
            held = []
            for i in range(SLOT // PB):
                block = brick * (SLOT // PB) + i
                samples = last_all[brick, :, i * PB:(i + 1) * PB]
                for entry in range(K_DEV):
                    target = jnp.where(
                        delay_ref[entry, block] == MAXOFF, dir_ref[entry, block], -1)
                    held.append(jnp.where(row == target, samples, 0.0))
            picked = jnp.concatenate(held, axis=1)
            last_lhs[:, brick * width:(brick + 1) * width] = jnp.concatenate(
                [picked, jnp.zeros_like(picked)], axis=0).astype(BF16)

    def all_weights():
        return wv[:ENTRIES].reshape(ENTRIES * PB, DB)

    def corr_copy(last, member):
        source, target = (last_out, last_in) if last else (corr_out, corr_in)
        return pltpu.make_async_remote_copy(
            src_ref=source, dst_ref=target.at[member],
            send_sem=last_ssem if last else corr_ssem,
            recv_sem=(last_rsem if last else corr_rsem).at[member],
            device_id=owner, device_id_type=MESH,
        )

    def corr_start(last):
        @pl.when(jnp.logical_not(is_owner))
        def _():
            corr_copy(last, group).start()

    far_pairs(0, 36, 12)
    leap(0)
    far_pairs(36, PAIRS - 36, 16)
    core_start()
    leap(1)

    slot_lane = lax.broadcasted_iota(jnp.int32, (PB, PB), 1)
    for i in range(SLOT // PB):
        slots = slice(i * PB, (i + 1) * PB)
        cell = jnp.broadcast_to(surf_ref[:, slots].astype(F32), (PB, PB)).T.astype(jnp.int32)
        cell_row = lax.shift_right_arithmetic(cell, 7)
        cellmask[slots, :] = jnp.where(
            slot_lane == jnp.bitwise_and(cell, CZ - 1), 1.0, 0.0)
        for q in range(CX * CY // PB):
            onehot[slots, q * PB:(q + 1) * PB] = jnp.where(
                slot_lane + q * PB == cell_row, 1.0, 0.0).astype(BF16)
    samp_send[...] = jnp.zeros_like(samp_send)
    spad[...] = jnp.zeros_like(spad)
    for half in range(2):
        core_finish(half)
        ring_begin(half)
    sample(0)
    sample(1)
    leap(2)
    save_prev = pltpu.make_async_copy(
        field_b.at[pl.ds(1, CX), pl.ds(LOW, CY)], prev_ref, load_sem.at[5])
    save_prev.start()
    sample(2)
    samp_start(0)
    for half in range(2):
        ring_forward(half)
    leap(3)
    sample(3)
    samp_start(1)
    save_next = pltpu.make_async_copy(
        field_a.at[pl.ds(1, CX), pl.ds(LOW, CY)], next_ref, load_sem.at[6])
    save_next.start()
    samp_wait(0)
    for brick in range(NY_DEV):
        for i in range(SLOT // PB):
            spad[brick * (SLOT // PB) + i, 32:40, :] = samp_all[brick, :, i * PB:(i + 1) * PB]
    lax.fori_loop(0, BLOCKS // 4, entry_rows, 0)
    corr_out[...] = jnp.dot(lhs[...], all_weights(), preferred_element_type=F32)
    corr_start(0)
    for half in range(2):
        ring_end(half)
    samp_wait(1)
    last_rows()
    last_out[...] = jnp.dot(
        last_lhs[...], all_weights(), preferred_element_type=F32)[:8]
    corr_start(1)
    for half in range(2):
        direct_end(half)

    @pl.when(is_owner)
    def _():
        def arrivals(last):
            def one(member, carry):
                corr_copy(last, member).wait_recv()
                return carry
            lax.fori_loop(0, OWNERS - 1, one, 0)

        arrivals(0)
        total = corr_out[...]
        for member in range(OWNERS - 1):
            total = total + corr_in[member]
        for j in range(TARGETS):
            piece = total[(j // 2) * 8:(j // 2) * 8 + 8, :]
            if j % 2 == 0:
                piece = pltpu.roll(piece, 4, 0)
            columns = slice(j * DB, (j + 1) * DB)
            far_ref[8:16, columns] = far_ref[8:16, columns] + jnp.where(row >= 4, piece, 0.0)
        arrivals(1)
        total = last_out[...]
        for member in range(OWNERS - 1):
            total = total + last_in[member]
        for j in range(TARGETS):
            columns = slice(j * DB, (j + 1) * DB)
            far_ref[15:16, columns] = far_ref[15:16, columns] + total[j:j + 1, :]

    for step in range(STEPS):
        halo_wait_send(step, (0, 1, 2) if step == STEPS - 1 else (1, 2))
    for half in range(2):
        core_copy(half).wait_send()
        for kind in range(3):
            for way in range(2):
                ring_copy(half, kind, way).wait_send()
        for offset in (1, 2, 3):
            direct_copy(half, offset).wait_send()
    for last in range(2):
        for offset in range(1, NY_DEV):
            samp_copy(last, offset).wait_send()

    @pl.when(jnp.logical_not(is_owner))
    def _():
        corr_copy(0, group).wait_send()
        corr_copy(1, group).wait_send()

    save_prev.wait()
    save_next.wait()


def hall(dirs, delays, surf_index, now, old, code, history, weights):
    any_space = pl.BlockSpec(memory_space=pl.ANY)
    smem = pl.BlockSpec(memory_space=pltpu.SMEM)
    vmem = pl.BlockSpec(memory_space=pltpu.VMEM)
    dma = pltpu.SemaphoreType.DMA
    brick = jax.ShapeDtypeStruct((CX, CY, CZ), F32)
    return pl.pallas_call(
        hall_kernel,
        out_shape=(brick, brick, jax.ShapeDtypeStruct((ROWS, TARGETS * DB), F32)),
        in_specs=[smem, smem, vmem, vmem] + [any_space] * 5,
        out_specs=(any_space, any_space, vmem),
        scratch_shapes=[
            pltpu.VMEM((CX + 2, PADROWS, CZ), F32),
            pltpu.VMEM((CX + 2, PADROWS, CZ), F32),
            pltpu.VMEM((CX, CY, CZ), jnp.int32),
            pltpu.VMEM((3, CX, CY, CZ), F32),
            pltpu.VMEM((STEPS, 2, CX, CZ), F32),
            pltpu.VMEM((STEPS, CY, CZ), F32),
            pltpu.VMEM((STEPS, 2, CY, CZ), F32),
            pltpu.VMEM((STEPS, 2, CX, CZ), F32),
            pltpu.VMEM((STEPS, 2, CY, CZ), F32),
            pltpu.VMEM((SLOT, CX * CY), BF16),
            pltpu.VMEM((SLOT, CZ), F32),
            pltpu.VMEM((2, CX * CY, CZ), BF16),
            pltpu.VMEM((8, SLOT), F32),
            pltpu.VMEM((NY_DEV, 8, SLOT), F32),
            pltpu.VMEM((8, SLOT), F32),
            pltpu.VMEM((NY_DEV, 8, SLOT), F32),
            pltpu.VMEM((BLOCKS, 48, PB), F32),
            pltpu.VMEM((32, ENTRIES * PB), BF16),
            pltpu.VMEM((16, ENTRIES * PB), BF16),
            pltpu.VMEM((ENTRIES + 1, PB, DB), BF16),
            pltpu.VMEM((BLOCKS, TW + MAXOFF, PB), F32),
            pltpu.VMEM((PAIRS + 1, TW, DB), F32),
            pltpu.VMEM((8, PB), jnp.int32),
            pltpu.SMEM((8, PB), jnp.int32),
            pltpu.VMEM((HOLD, BLOCKS * PB), BF16),
            pltpu.VMEM((TARGETS, 4, 4, 2, ROWS, DB), F32),
            pltpu.VMEM((TARGETS, 4, 4, ROWS, DB), F32),
            pltpu.VMEM((2, 4, 4, 4, ROWS, DB), F32),
            pltpu.VMEM((2, 4, 4, ROWS, DB), F32),
            pltpu.VMEM((2, 3, 2, 2, 4, ROWS, DB), F32),
            pltpu.VMEM((2, 3, 4, ROWS, DB), F32),
            pltpu.VMEM((32, DB), F32),
            pltpu.VMEM((OWNERS, 32, DB), F32),
            pltpu.VMEM((8, DB), F32),
            pltpu.VMEM((OWNERS, 8, DB), F32),
            dma((8,)),
            dma((STEPS, 3, 2)), dma((STEPS, 3, 2)),
            dma((2, 3)), dma((2, 3)),
            dma((2,)), dma((2,)),
            dma((2, 3, 2)), dma((2, 3, 2)), dma((2, 3)), dma((2, 3)),
            dma, dma((OWNERS,)), dma, dma((OWNERS,)),
        ],
        compiler_params=pltpu.CompilerParams(
            collective_id=0, has_side_effects=True, vmem_limit_bytes=58 * 1024 * 1024),
    )(dirs, delays, dirs, surf_index, history, now, old, code, weights)


def save_kernel(*refs):
    sources, targets, held, sems = refs[:3], refs[3:6], refs[6:9], refs[9]
    arrivals = [pltpu.make_async_copy(sources[i], held[i], sems.at[0, i]) for i in range(3)]
    leaves = [pltpu.make_async_copy(held[i], targets[i], sems.at[1, i]) for i in range(3)]
    for copy in arrivals:
        copy.start()
    for arrival, leave in zip(arrivals, leaves):
        arrival.wait()
        leave.start()
    for copy in leaves:
        copy.wait()


def save(arrays):
    any_space = pl.BlockSpec(memory_space=pl.ANY)
    return pl.pallas_call(
        save_kernel,
        out_shape=tuple(jax.ShapeDtypeStruct(a.shape, a.dtype) for a in arrays),
        in_specs=[any_space] * 3,
        out_specs=(any_space,) * 3,
        scratch_shapes=[pltpu.VMEM(a.shape, a.dtype) for a in arrays]
        + [pltpu.SemaphoreType.DMA((2, 3))],
    )(*arrays)


def shards(pressure_now, pressure_old, cell_code, surf_index, history, dir_slot, delay, weights):
    flat_weights = weights.reshape(BLOCKS * K_DEV, PB, DB)
    return save(hall(
        dir_slot.T, delay.T, surf_index, pressure_now, pressure_old, cell_code, history,
        flat_weights))


def solution(mesh):
    return jax.shard_map(
        shards,
        mesh=mesh,
        in_specs=(
            P("gx", "gy", "gz"),
            P("gx", "gy", "gz"),
            P("gx", "gy", "gz"),
            P(("gx", "gz"), "gy"),
            P(None, ("gx", "gz")),
            P(("gx", "gz"), "gy"),
            P(("gx", "gz"), "gy"),
            P(("gx", "gz"), "gy", None, None),
        ),
        out_specs=(P("gx", "gy", "gz"), P("gx", "gy", "gz"), P(("gx", "gz"), "gy")),
        check_vma=False,
    )
```

```python
import functools

import jax
import jax.numpy as jnp
import numpy as np
from jax import lax
from jax.experimental import pallas as pl
from jax.experimental.pallas import tpu as pltpu
from jax.sharding import PartitionSpec as P

MESH = pl.DeviceIdType.MESH
F32 = jnp.float32
BF16 = jnp.bfloat16

STEPS = 4
CX, CY, CZ = 32, 32, 128
SLOT = 512
TW = 512
MAXOFF = 32
HOLD = 540
PB = 128
DB = 128
K_DEV = 6
BLOCKS = 16
ENTRIES = K_DEV * BLOCKS
PAIRS = ENTRIES // 2 + 4
TARGETS = 8
OWNERS = 32
ROWS = 16
NX_DEV, NY_DEV, NZ_DEV = 8, 4, 4
LOW, HIGH = 8, 40
PADROWS = 48


def coefficient_table():
    speeds = np.array([0.32, 0.26, 0.19, 0.11], np.float32).astype(np.float64)
    damping = np.array([0.0, 0.02, 0.08, 0.3], np.float32).astype(np.float64)
    here = (2.0 - 6.0 * speeds) / (1.0 + damping)
    before = -(1.0 - damping) / (1.0 + damping)
    around = speeds / (1.0 + damping)
    return [[float(np.float32(v)) for v in row] for row in (here, before, around)]


COEFFICIENTS = coefficient_table()


def hall_kernel(
    dir_ref, delay_ref, dirs_ref, surf_ref, hist_ref, now_ref, old_ref, code_ref, w_ref,
    next_ref, prev_ref, far_ref,
    field_a, field_b, codes, coef, ystage, zstage, xrecv, yrecv, zrecv,
    onehot, cellmask, rounded, samp_send, samp_all, last_send, last_all, spad, lhs, last_lhs, wv,
    signal, trail, table, order, hist, part, core_recv, sums, totals, ring1, ring2, corr_out, corr_in, last_out, last_in,
    load_sem, halo_send, halo_recv, samp_ssem, samp_rsem,
    core_ssem, core_rsem, ring_send, ring_recv, direct_send, direct_recv, corr_ssem, corr_rsem, last_ssem, last_rsem,
):
    fields = (field_a, field_b)
    gx, gy, gz = lax.axis_index("gx"), lax.axis_index("gy"), lax.axis_index("gz")
    y, z_hi = gx // 2, lax.rem(gx, 2)
    z_lo, core = gz // 2, lax.rem(gz, 2)
    z = z_hi * 2 + z_lo
    group = gx * 4 + gz
    is_owner = group == OWNERS - 1

    def place(yy, zz):
        return (yy * 2 + zz // 2, gy, lax.rem(zz, 2) * 2 + core)

    def ring_neighbour(axis, offset):
        if axis == "z":
            return place(y, lax.rem(z + offset, 4))
        return place(lax.rem(y + offset, 4), z)

    sibling = (gx, gy, z_lo * 2 + 1 - core)
    owner = (NX_DEV - 1, gy, NZ_DEV - 1)
    coords = (gx, gy, gz)
    extents = (NX_DEV, NY_DEV, NZ_DEV)

    def beside(axis, side):
        moved = list(coords)
        moved[axis] = coords[axis] + (1 if side else -1)
        return tuple(moved)

    def exists(axis, side):
        return coords[axis] < extents[axis] - 1 if side else coords[axis] > 0

    barrier = pltpu.get_barrier_semaphore()

    def greet(device):
        pl.semaphore_signal(barrier, inc=1, device_id=device, device_id_type=MESH)

    expected = jnp.int32(10)
    for axis in range(3):
        for side in range(2):
            @pl.when(exists(axis, side))
            def _():
                greet(beside(axis, side))
            expected = expected + exists(axis, side).astype(jnp.int32)
    greet(sibling)
    for axis in ("y", "z"):
        for offset in (1, 2, 3):
            greet(ring_neighbour(axis, offset))
    for offset in range(1, NY_DEV):
        greet((gx, lax.rem(gy + offset, NY_DEV), gz))

    @pl.when(is_owner)
    def _():
        def greet_one(member, carry):
            greet((member // 4, gy, lax.rem(member, 4)))
            return carry
        lax.fori_loop(0, OWNERS - 1, greet_one, 0)

    expected = expected + jnp.where(is_owner, 0, 1)

    loads = [
        pltpu.make_async_copy(now_ref, field_a.at[pl.ds(1, CX), pl.ds(LOW, CY)], load_sem.at[0]),
        pltpu.make_async_copy(hist_ref, hist, load_sem.at[3]),
        pltpu.make_async_copy(w_ref, wv.at[pl.ds(0, ENTRIES)], load_sem.at[4]),
        pltpu.make_async_copy(code_ref, codes, load_sem.at[2]),
        pltpu.make_async_copy(old_ref, field_b.at[pl.ds(1, CX), pl.ds(LOW, CY)], load_sem.at[1]),
    ]
    for load in loads:
        load.start()

    lane = lax.broadcasted_iota(jnp.int32, (CY, CZ), 1)
    zero_plane = jnp.zeros((CY, CZ), F32)

    def over_planes(body, init, unroll=8):
        def chunk(i, carry):
            return body([i * unroll + u for u in range(unroll)], carry)
        return lax.fori_loop(0, CX // unroll, chunk, init)

    def take_faces(step, xs, planes, held):
        for x, plane in zip(xs, planes):
            mine = jnp.logical_or(lane == 2 * x, lane == lax.rem(2 * x + CZ - 1, CZ))
            held = jnp.where(mine, pltpu.roll(plane, 2 * x, 1), held)
        for x, plane in zip(xs, planes):
            ystage[step, 0, pl.ds(x, 1), :] = plane[0:1, :]
            ystage[step, 1, pl.ds(x, 1), :] = plane[CY - 1:CY, :]
        return held

    def halo_copy(step, axis, side):
        current = step % 2
        if axis == 0:
            source = fields[current].at[CX if side else 1, pl.ds(LOW, CY)]
            target = xrecv.at[step, 1 - side]
        elif axis == 1:
            source, target = ystage.at[step, side], yrecv.at[step, 1 - side]
        else:
            source, target = zstage.at[step], zrecv.at[step, 1 - side]
        return pltpu.make_async_remote_copy(
            src_ref=source, dst_ref=target,
            send_sem=halo_send.at[step, axis, side],
            recv_sem=halo_recv.at[step, axis, 1 - side],
            device_id=beside(axis, side), device_id_type=MESH,
        )

    def halo_start(step):
        for axis in range(3):
            for side in range(2):
                @pl.when(exists(axis, side))
                def _():
                    halo_copy(step, axis, side).start()

    def halo_wait_send(step, axes=(0, 1, 2)):
        for axis in axes:
            for side in range(2):
                @pl.when(exists(axis, side))
                def _():
                    halo_copy(step, axis, side).wait_send()

    def halo_wait_recv(step, axes):
        for axis in axes:
            buffer = (xrecv, yrecv, zrecv)[axis]
            for side in range(2):
                @pl.when(exists(axis, side))
                def _():
                    halo_copy(step, axis, 1 - side).wait_recv()
                @pl.when(jnp.logical_not(exists(axis, side)))
                def _():
                    buffer[step, side] = zero_plane

    dirs = dirs_ref[...]
    targets = jnp.concatenate(
        [dirs[k:k + 1, :] for k in range(K_DEV)]
        + [jnp.full((1, PB - ENTRIES), -1, jnp.int32)], axis=1)
    targets = jnp.where(targets >= 0, targets, TARGETS).astype(F32)
    by_lane = jnp.broadcast_to(targets, (PB, PB))
    by_row = by_lane.T
    lanes = lax.broadcasted_iota(jnp.int32, (PB, PB), 1).astype(F32)
    rows = lax.broadcasted_iota(jnp.int32, (PB, PB), 0).astype(F32)

    def count(mask, axis):
        return jnp.sum(jnp.where(mask, 1.0, 0.0), axis=axis, keepdims=True)

    def even(amount):
        return 2.0 * jnp.floor(0.5 * (amount + 1.0))

    member = by_row == lanes
    along_lanes = count(member, 0)
    along_rows = count(by_lane == rows, 1)
    first_lanes = jnp.sum(jnp.where(rows < lanes, even(along_rows), 0.0), axis=0, keepdims=True)
    first_rows = jnp.sum(jnp.where(lanes < rows, even(along_lanes), 0.0), axis=1, keepdims=True)
    before = count(jnp.logical_and(by_lane == by_row, lanes < rows), 1)
    slot = before + jnp.sum(jnp.where(member, first_lanes, 0.0), axis=1, keepdims=True)
    taken = jnp.logical_and(slot == lanes, by_row < TARGETS)
    sequence = ENTRIES + jnp.sum(jnp.where(taken, rows - ENTRIES, 0.0), axis=0, keepdims=True)
    ends = jnp.where(along_lanes > 0, 0.5 * (first_lanes + even(along_lanes)), 0.0)
    opens = count(
        jnp.logical_and(jnp.logical_and(0.5 * first_rows == lanes, along_rows > 0), rows < TARGETS), 0)
    table[0:1, :] = sequence.astype(jnp.int32)
    table[1:2, :] = ends.astype(jnp.int32)
    table[2:3, :] = opens.astype(jnp.int32)
    table[3:8, :] = jnp.zeros((5, PB), jnp.int32)
    order_load = pltpu.make_async_copy(table, order, load_sem.at[7])
    order_load.start()

    def core_copy(half):
        return pltpu.make_async_remote_copy(
            src_ref=part.at[pl.ds(half * 4, 4), :, :, 1 - core],
            dst_ref=core_recv.at[pl.ds(half * 4, 4)],
            send_sem=core_ssem.at[half], recv_sem=core_rsem.at[half],
            device_id=sibling, device_id_type=MESH,
        )

    samp_send[...] = jnp.zeros_like(samp_send)
    spad[...] = jnp.zeros_like(spad)
    trail[0] = jnp.zeros((TW, DB), F32)
    wv[ENTRIES] = jnp.zeros((PB, DB), BF16)
    for block in range(BLOCKS):
        signal[block, HOLD:, :] = jnp.zeros((TW + MAXOFF - HOLD, PB), F32)

    loads[0].wait()

    def first_faces(xs, carry):
        return take_faces(0, xs, [field_a[x + 1, LOW:HIGH, :] for x in xs], carry)

    zstage[0] = over_planes(first_faces, zero_plane)

    pl.semaphore_wait(barrier, expected)
    halo_start(0)

    loads[1].wait()

    for block in range(BLOCKS):
        signal[block, :HOLD, :] = hist[:, block * PB:(block + 1) * PB].astype(F32)
    order_load.wait()
    loads[2].wait()


    def far_pair(p):
        windows, blocks = [], []
        for u in range(2):
            entry = jnp.clip(order[0, 2 * p + u], 0, ENTRIES)
            k = jnp.minimum(lax.shift_right_logical(entry, 4), K_DEV - 1)
            block = jnp.bitwise_and(entry, BLOCKS - 1)
            windows.append(signal[block, pl.ds(delay_ref[k, block], TW), :].astype(BF16))
            blocks.append(wv[jnp.where(entry < ENTRIES, block * K_DEV + k, ENTRIES)])
        term = jnp.dot(
            jnp.concatenate(windows, axis=1), jnp.concatenate(blocks, axis=0),
            preferred_element_type=F32)
        trail[p + 1] = term + trail[jnp.where(order[2, p] > 0, 0, p)]

    def far_pairs(first, amount, unroll):
        def chunk(i, carry):
            for u in range(unroll):
                far_pair(first + i * unroll + u)
            return carry
        lax.fori_loop(0, amount // unroll, chunk, 0)

    def far_collect():
        for j in range(TARGETS):
            end = jnp.clip(order[1, j], 0, PAIRS)
            for quarter in range(4):
                found = trail[end, quarter * 128:(quarter + 1) * 128, :]
                part[j, quarter] = found.reshape(4, 2, ROWS, DB)

    def core_start():
        far_collect()
        for half in range(2):
            core_copy(half).start()

    loads[3].wait()

    def plane_coefficients(xs, carry):
        for x in xs:
            code = codes[x]
            for index, values in enumerate(COEFFICIENTS):
                coef[index, x] = jnp.where(
                    code == 0, values[0],
                    jnp.where(code == 1, values[1], jnp.where(code == 2, values[2], values[3])),
                ).astype(F32)
        return carry

    over_planes(plane_coefficients, 0)
    slot_lane = lax.broadcasted_iota(jnp.int32, (PB, PB), 1)
    for i in range(SLOT // PB):
        slots = slice(i * PB, (i + 1) * PB)
        cell = jnp.broadcast_to(surf_ref[:, slots].astype(F32), (PB, PB)).T.astype(jnp.int32)
        cell_row = lax.shift_right_arithmetic(cell, 7)
        cellmask[slots, :] = jnp.where(
            slot_lane == jnp.bitwise_and(cell, CZ - 1), 1.0, 0.0)
        for q in range(CX * CY // PB):
            onehot[slots, q * PB:(q + 1) * PB] = jnp.where(
                slot_lane + q * PB == cell_row, 1.0, 0.0).astype(BF16)
    loads[4].wait()

    def leap(step):
        here_ref, other_ref = fields[step % 2], fields[1 - step % 2]
        last = step == STEPS - 1
        halo_wait_recv(step, (1, 2))

        def y_rows(xs, carry):
            rows = [(yrecv[step, 0, pl.ds(x, 1), :], yrecv[step, 1, pl.ds(x, 1), :]) for x in xs]
            for x, (low, high) in zip(xs, rows):
                here_ref[x + 1, LOW - 1:LOW, :] = low
                here_ref[x + 1, HIGH:HIGH + 1, :] = high
            return carry

        over_planes(y_rows, 0, 16)
        z_halo = jnp.where(
            jnp.bitwise_and(lane, 1) == 0,
            pltpu.roll(zrecv[step, 0], 1, 1), pltpu.roll(zrecv[step, 1], CZ - 1, 1))
        ends = jnp.logical_or(lane == 0, lane == CZ - 1)

        def plane_step(xs, carry):
            planes = []
            for x in xs:
                here = here_ref[x + 1, LOW:HIGH, :]
                around = here_ref[x, LOW:HIGH, :] + here_ref[x + 2, LOW:HIGH, :]
                around = around + (
                    here_ref[x + 1, LOW - 1:HIGH - 1, :] + here_ref[x + 1, LOW + 1:HIGH + 1, :])
                beside_z = (jnp.where(lane == 0, 0.0, pltpu.roll(here, 1, 1))
                            + jnp.where(lane == CZ - 1, 0.0, pltpu.roll(here, CZ - 1, 1)))
                outside = pltpu.roll(z_halo, lax.rem(2 * (CZ - x), CZ), 1)
                around = around + (beside_z + jnp.where(ends, outside, 0.0))
                before = other_ref[x + 1, LOW:HIGH, :]
                planes.append(coef[0, x] * here + coef[1, x] * before + coef[2, x] * around)
            for x, new in zip(xs, planes):
                other_ref[x + 1, LOW:HIGH, :] = new
                rounded[step % 2, pl.ds(x * CY if isinstance(x, int) else pl.multiple_of(x * CY, CY), CY), :] = new.astype(BF16)
            if last:
                return carry
            return take_faces(step + 1, xs, planes, carry)

        def inner(i, carry):
            return plane_step([1 + i * 10 + u for u in range(10)], carry)

        carry = lax.fori_loop(
            0, (CX - 2) // 10, inner, 0 if last else zero_plane)
        halo_wait_recv(step, (0,))
        if step > 0:
            halo_wait_send(step - 1, (0,))
        here_ref[0, LOW:HIGH, :] = xrecv[step, 0]
        here_ref[CX + 1, LOW:HIGH, :] = xrecv[step, 1]
        carry = plane_step([0, CX - 1], carry)
        if not last:
            zstage[step + 1] = carry
            halo_start(step + 1)

    def sample(step):
        picked = jnp.dot(onehot[...], rounded[step % 2], preferred_element_type=F32)
        values = lax.dot_general(
            jnp.ones((8, CZ), BF16), (picked * cellmask[...]).astype(BF16),
            (((1,), (1,)), ((), ())), preferred_element_type=F32)
        if step < STEPS - 1:
            samp_send[4 + step:5 + step, :] = values[0:1, :]
        else:
            last_send[...] = values

    axes = (("z", "y"), ("y", "z"))

    def index_on(axis):
        return z if axis == "z" else y

    def ring_copy(half, kind, way):
        axis = axes[half][0]
        place_now = index_on(axis)
        step_to = 1 if way == 0 else 3
        chunk = lax.rem(place_now + (2 if kind == 0 else step_to), 4)
        part_now = pl.ds(0 if (kind == 1) == (way == 1) else 2, 2)
        return pltpu.make_async_remote_copy(
            src_ref=sums.at[half, chunk, part_now], dst_ref=ring1.at[half, kind, way],
            send_sem=ring_send.at[half, kind, way],
            recv_sem=ring_recv.at[half, kind, way],
            device_id=ring_neighbour(axis, step_to), device_id_type=MESH,
        )

    def direct_copy(half, offset):
        axis = axes[half][1]
        return pltpu.make_async_remote_copy(
            src_ref=totals.at[half, lax.rem(index_on(axis) + offset, 4)],
            dst_ref=ring2.at[half, offset - 1],
            send_sem=direct_send.at[half, offset - 1],
            recv_sem=direct_recv.at[half, offset - 1],
            device_id=ring_neighbour(axis, offset), device_id_type=MESH,
        )

    def core_finish(half):
        core_copy(half).wait_recv()

        for yy in range(4):
            for zz in range(4):
                total = (part[half * 4:half * 4 + 4, yy, zz, core]
                         + core_recv[half * 4:half * 4 + 4, yy, zz])
                if half == 0:
                    sums[0, zz, yy] = total
                else:
                    sums[1, yy, zz] = total

    def ring_begin(half):
        for kind in (0, 1):
            for way in (0, 1):
                ring_copy(half, kind, way).start()

    def ring_forward(half):
        place_now = index_on(axes[half][0])
        for way in (0, 1):
            ring_copy(half, 0, way).wait_recv()
            chunk = lax.rem(place_now + (1 if way == 0 else 3), 4)
            first = 0 if way == 0 else 2
            sums[half, chunk, first:first + 2] = (
                sums[half, chunk, first:first + 2] + ring1[half, 0, way])
            ring_copy(half, 2, way).start()

    def ring_end(half):
        place_now = index_on(axes[half][0])
        for kind in (1, 2):
            for way in (0, 1):
                ring_copy(half, kind, way).wait_recv()
        totals[half, 0:2] = sums[half, place_now, 0:2] + (ring1[half, 2, 0] + ring1[half, 1, 1])
        totals[half, 2:4] = sums[half, place_now, 2:4] + (ring1[half, 1, 0] + ring1[half, 2, 1])
        for offset in (2, 1, 3):
            direct_copy(half, offset).start()

    def direct_end(half):
        for offset in (1, 2, 3):
            direct_copy(half, offset).wait_recv()
        result = totals[half, index_on(axes[half][1])]
        result = result + (ring2[half, 0] + (ring2[half, 1] + ring2[half, 2]))
        for j in range(4):
            columns = slice((half * 4 + j) * DB, (half * 4 + j + 1) * DB)
            far_ref[:, columns] = result[j]

    def samp_copy(last, offset, arriving=False):
        source, target = (last_send, last_all) if last else (samp_send, samp_all)
        slot = lax.rem(gy + NY_DEV - offset, NY_DEV) if arriving else gy
        return pltpu.make_async_remote_copy(
            src_ref=source, dst_ref=target.at[slot],
            send_sem=samp_ssem.at[last, offset - 1], recv_sem=samp_rsem.at[last, offset - 1],
            device_id=(gx, lax.rem(gy + offset, NY_DEV), gz), device_id_type=MESH,
        )

    def samp_start(last):
        for offset in range(1, NY_DEV):
            samp_copy(last, offset).start()
        if last:
            last_all[gy] = last_send[...]
        else:
            samp_all[gy] = samp_send[...]

    def samp_wait(last):
        for offset in range(1, NY_DEV):
            samp_copy(last, offset, True).wait_recv()

    row = lax.broadcasted_iota(jnp.int32, (8, PB), 0)
    width = 4 * K_DEV * PB

    def entry_rows(i, carry):
        held = []
        for block in [i * 4 + u for u in range(4)]:
            for entry in range(K_DEV):
                offset = delay_ref[entry, block]
                target = dir_ref[entry, block]
                early = spad[block, pl.ds(offset + 4, 8), :]
                late = spad[block, pl.ds(offset, 8), :]
                pair = jnp.where(row < 4, early, late)
                pieces = []
                for k in range(TARGETS // 2):
                    wanted = jnp.where(row < 4, 2 * k, 2 * k + 1)
                    pieces.append(jnp.where(wanted == target, pair, 0.0))
                held.append(jnp.concatenate(pieces, axis=0).astype(BF16))
        part_rows = pl.ds(pl.multiple_of((i // 2) * 32, 32), 32)
        columns = pl.ds(pl.multiple_of(lax.rem(i, 2) * width, width), width)
        lhs[part_rows, columns] = jnp.concatenate(held, axis=1)
        return carry

    def last_rows():
        for brick in range(NY_DEV // 2):
            rows = []
            for part_of in (brick, brick + NY_DEV // 2):
                held = []
                for i in range(SLOT // PB):
                    block = part_of * (SLOT // PB) + i
                    samples = last_all[part_of, :, i * PB:(i + 1) * PB]
                    for entry in range(K_DEV):
                        target = jnp.where(
                            delay_ref[entry, block] == MAXOFF, dir_ref[entry, block], -1)
                        held.append(jnp.where(row == target, samples, 0.0))
                rows.append(jnp.concatenate(held, axis=1))
            last_lhs[:, brick * width:(brick + 1) * width] = (
                jnp.concatenate(rows, axis=0).astype(BF16))

    def times_weights(rows_ref):
        half = ENTRIES // 2
        beside_each_other = jnp.concatenate(
            [wv[:half].reshape(half * PB, DB), wv[half:ENTRIES].reshape(half * PB, DB)], axis=1)
        product = jnp.dot(rows_ref[...], beside_each_other, preferred_element_type=F32)
        count_rows = product.shape[0] // 2
        return product[:count_rows, :DB] + product[count_rows:, DB:]

    def corr_copy(last, member):
        source, target = (last_out, last_in) if last else (corr_out, corr_in)
        return pltpu.make_async_remote_copy(
            src_ref=source, dst_ref=target.at[member],
            send_sem=last_ssem if last else corr_ssem,
            recv_sem=(last_rsem if last else corr_rsem).at[member],
            device_id=owner, device_id_type=MESH,
        )

    def corr_start(last):
        @pl.when(jnp.logical_not(is_owner))
        def _():
            corr_copy(last, group).start()

    far_pairs(0, 28, 14)
    leap(0)
    far_pairs(28, PAIRS - 28, 12)
    core_start()
    leap(1)
    sample(0)
    sample(1)
    for half in range(2):
        core_finish(half)
        ring_begin(half)
    leap(2)
    save_prev = pltpu.make_async_copy(
        field_b.at[pl.ds(1, CX), pl.ds(LOW, CY)], prev_ref, load_sem.at[5])
    save_prev.start()
    sample(2)
    samp_start(0)
    for half in range(2):
        ring_forward(half)
    leap(3)
    sample(3)
    samp_start(1)
    save_next = pltpu.make_async_copy(
        field_a.at[pl.ds(1, CX), pl.ds(LOW, CY)], next_ref, load_sem.at[6])
    save_next.start()
    for half in range(2):
        ring_end(half)
    samp_wait(0)
    for brick in range(NY_DEV):
        for i in range(SLOT // PB):
            spad[brick * (SLOT // PB) + i, 32:40, :] = samp_all[brick, :, i * PB:(i + 1) * PB]
    lax.fori_loop(0, BLOCKS // 4, entry_rows, 0)
    corr_out[...] = times_weights(lhs)
    corr_start(0)
    samp_wait(1)
    last_rows()
    last_out[...] = times_weights(last_lhs)
    corr_start(1)
    for half in range(2):
        direct_end(half)

    @pl.when(is_owner)
    def _():
        def arrivals(last):
            def one(member, carry):
                corr_copy(last, member).wait_recv()
                return carry
            lax.fori_loop(0, OWNERS - 1, one, 0)

        arrivals(0)
        total = corr_out[...]
        for member in range(OWNERS - 1):
            total = total + corr_in[member]
        for j in range(TARGETS):
            piece = total[(j // 2) * 8:(j // 2) * 8 + 8, :]
            if j % 2 == 0:
                piece = pltpu.roll(piece, 4, 0)
            columns = slice(j * DB, (j + 1) * DB)
            far_ref[8:16, columns] = far_ref[8:16, columns] + jnp.where(row >= 4, piece, 0.0)
        arrivals(1)
        total = last_out[...]
        for member in range(OWNERS - 1):
            total = total + last_in[member]
        for j in range(TARGETS):
            columns = slice(j * DB, (j + 1) * DB)
            far_ref[15:16, columns] = far_ref[15:16, columns] + total[j:j + 1, :]

    for step in range(STEPS):
        halo_wait_send(step, (0, 1, 2) if step == STEPS - 1 else (1, 2))
    for half in range(2):
        core_copy(half).wait_send()
        for kind in range(3):
            for way in range(2):
                ring_copy(half, kind, way).wait_send()
        for offset in (1, 2, 3):
            direct_copy(half, offset).wait_send()
    for last in range(2):
        for offset in range(1, NY_DEV):
            samp_copy(last, offset).wait_send()

    @pl.when(jnp.logical_not(is_owner))
    def _():
        corr_copy(0, group).wait_send()
        corr_copy(1, group).wait_send()

    save_prev.wait()
    save_next.wait()


def hall(dirs, delays, surf_index, now, old, code, history, weights):
    any_space = pl.BlockSpec(memory_space=pl.ANY)
    smem = pl.BlockSpec(memory_space=pltpu.SMEM)
    vmem = pl.BlockSpec(memory_space=pltpu.VMEM)
    dma = pltpu.SemaphoreType.DMA
    brick = jax.ShapeDtypeStruct((CX, CY, CZ), F32)
    return pl.pallas_call(
        hall_kernel,
        out_shape=(brick, brick, jax.ShapeDtypeStruct((ROWS, TARGETS * DB), F32)),
        in_specs=[smem, smem, vmem, vmem] + [any_space] * 5,
        out_specs=(any_space, any_space, vmem),
        scratch_shapes=[
            pltpu.VMEM((CX + 2, PADROWS, CZ), F32),
            pltpu.VMEM((CX + 2, PADROWS, CZ), F32),
            pltpu.VMEM((CX, CY, CZ), jnp.int32),
            pltpu.VMEM((3, CX, CY, CZ), F32),
            pltpu.VMEM((STEPS, 2, CX, CZ), F32),
            pltpu.VMEM((STEPS, CY, CZ), F32),
            pltpu.VMEM((STEPS, 2, CY, CZ), F32),
            pltpu.VMEM((STEPS, 2, CX, CZ), F32),
            pltpu.VMEM((STEPS, 2, CY, CZ), F32),
            pltpu.VMEM((SLOT, CX * CY), BF16),
            pltpu.VMEM((SLOT, CZ), F32),
            pltpu.VMEM((2, CX * CY, CZ), BF16),
            pltpu.VMEM((8, SLOT), F32),
            pltpu.VMEM((NY_DEV, 8, SLOT), F32),
            pltpu.VMEM((8, SLOT), F32),
            pltpu.VMEM((NY_DEV, 8, SLOT), F32),
            pltpu.VMEM((BLOCKS, 48, PB), F32),
            pltpu.VMEM((64, ENTRIES // 2 * PB), BF16),
            pltpu.VMEM((16, ENTRIES // 2 * PB), BF16),
            pltpu.VMEM((ENTRIES + 1, PB, DB), BF16),
            pltpu.VMEM((BLOCKS, TW + MAXOFF, PB), F32),
            pltpu.VMEM((PAIRS + 1, TW, DB), F32),
            pltpu.VMEM((8, PB), jnp.int32),
            pltpu.SMEM((8, PB), jnp.int32),
            pltpu.VMEM((HOLD, BLOCKS * PB), BF16),
            pltpu.VMEM((TARGETS, 4, 4, 2, ROWS, DB), F32),
            pltpu.VMEM((TARGETS, 4, 4, ROWS, DB), F32),
            pltpu.VMEM((2, 4, 4, 4, ROWS, DB), F32),
            pltpu.VMEM((2, 4, 4, ROWS, DB), F32),
            pltpu.VMEM((2, 3, 2, 2, 4, ROWS, DB), F32),
            pltpu.VMEM((2, 3, 4, ROWS, DB), F32),
            pltpu.VMEM((32, DB), F32),
            pltpu.VMEM((OWNERS, 32, DB), F32),
            pltpu.VMEM((8, DB), F32),
            pltpu.VMEM((OWNERS, 8, DB), F32),
            dma((8,)),
            dma((STEPS, 3, 2)), dma((STEPS, 3, 2)),
            dma((2, 3)), dma((2, 3)),
            dma((2,)), dma((2,)),
            dma((2, 3, 2)), dma((2, 3, 2)), dma((2, 3)), dma((2, 3)),
            dma, dma((OWNERS,)), dma, dma((OWNERS,)),
        ],
        compiler_params=pltpu.CompilerParams(
            collective_id=0, has_side_effects=True, vmem_limit_bytes=58 * 1024 * 1024),
    )(dirs, delays, dirs, surf_index, history, now, old, code, weights)


def save_kernel(*refs):
    sources, targets, held, sems = refs[:3], refs[3:6], refs[6:9], refs[9]
    pieces = [(i, slice(first, first + CX // 4)) for first in range(0, CX, CX // 4) for i in (0, 1)]
    pieces.append((2, slice(0, ROWS)))
    arrivals, leaves = [], []
    for number, (i, part) in enumerate(pieces):
        arrivals.append(pltpu.make_async_copy(
            sources[i].at[part], held[i].at[part], sems.at[0, number]))
        leaves.append(pltpu.make_async_copy(
            held[i].at[part], targets[i].at[part], sems.at[1, number]))
    for copy in arrivals:
        copy.start()
    for arrival, leave in zip(arrivals, leaves):
        arrival.wait()
        leave.start()
    for copy in leaves:
        copy.wait()


def save(arrays):
    any_space = pl.BlockSpec(memory_space=pl.ANY)
    return pl.pallas_call(
        save_kernel,
        out_shape=tuple(jax.ShapeDtypeStruct(a.shape, a.dtype) for a in arrays),
        in_specs=[any_space] * 3,
        out_specs=(any_space,) * 3,
        scratch_shapes=[pltpu.VMEM(a.shape, a.dtype) for a in arrays]
        + [pltpu.SemaphoreType.DMA((2, 9))],
    )(*arrays)


def shards(pressure_now, pressure_old, cell_code, surf_index, history, dir_slot, delay, weights):
    flat_weights = weights.reshape(BLOCKS * K_DEV, PB, DB)
    return save(hall(
        dir_slot.T, delay.T, surf_index, pressure_now, pressure_old, cell_code, history,
        flat_weights))


def solution(mesh):
    return jax.shard_map(
        shards,
        mesh=mesh,
        in_specs=(
            P("gx", "gy", "gz"),
            P("gx", "gy", "gz"),
            P("gx", "gy", "gz"),
            P(("gx", "gz"), "gy"),
            P(None, ("gx", "gz")),
            P(("gx", "gz"), "gy"),
            P(("gx", "gz"), "gy"),
            P(("gx", "gz"), "gy", None, None),
        ),
        out_specs=(P("gx", "gy", "gz"), P("gx", "gy", "gz"), P(("gx", "gz"), "gy")),
        check_vma=False,
    )
```

```python
import functools

import jax
import jax.numpy as jnp
import numpy as np
from jax import lax
from jax.experimental import pallas as pl
from jax.experimental.pallas import tpu as pltpu
from jax.sharding import PartitionSpec as P

MESH = pl.DeviceIdType.MESH
F32 = jnp.float32
BF16 = jnp.bfloat16

STEPS = 4
CX, CY, CZ = 32, 32, 128
SLOT = 512
TW = 512
MAXOFF = 32
HOLD = 540
PB = 128
DB = 128
K_DEV = 6
BLOCKS = 16
ENTRIES = K_DEV * BLOCKS
PAIRS = ENTRIES // 2 + 4
TARGETS = 8
OWNERS = 32
ROWS = 16
NX_DEV, NY_DEV, NZ_DEV = 8, 4, 4
LOW, HIGH = 8, 40
PADROWS = 48


def coefficient_table():
    speeds = np.array([0.32, 0.26, 0.19, 0.11], np.float32).astype(np.float64)
    damping = np.array([0.0, 0.02, 0.08, 0.3], np.float32).astype(np.float64)
    here = (2.0 - 6.0 * speeds) / (1.0 + damping)
    before = -(1.0 - damping) / (1.0 + damping)
    around = speeds / (1.0 + damping)
    return [[float(np.float32(v)) for v in row] for row in (here, before, around)]


COEFFICIENTS = coefficient_table()


def hall_kernel(
    dir_ref, delay_ref, dirs_ref, surf_ref, hist_ref, now_ref, old_ref, code_ref, w_ref,
    next_ref, prev_ref, far_ref,
    field_a, field_b, codes, coef, ystage, zstage, xrecv, yrecv, zrecv,
    onehot, cellmask, rounded, samp_send, samp_all, last_send, last_all, spad, lhs, last_lhs, wv,
    signal, trail, table, order, hist, part, core_recv, sums, totals, ring1, ring2, corr_out, corr_in, last_out, last_in,
    load_sem, idle_sem, halo_send, halo_recv, samp_ssem, samp_rsem,
    core_ssem, core_rsem, ring_send, ring_recv, direct_send, direct_recv, corr_ssem, corr_rsem, last_ssem, last_rsem,
):
    fields = (field_a, field_b)
    gx, gy, gz = lax.axis_index("gx"), lax.axis_index("gy"), lax.axis_index("gz")
    y, z_hi = gx // 2, lax.rem(gx, 2)
    z_lo, core = gz // 2, lax.rem(gz, 2)
    z = z_hi * 2 + z_lo
    group = gx * 4 + gz
    is_owner = group == OWNERS - 1

    def place(yy, zz):
        return (yy * 2 + zz // 2, gy, lax.rem(zz, 2) * 2 + core)

    def ring_neighbour(axis, offset):
        if axis == "z":
            return place(y, lax.rem(z + offset, 4))
        return place(lax.rem(y + offset, 4), z)

    sibling = (gx, gy, z_lo * 2 + 1 - core)
    owner = (NX_DEV - 1, gy, NZ_DEV - 1)
    coords = (gx, gy, gz)
    extents = (NX_DEV, NY_DEV, NZ_DEV)

    def beside(axis, side):
        moved = list(coords)
        moved[axis] = coords[axis] + (1 if side else -1)
        return tuple(moved)

    def exists(axis, side):
        return coords[axis] < extents[axis] - 1 if side else coords[axis] > 0

    barrier = pltpu.get_barrier_semaphore()

    def greet(device):
        pl.semaphore_signal(barrier, inc=1, device_id=device, device_id_type=MESH)

    expected = jnp.int32(10)
    for axis in range(3):
        for side in range(2):
            @pl.when(exists(axis, side))
            def _():
                greet(beside(axis, side))
            expected = expected + exists(axis, side).astype(jnp.int32)
    greet(sibling)
    for axis in ("y", "z"):
        for offset in (1, 2, 3):
            greet(ring_neighbour(axis, offset))
    for offset in range(1, NY_DEV):
        greet((gx, lax.rem(gy + offset, NY_DEV), gz))

    @pl.when(is_owner)
    def _():
        def greet_one(member, carry):
            greet((member // 4, gy, lax.rem(member, 4)))
            return carry
        lax.fori_loop(0, OWNERS - 1, greet_one, 0)

    expected = expected + jnp.where(is_owner, 0, 1)

    loads = [
        pltpu.make_async_copy(now_ref, field_a.at[pl.ds(1, CX), pl.ds(LOW, CY)], load_sem.at[0]),
        pltpu.make_async_copy(hist_ref, hist, load_sem.at[3]),
        pltpu.make_async_copy(w_ref, wv.at[pl.ds(0, ENTRIES)], load_sem.at[4]),
        pltpu.make_async_copy(code_ref, codes, load_sem.at[2]),
        pltpu.make_async_copy(old_ref, field_b.at[pl.ds(1, CX), pl.ds(LOW, CY)], load_sem.at[1]),
    ]
    for load in loads:
        load.start()

    lane = lax.broadcasted_iota(jnp.int32, (CY, CZ), 1)
    zero_plane = jnp.zeros((CY, CZ), F32)

    def over_planes(body, init, unroll=8):
        def chunk(i, carry):
            return body([i * unroll + u for u in range(unroll)], carry)
        return lax.fori_loop(0, CX // unroll, chunk, init)

    def take_faces(step, xs, planes, held):
        for x, plane in zip(xs, planes):
            mine = jnp.logical_or(lane == 2 * x, lane == lax.rem(2 * x + CZ - 1, CZ))
            held = jnp.where(mine, pltpu.roll(plane, 2 * x, 1), held)
        for x, plane in zip(xs, planes):
            ystage[step, 0, pl.ds(x, 1), :] = plane[0:1, :]
            ystage[step, 1, pl.ds(x, 1), :] = plane[CY - 1:CY, :]
        return held

    def halo_copy(step, axis, side):
        current = step % 2
        if axis == 0:
            source = fields[current].at[CX if side else 1, pl.ds(LOW, CY)]
            target = xrecv.at[step, 1 - side]
        elif axis == 1:
            source, target = ystage.at[step, side], yrecv.at[step, 1 - side]
        else:
            source, target = zstage.at[step], zrecv.at[step, 1 - side]
        return pltpu.make_async_remote_copy(
            src_ref=source, dst_ref=target,
            send_sem=halo_send.at[step, axis, side],
            recv_sem=halo_recv.at[step, axis, 1 - side],
            device_id=beside(axis, side), device_id_type=MESH,
        )

    def halo_start(step):
        for axis in range(3):
            for side in range(2):
                @pl.when(exists(axis, side))
                def _():
                    halo_copy(step, axis, side).start()

    def halo_wait_send(step, axes=(0, 1, 2)):
        for axis in axes:
            for side in range(2):
                @pl.when(exists(axis, side))
                def _():
                    halo_copy(step, axis, side).wait_send()

    def halo_wait_recv(step, axes):
        for axis in axes:
            buffer = (xrecv, yrecv, zrecv)[axis]
            for side in range(2):
                @pl.when(exists(axis, side))
                def _():
                    halo_copy(step, axis, 1 - side).wait_recv()
                @pl.when(jnp.logical_not(exists(axis, side)))
                def _():
                    buffer[step, side] = zero_plane

    dirs = dirs_ref[...]
    targets = jnp.concatenate(
        [dirs[k:k + 1, :] for k in range(K_DEV)]
        + [jnp.full((1, PB - ENTRIES), -1, jnp.int32)], axis=1)
    targets = jnp.where(targets >= 0, targets, TARGETS).astype(F32)
    by_lane = jnp.broadcast_to(targets, (PB, PB))
    by_row = by_lane.T
    lanes = lax.broadcasted_iota(jnp.int32, (PB, PB), 1).astype(F32)
    rows = lax.broadcasted_iota(jnp.int32, (PB, PB), 0).astype(F32)

    def count(mask, axis):
        return jnp.sum(jnp.where(mask, 1.0, 0.0), axis=axis, keepdims=True)

    def even(amount):
        return 2.0 * jnp.floor(0.5 * (amount + 1.0))

    member = by_row == lanes
    along_lanes = count(member, 0)
    along_rows = count(by_lane == rows, 1)
    first_lanes = jnp.sum(jnp.where(rows < lanes, even(along_rows), 0.0), axis=0, keepdims=True)
    first_rows = jnp.sum(jnp.where(lanes < rows, even(along_lanes), 0.0), axis=1, keepdims=True)
    before = count(jnp.logical_and(by_lane == by_row, lanes < rows), 1)
    slot = before + jnp.sum(jnp.where(member, first_lanes, 0.0), axis=1, keepdims=True)
    taken = jnp.logical_and(slot == lanes, by_row < TARGETS)
    sequence = ENTRIES + jnp.sum(jnp.where(taken, rows - ENTRIES, 0.0), axis=0, keepdims=True)
    ends = jnp.where(along_lanes > 0, 0.5 * (first_lanes + even(along_lanes)), 0.0)
    opens = count(
        jnp.logical_and(jnp.logical_and(0.5 * first_rows == lanes, along_rows > 0), rows < TARGETS), 0)
    table[0:1, :] = sequence.astype(jnp.int32)
    table[1:2, :] = ends.astype(jnp.int32)
    table[2:3, :] = opens.astype(jnp.int32)
    table[3:8, :] = jnp.zeros((5, PB), jnp.int32)
    order_load = pltpu.make_async_copy(table, order, load_sem.at[7])
    order_load.start()

    def core_copy(half):
        return pltpu.make_async_remote_copy(
            src_ref=part.at[pl.ds(half * 4, 4), :, :, 1 - core],
            dst_ref=core_recv.at[pl.ds(half * 4, 4)],
            send_sem=core_ssem.at[half], recv_sem=core_rsem.at[half],
            device_id=sibling, device_id_type=MESH,
        )

    samp_send[...] = jnp.zeros_like(samp_send)
    spad[...] = jnp.zeros_like(spad)
    trail[0] = jnp.zeros((TW, DB), F32)
    wv[ENTRIES] = jnp.zeros((PB, DB), BF16)
    for block in range(BLOCKS):
        signal[block, HOLD:, :] = jnp.zeros((TW + MAXOFF - HOLD, PB), F32)

    loads[0].wait()

    def first_faces(xs, carry):
        return take_faces(0, xs, [field_a[x + 1, LOW:HIGH, :] for x in xs], carry)

    zstage[0] = over_planes(first_faces, zero_plane)

    pl.semaphore_wait(barrier, expected)
    halo_start(0)

    loads[1].wait()

    for block in range(BLOCKS):
        signal[block, :HOLD, :] = hist[:, block * PB:(block + 1) * PB].astype(F32)
    order_load.wait()
    loads[2].wait()


    def far_pair(p):
        windows, blocks = [], []
        for u in range(2):
            entry = jnp.clip(order[0, 2 * p + u], 0, ENTRIES)
            k = jnp.minimum(lax.shift_right_logical(entry, 4), K_DEV - 1)
            block = jnp.bitwise_and(entry, BLOCKS - 1)
            windows.append(signal[block, pl.ds(delay_ref[k, block], TW), :].astype(BF16))
            blocks.append(wv[jnp.where(entry < ENTRIES, block * K_DEV + k, ENTRIES)])
        term = jnp.dot(
            jnp.concatenate(windows, axis=1), jnp.concatenate(blocks, axis=0),
            preferred_element_type=F32)
        trail[p + 1] = term + trail[jnp.where(order[2, p] > 0, 0, p)]

    def far_pairs(first, amount, unroll):
        def chunk(i, carry):
            for u in range(unroll):
                far_pair(first + i * unroll + u)
            return carry
        lax.fori_loop(0, amount // unroll, chunk, 0)

    def far_collect():
        for j in range(TARGETS):
            end = jnp.clip(order[1, j], 0, PAIRS)
            for quarter in range(4):
                found = trail[end, quarter * 128:(quarter + 1) * 128, :]
                part[j, quarter] = found.reshape(4, 2, ROWS, DB)

    def core_start():
        far_collect()
        for half in range(2):
            core_copy(half).start()

    loads[3].wait()

    def plane_coefficients(xs, carry):
        for x in xs:
            code = codes[x]
            for index, values in enumerate(COEFFICIENTS):
                coef[index, x] = jnp.where(
                    code == 0, values[0],
                    jnp.where(code == 1, values[1], jnp.where(code == 2, values[2], values[3])),
                ).astype(F32)
        return carry

    over_planes(plane_coefficients, 0)
    slot_lane = lax.broadcasted_iota(jnp.int32, (PB, PB), 1)
    for i in range(SLOT // PB):
        slots = slice(i * PB, (i + 1) * PB)
        cell = jnp.broadcast_to(surf_ref[:, slots].astype(F32), (PB, PB)).T.astype(jnp.int32)
        cell_row = lax.shift_right_arithmetic(cell, 7)
        cellmask[slots, :] = jnp.where(
            slot_lane == jnp.bitwise_and(cell, CZ - 1), 1.0, 0.0)
        for q in range(CX * CY // PB):
            onehot[slots, q * PB:(q + 1) * PB] = jnp.where(
                slot_lane + q * PB == cell_row, 1.0, 0.0).astype(BF16)
    loads[4].wait()

    def leap(step):
        here_ref, other_ref = fields[step % 2], fields[1 - step % 2]
        last = step == STEPS - 1
        halo_wait_recv(step, (1, 2))

        def y_rows(xs, carry):
            rows = [(yrecv[step, 0, pl.ds(x, 1), :], yrecv[step, 1, pl.ds(x, 1), :]) for x in xs]
            for x, (low, high) in zip(xs, rows):
                here_ref[x + 1, LOW - 1:LOW, :] = low
                here_ref[x + 1, HIGH:HIGH + 1, :] = high
            return carry

        over_planes(y_rows, 0, 16)
        z_halo = jnp.where(
            jnp.bitwise_and(lane, 1) == 0,
            pltpu.roll(zrecv[step, 0], 1, 1), pltpu.roll(zrecv[step, 1], CZ - 1, 1))
        ends = jnp.logical_or(lane == 0, lane == CZ - 1)

        def plane_step(xs, carry):
            planes = []
            for x in xs:
                here = here_ref[x + 1, LOW:HIGH, :]
                around = here_ref[x, LOW:HIGH, :] + here_ref[x + 2, LOW:HIGH, :]
                around = around + (
                    here_ref[x + 1, LOW - 1:HIGH - 1, :] + here_ref[x + 1, LOW + 1:HIGH + 1, :])
                beside_z = (jnp.where(lane == 0, 0.0, pltpu.roll(here, 1, 1))
                            + jnp.where(lane == CZ - 1, 0.0, pltpu.roll(here, CZ - 1, 1)))
                outside = pltpu.roll(z_halo, lax.rem(2 * (CZ - x), CZ), 1)
                around = around + (beside_z + jnp.where(ends, outside, 0.0))
                before = other_ref[x + 1, LOW:HIGH, :]
                planes.append(coef[0, x] * here + coef[1, x] * before + coef[2, x] * around)
            for x, new in zip(xs, planes):
                other_ref[x + 1, LOW:HIGH, :] = new
                rounded[step % 2, pl.ds(x * CY if isinstance(x, int) else pl.multiple_of(x * CY, CY), CY), :] = new.astype(BF16)
            if last:
                return carry
            return take_faces(step + 1, xs, planes, carry)

        def inner(i, carry):
            return plane_step([1 + i * 10 + u for u in range(10)], carry)

        carry = lax.fori_loop(
            0, (CX - 2) // 10, inner, 0 if last else zero_plane)
        halo_wait_recv(step, (0,))
        if step > 0:
            halo_wait_send(step - 1, (0,))
        here_ref[0, LOW:HIGH, :] = xrecv[step, 0]
        here_ref[CX + 1, LOW:HIGH, :] = xrecv[step, 1]
        carry = plane_step([0, CX - 1], carry)
        if not last:
            zstage[step + 1] = carry
            halo_start(step + 1)

    def sample(step):
        picked = jnp.dot(onehot[...], rounded[step % 2], preferred_element_type=F32)
        values = lax.dot_general(
            jnp.ones((8, CZ), BF16), (picked * cellmask[...]).astype(BF16),
            (((1,), (1,)), ((), ())), preferred_element_type=F32)
        if step < STEPS - 1:
            samp_send[4 + step:5 + step, :] = values[0:1, :]
        else:
            last_send[...] = values

    def wait_all_recv(ref, sem):
        pltpu.make_async_remote_copy(
            src_ref=ref, dst_ref=ref, send_sem=idle_sem, recv_sem=sem,
            device_id=sibling, device_id_type=MESH).wait_recv()

    def wait_all_send(ref, sem):
        pltpu.make_async_remote_copy(
            src_ref=ref, dst_ref=ref, send_sem=sem, recv_sem=idle_sem,
            device_id=sibling, device_id_type=MESH).wait_send()

    axes = (("z", "y"), ("y", "z"))

    def index_on(axis):
        return z if axis == "z" else y

    def ring_copy(half, kind, way):
        axis = axes[half][0]
        place_now = index_on(axis)
        step_to = 1 if way == 0 else 3
        chunk = lax.rem(place_now + (2 if kind == 0 else step_to), 4)
        part_now = pl.ds(0 if (kind == 1) == (way == 1) else 2, 2)
        return pltpu.make_async_remote_copy(
            src_ref=sums.at[half, chunk, part_now], dst_ref=ring1.at[half, kind, way],
            send_sem=ring_send, recv_sem=ring_recv.at[0 if kind == 0 else 1],
            device_id=ring_neighbour(axis, step_to), device_id_type=MESH,
        )

    def direct_copy(half, offset):
        axis = axes[half][1]
        return pltpu.make_async_remote_copy(
            src_ref=totals.at[half, lax.rem(index_on(axis) + offset, 4)],
            dst_ref=ring2.at[half, offset - 1],
            send_sem=direct_send, recv_sem=direct_recv,
            device_id=ring_neighbour(axis, offset), device_id_type=MESH,
        )

    def core_finish(half):
        core_copy(half).wait_recv()

        for yy in range(4):
            for zz in range(4):
                total = (part[half * 4:half * 4 + 4, yy, zz, core]
                         + core_recv[half * 4:half * 4 + 4, yy, zz])
                if half == 0:
                    sums[0, zz, yy] = total
                else:
                    sums[1, yy, zz] = total

    def ring_begin(half):
        for kind in (0, 1):
            for way in (0, 1):
                ring_copy(half, kind, way).start()

    def ring_forward():
        wait_all_recv(ring1.at[:, 0], ring_recv.at[0])
        for half in range(2):
            place_now = index_on(axes[half][0])
            for way in (0, 1):
                chunk = lax.rem(place_now + (1 if way == 0 else 3), 4)
                first = 0 if way == 0 else 2
                sums[half, chunk, first:first + 2] = (
                    sums[half, chunk, first:first + 2] + ring1[half, 0, way])
                ring_copy(half, 2, way).start()

    def ring_end():
        wait_all_recv(ring1.at[:, pl.ds(1, 2)], ring_recv.at[1])
        for half in range(2):
            place_now = index_on(axes[half][0])
            totals[half, 0:2] = (
                sums[half, place_now, 0:2] + (ring1[half, 2, 0] + ring1[half, 1, 1]))
            totals[half, 2:4] = (
                sums[half, place_now, 2:4] + (ring1[half, 1, 0] + ring1[half, 2, 1]))
            for offset in (2, 1, 3):
                direct_copy(half, offset).start()

    def direct_end():
        wait_all_recv(ring2, direct_recv)
        for half in range(2):
            result = totals[half, index_on(axes[half][1])]
            result = result + (ring2[half, 0] + (ring2[half, 1] + ring2[half, 2]))
            for j in range(4):
                columns = slice((half * 4 + j) * DB, (half * 4 + j + 1) * DB)
                far_ref[:, columns] = result[j]

    def samp_copy(last, offset):
        source, target = (last_send, last_all) if last else (samp_send, samp_all)
        return pltpu.make_async_remote_copy(
            src_ref=source, dst_ref=target.at[gy],
            send_sem=samp_ssem.at[last], recv_sem=samp_rsem.at[last],
            device_id=(gx, lax.rem(gy + offset, NY_DEV), gz), device_id_type=MESH,
        )

    def samp_start(last):
        for offset in range(1, NY_DEV):
            samp_copy(last, offset).start()
        if last:
            last_all[gy] = last_send[...]
        else:
            samp_all[gy] = samp_send[...]

    def samp_wait(last):
        wait_all_recv((last_all if last else samp_all).at[pl.ds(0, NY_DEV - 1)], samp_rsem.at[last])

    row = lax.broadcasted_iota(jnp.int32, (8, PB), 0)
    width = 4 * K_DEV * PB

    def entry_rows(i, carry):
        held = []
        for block in [i * 4 + u for u in range(4)]:
            for entry in range(K_DEV):
                offset = delay_ref[entry, block]
                target = dir_ref[entry, block]
                early = spad[block, pl.ds(offset + 4, 8), :]
                late = spad[block, pl.ds(offset, 8), :]
                pair = jnp.where(row < 4, early, late)
                pieces = []
                for k in range(TARGETS // 2):
                    wanted = jnp.where(row < 4, 2 * k, 2 * k + 1)
                    pieces.append(jnp.where(wanted == target, pair, 0.0))
                held.append(jnp.concatenate(pieces, axis=0).astype(BF16))
        part_rows = pl.ds(pl.multiple_of((i // 2) * 32, 32), 32)
        columns = pl.ds(pl.multiple_of(lax.rem(i, 2) * width, width), width)
        lhs[part_rows, columns] = jnp.concatenate(held, axis=1)
        return carry

    def last_rows():
        for brick in range(NY_DEV // 2):
            rows = []
            for part_of in (brick, brick + NY_DEV // 2):
                held = []
                for i in range(SLOT // PB):
                    block = part_of * (SLOT // PB) + i
                    samples = last_all[part_of, :, i * PB:(i + 1) * PB]
                    for entry in range(K_DEV):
                        target = jnp.where(
                            delay_ref[entry, block] == MAXOFF, dir_ref[entry, block], -1)
                        held.append(jnp.where(row == target, samples, 0.0))
                rows.append(jnp.concatenate(held, axis=1))
            last_lhs[:, brick * width:(brick + 1) * width] = (
                jnp.concatenate(rows, axis=0).astype(BF16))

    def times_weights(rows_ref):
        half = ENTRIES // 2
        beside_each_other = jnp.concatenate(
            [wv[:half].reshape(half * PB, DB), wv[half:ENTRIES].reshape(half * PB, DB)], axis=1)
        product = jnp.dot(rows_ref[...], beside_each_other, preferred_element_type=F32)
        count_rows = product.shape[0] // 2
        return product[:count_rows, :DB] + product[count_rows:, DB:]

    def corr_copy(last, member):
        source, target = (last_out, last_in) if last else (corr_out, corr_in)
        return pltpu.make_async_remote_copy(
            src_ref=source, dst_ref=target.at[member],
            send_sem=last_ssem if last else corr_ssem,
            recv_sem=last_rsem if last else corr_rsem,
            device_id=owner, device_id_type=MESH,
        )

    def corr_start(last):
        @pl.when(jnp.logical_not(is_owner))
        def _():
            corr_copy(last, group).start()

    far_pairs(0, 28, 14)
    leap(0)
    far_pairs(28, PAIRS - 28, 12)
    core_start()
    halo_wait_send(0, (1, 2))
    leap(1)
    sample(0)
    sample(1)
    for half in range(2):
        core_finish(half)
        ring_begin(half)
    halo_wait_send(1, (1, 2))
    leap(2)
    save_prev = pltpu.make_async_copy(
        field_b.at[pl.ds(1, CX), pl.ds(LOW, CY)], prev_ref, load_sem.at[5])
    save_prev.start()
    sample(2)
    samp_start(0)
    ring_forward()
    halo_wait_send(2, (1, 2))
    leap(3)
    sample(3)
    samp_start(1)
    save_next = pltpu.make_async_copy(
        field_a.at[pl.ds(1, CX), pl.ds(LOW, CY)], next_ref, load_sem.at[6])
    save_next.start()
    ring_end()
    halo_wait_send(STEPS - 1)
    for half in range(2):
        core_copy(half).wait_send()
    wait_all_send(ring1, ring_send)
    wait_all_send(samp_all.at[pl.ds(0, NY_DEV - 1)], samp_ssem.at[0])
    samp_wait(0)
    for brick in range(NY_DEV):
        for i in range(SLOT // PB):
            spad[brick * (SLOT // PB) + i, 32:40, :] = samp_all[brick, :, i * PB:(i + 1) * PB]
    lax.fori_loop(0, BLOCKS // 4, entry_rows, 0)
    corr_out[...] = times_weights(lhs)
    corr_start(0)
    samp_wait(1)
    last_rows()
    last_out[...] = times_weights(last_lhs)
    corr_start(1)
    direct_end()

    @pl.when(is_owner)
    def _():
        def arrivals(last):
            held, sem = (last_in, last_rsem) if last else (corr_in, corr_rsem)
            wait_all_recv(held.at[pl.ds(0, OWNERS - 1)], sem)

        arrivals(0)
        total = corr_out[...]
        for member in range(OWNERS - 1):
            total = total + corr_in[member]
        for j in range(TARGETS):
            piece = total[(j // 2) * 8:(j // 2) * 8 + 8, :]
            if j % 2 == 0:
                piece = pltpu.roll(piece, 4, 0)
            columns = slice(j * DB, (j + 1) * DB)
            far_ref[8:16, columns] = far_ref[8:16, columns] + jnp.where(row >= 4, piece, 0.0)
        arrivals(1)
        total = last_out[...]
        for member in range(OWNERS - 1):
            total = total + last_in[member]
        for j in range(TARGETS):
            columns = slice(j * DB, (j + 1) * DB)
            far_ref[15:16, columns] = far_ref[15:16, columns] + total[j:j + 1, :]

    wait_all_send(ring2, direct_send)
    wait_all_send(last_all.at[pl.ds(0, NY_DEV - 1)], samp_ssem.at[1])

    @pl.when(jnp.logical_not(is_owner))
    def _():
        corr_copy(0, group).wait_send()
        corr_copy(1, group).wait_send()

    save_prev.wait()
    save_next.wait()


def hall(dirs, delays, surf_index, now, old, code, history, weights):
    any_space = pl.BlockSpec(memory_space=pl.ANY)
    smem = pl.BlockSpec(memory_space=pltpu.SMEM)
    vmem = pl.BlockSpec(memory_space=pltpu.VMEM)
    dma = pltpu.SemaphoreType.DMA
    brick = jax.ShapeDtypeStruct((CX, CY, CZ), F32)
    return pl.pallas_call(
        hall_kernel,
        out_shape=(brick, brick, jax.ShapeDtypeStruct((ROWS, TARGETS * DB), F32)),
        in_specs=[smem, smem, vmem, vmem] + [any_space] * 5,
        out_specs=(any_space, any_space, vmem),
        scratch_shapes=[
            pltpu.VMEM((CX + 2, PADROWS, CZ), F32),
            pltpu.VMEM((CX + 2, PADROWS, CZ), F32),
            pltpu.VMEM((CX, CY, CZ), jnp.int32),
            pltpu.VMEM((3, CX, CY, CZ), F32),
            pltpu.VMEM((STEPS, 2, CX, CZ), F32),
            pltpu.VMEM((STEPS, CY, CZ), F32),
            pltpu.VMEM((STEPS, 2, CY, CZ), F32),
            pltpu.VMEM((STEPS, 2, CX, CZ), F32),
            pltpu.VMEM((STEPS, 2, CY, CZ), F32),
            pltpu.VMEM((SLOT, CX * CY), BF16),
            pltpu.VMEM((SLOT, CZ), F32),
            pltpu.VMEM((2, CX * CY, CZ), BF16),
            pltpu.VMEM((8, SLOT), F32),
            pltpu.VMEM((NY_DEV, 8, SLOT), F32),
            pltpu.VMEM((8, SLOT), F32),
            pltpu.VMEM((NY_DEV, 8, SLOT), F32),
            pltpu.VMEM((BLOCKS, 48, PB), F32),
            pltpu.VMEM((64, ENTRIES // 2 * PB), BF16),
            pltpu.VMEM((16, ENTRIES // 2 * PB), BF16),
            pltpu.VMEM((ENTRIES + 1, PB, DB), BF16),
            pltpu.VMEM((BLOCKS, TW + MAXOFF, PB), F32),
            pltpu.VMEM((PAIRS + 1, TW, DB), F32),
            pltpu.VMEM((8, PB), jnp.int32),
            pltpu.SMEM((8, PB), jnp.int32),
            pltpu.VMEM((HOLD, BLOCKS * PB), BF16),
            pltpu.VMEM((TARGETS, 4, 4, 2, ROWS, DB), F32),
            pltpu.VMEM((TARGETS, 4, 4, ROWS, DB), F32),
            pltpu.VMEM((2, 4, 4, 4, ROWS, DB), F32),
            pltpu.VMEM((2, 4, 4, ROWS, DB), F32),
            pltpu.VMEM((2, 3, 2, 2, 4, ROWS, DB), F32),
            pltpu.VMEM((2, 3, 4, ROWS, DB), F32),
            pltpu.VMEM((32, DB), F32),
            pltpu.VMEM((OWNERS, 32, DB), F32),
            pltpu.VMEM((8, DB), F32),
            pltpu.VMEM((OWNERS, 8, DB), F32),
            dma((8,)), dma,
            dma((STEPS, 3, 2)), dma((STEPS, 3, 2)),
            dma((2,)), dma((2,)),
            dma((2,)), dma((2,)),
            dma, dma((2,)), dma, dma,
            dma, dma, dma, dma,
        ],
        compiler_params=pltpu.CompilerParams(
            collective_id=0, has_side_effects=True, vmem_limit_bytes=58 * 1024 * 1024),
    )(dirs, delays, dirs, surf_index, history, now, old, code, weights)


def save_kernel(*refs):
    sources, targets, held, sems = refs[:3], refs[3:6], refs[6:9], refs[9]
    pieces = [(i, slice(first, first + CX // 4)) for first in range(0, CX, CX // 4) for i in (0, 1)]
    pieces.append((2, slice(0, ROWS)))
    arrivals, leaves = [], []
    for number, (i, part) in enumerate(pieces):
        arrivals.append(pltpu.make_async_copy(
            sources[i].at[part], held[i].at[part], sems.at[0, number]))
        leaves.append(pltpu.make_async_copy(
            held[i].at[part], targets[i].at[part], sems.at[1, number]))
    for copy in arrivals:
        copy.start()
    for arrival, leave in zip(arrivals, leaves):
        arrival.wait()
        leave.start()
    for copy in leaves:
        copy.wait()


def save(arrays):
    any_space = pl.BlockSpec(memory_space=pl.ANY)
    return pl.pallas_call(
        save_kernel,
        out_shape=tuple(jax.ShapeDtypeStruct(a.shape, a.dtype) for a in arrays),
        in_specs=[any_space] * 3,
        out_specs=(any_space,) * 3,
        scratch_shapes=[pltpu.VMEM(a.shape, a.dtype) for a in arrays]
        + [pltpu.SemaphoreType.DMA((2, 9))],
    )(*arrays)


def shards(pressure_now, pressure_old, cell_code, surf_index, history, dir_slot, delay, weights):
    flat_weights = weights.reshape(BLOCKS * K_DEV, PB, DB)
    return save(hall(
        dir_slot.T, delay.T, surf_index, pressure_now, pressure_old, cell_code, history,
        flat_weights))


def solution(mesh):
    return jax.shard_map(
        shards,
        mesh=mesh,
        in_specs=(
            P("gx", "gy", "gz"),
            P("gx", "gy", "gz"),
            P("gx", "gy", "gz"),
            P(("gx", "gz"), "gy"),
            P(None, ("gx", "gz")),
            P(("gx", "gz"), "gy"),
            P(("gx", "gz"), "gy"),
            P(("gx", "gz"), "gy", None, None),
        ),
        out_specs=(P("gx", "gy", "gz"), P("gx", "gy", "gz"), P(("gx", "gz"), "gy")),
        check_vma=False,
    )
```

```python
import functools

import jax
import jax.numpy as jnp
import numpy as np
from jax import lax
from jax.experimental import pallas as pl
from jax.experimental.pallas import tpu as pltpu
from jax.sharding import PartitionSpec as P

MESH = pl.DeviceIdType.MESH
F32 = jnp.float32
BF16 = jnp.bfloat16

STEPS = 4
CX, CY, CZ = 32, 32, 128
SLOT = 512
TW = 512
MAXOFF = 32
HOLD = 540
PB = 128
DB = 128
K_DEV = 6
BLOCKS = 16
ENTRIES = K_DEV * BLOCKS
PAIRS = ENTRIES // 2 + 4
TARGETS = 8
OWNERS = 32
ROWS = 16
NX_DEV, NY_DEV, NZ_DEV = 8, 4, 4
LOW, HIGH = 8, 40
PADROWS = 48


def coefficient_table():
    speeds = np.array([0.32, 0.26, 0.19, 0.11], np.float32).astype(np.float64)
    damping = np.array([0.0, 0.02, 0.08, 0.3], np.float32).astype(np.float64)
    here = (2.0 - 6.0 * speeds) / (1.0 + damping)
    before = -(1.0 - damping) / (1.0 + damping)
    around = speeds / (1.0 + damping)
    return [[float(np.float32(v)) for v in row] for row in (here, before, around)]


COEFFICIENTS = coefficient_table()


def hall_kernel(
    dir_ref, delay_ref, dirs_ref, surf_ref, hist_ref, now_ref, old_ref, code_ref, w_ref,
    next_ref, prev_ref, far_ref,
    field_a, field_b, codes, coef, ystage, zstage, xrecv, yrecv, zrecv,
    onehot, cellmask, rounded, samp_send, samp_all, last_send, last_all, spad, lhs, last_lhs, wv,
    signal, trail, table, order, hist, part, core_recv, sums, totals, ring1, ring2, corr_out, corr_in, last_out, last_in,
    load_sem, idle_sem, halo_send, halo_recv, samp_ssem, samp_rsem,
    core_ssem, core_rsem, ring_send, ring_recv, direct_send, direct_recv, corr_ssem, corr_rsem, last_ssem, last_rsem,
):
    fields = (field_a, field_b)
    gx, gy, gz = lax.axis_index("gx"), lax.axis_index("gy"), lax.axis_index("gz")
    y, z_hi = gx // 2, lax.rem(gx, 2)
    z_lo, core = gz // 2, lax.rem(gz, 2)
    z = z_hi * 2 + z_lo
    group = gx * 4 + gz
    is_owner = group == OWNERS - 1

    def place(yy, zz):
        return (yy * 2 + zz // 2, gy, lax.rem(zz, 2) * 2 + core)

    def ring_neighbour(axis, offset):
        if axis == "z":
            return place(y, lax.rem(z + offset, 4))
        return place(lax.rem(y + offset, 4), z)

    sibling = (gx, gy, z_lo * 2 + 1 - core)
    owner = (NX_DEV - 1, gy, NZ_DEV - 1)
    coords = (gx, gy, gz)
    extents = (NX_DEV, NY_DEV, NZ_DEV)

    def beside(axis, side):
        moved = list(coords)
        moved[axis] = coords[axis] + (1 if side else -1)
        return tuple(moved)

    def exists(axis, side):
        return coords[axis] < extents[axis] - 1 if side else coords[axis] > 0

    barrier = pltpu.get_barrier_semaphore()

    def greet(device):
        pl.semaphore_signal(barrier, inc=1, device_id=device, device_id_type=MESH)

    expected = jnp.int32(10)
    for axis in range(3):
        for side in range(2):
            @pl.when(exists(axis, side))
            def _():
                greet(beside(axis, side))
            expected = expected + exists(axis, side).astype(jnp.int32)
    greet(sibling)
    for axis in ("y", "z"):
        for offset in (1, 2, 3):
            greet(ring_neighbour(axis, offset))
    for offset in range(1, NY_DEV):
        greet((gx, lax.rem(gy + offset, NY_DEV), gz))

    @pl.when(is_owner)
    def _():
        def greet_one(member, carry):
            greet((member // 4, gy, lax.rem(member, 4)))
            return carry
        lax.fori_loop(0, OWNERS - 1, greet_one, 0)

    expected = expected + jnp.where(is_owner, 0, 1)

    loads = [
        pltpu.make_async_copy(now_ref, field_a.at[pl.ds(1, CX), pl.ds(LOW, CY)], load_sem.at[0]),
        pltpu.make_async_copy(hist_ref, hist, load_sem.at[3]),
        pltpu.make_async_copy(w_ref, wv.at[pl.ds(0, ENTRIES)], load_sem.at[4]),
        pltpu.make_async_copy(code_ref, codes, load_sem.at[2]),
        pltpu.make_async_copy(old_ref, field_b.at[pl.ds(1, CX), pl.ds(LOW, CY)], load_sem.at[1]),
    ]
    for load in loads:
        load.start()

    lane = lax.broadcasted_iota(jnp.int32, (CY, CZ), 1)
    zero_plane = jnp.zeros((CY, CZ), F32)

    def over_planes(body, init, unroll=16):
        def chunk(i, carry):
            return body([i * unroll + u for u in range(unroll)], carry)
        return lax.fori_loop(0, CX // unroll, chunk, init)

    def take_faces(step, xs, planes, held):
        for x, plane in zip(xs, planes):
            mine = jnp.logical_or(lane == 2 * x, lane == lax.rem(2 * x + CZ - 1, CZ))
            held = jnp.where(mine, pltpu.roll(plane, 2 * x, 1), held)
        for x, plane in zip(xs, planes):
            ystage[step, 0, pl.ds(x, 1), :] = plane[0:1, :]
            ystage[step, 1, pl.ds(x, 1), :] = plane[CY - 1:CY, :]
        return held

    def halo_copy(step, axis, side):
        current = step % 2
        if axis == 0:
            source = fields[current].at[CX if side else 1, pl.ds(LOW, CY)]
            target = xrecv.at[step, 1 - side]
        elif axis == 1:
            source, target = ystage.at[step, side], yrecv.at[step, 1 - side]
        else:
            source, target = zstage.at[step], zrecv.at[step, 1 - side]
        return pltpu.make_async_remote_copy(
            src_ref=source, dst_ref=target,
            send_sem=halo_send.at[step, axis, side],
            recv_sem=halo_recv.at[step, axis, 1 - side],
            device_id=beside(axis, side), device_id_type=MESH,
        )

    def halo_start(step):
        for axis in range(3):
            for side in range(2):
                @pl.when(exists(axis, side))
                def _():
                    halo_copy(step, axis, side).start()

    def halo_wait_send(step, axes=(0, 1, 2)):
        for axis in axes:
            for side in range(2):
                @pl.when(exists(axis, side))
                def _():
                    halo_copy(step, axis, side).wait_send()

    def halo_wait_recv(step, axes):
        for axis in axes:
            buffer = (xrecv, yrecv, zrecv)[axis]
            for side in range(2):
                @pl.when(exists(axis, side))
                def _():
                    halo_copy(step, axis, 1 - side).wait_recv()
                @pl.when(jnp.logical_not(exists(axis, side)))
                def _():
                    buffer[step, side] = zero_plane

    dirs = dirs_ref[...]
    targets = jnp.concatenate(
        [dirs[k:k + 1, :] for k in range(K_DEV)]
        + [jnp.full((1, PB - ENTRIES), -1, jnp.int32)], axis=1)
    targets = jnp.where(targets >= 0, targets, TARGETS).astype(F32)
    by_lane = jnp.broadcast_to(targets, (PB, PB))
    by_row = by_lane.T
    lanes = lax.broadcasted_iota(jnp.int32, (PB, PB), 1).astype(F32)
    rows = lax.broadcasted_iota(jnp.int32, (PB, PB), 0).astype(F32)

    def count(mask, axis):
        return jnp.sum(jnp.where(mask, 1.0, 0.0), axis=axis, keepdims=True)

    def even(amount):
        return 2.0 * jnp.floor(0.5 * (amount + 1.0))

    member = by_row == lanes
    along_lanes = count(member, 0)
    along_rows = count(by_lane == rows, 1)
    first_lanes = jnp.sum(jnp.where(rows < lanes, even(along_rows), 0.0), axis=0, keepdims=True)
    first_rows = jnp.sum(jnp.where(lanes < rows, even(along_lanes), 0.0), axis=1, keepdims=True)
    before = count(jnp.logical_and(by_lane == by_row, lanes < rows), 1)
    slot = before + jnp.sum(jnp.where(member, first_lanes, 0.0), axis=1, keepdims=True)
    taken = jnp.logical_and(slot == lanes, by_row < TARGETS)
    sequence = ENTRIES + jnp.sum(jnp.where(taken, rows - ENTRIES, 0.0), axis=0, keepdims=True)
    ends = jnp.where(along_lanes > 0, 0.5 * (first_lanes + even(along_lanes)), 0.0)
    opens = count(
        jnp.logical_and(jnp.logical_and(0.5 * first_rows == lanes, along_rows > 0), rows < TARGETS), 0)
    table[0:1, :] = sequence.astype(jnp.int32)
    table[1:2, :] = ends.astype(jnp.int32)
    table[2:3, :] = opens.astype(jnp.int32)
    table[3:8, :] = jnp.zeros((5, PB), jnp.int32)
    order_load = pltpu.make_async_copy(table, order, load_sem.at[7])
    order_load.start()

    def core_copy(half):
        return pltpu.make_async_remote_copy(
            src_ref=part.at[pl.ds(half * 4, 4), :, :, 1 - core],
            dst_ref=core_recv.at[pl.ds(half * 4, 4)],
            send_sem=core_ssem.at[half], recv_sem=core_rsem.at[half],
            device_id=sibling, device_id_type=MESH,
        )

    samp_send[...] = jnp.zeros_like(samp_send)
    spad[...] = jnp.zeros_like(spad)
    trail[0] = jnp.zeros((TW, DB), F32)
    wv[ENTRIES] = jnp.zeros((PB, DB), BF16)
    for block in range(BLOCKS):
        signal[block, HOLD:, :] = jnp.zeros((TW + MAXOFF - HOLD, PB), F32)

    loads[0].wait()

    def first_faces(xs, carry):
        return take_faces(0, xs, [field_a[x + 1, LOW:HIGH, :] for x in xs], carry)

    zstage[0] = over_planes(first_faces, zero_plane)

    pl.semaphore_wait(barrier, expected)
    halo_start(0)

    loads[1].wait()

    for block in range(BLOCKS):
        signal[block, :HOLD, :] = hist[:, block * PB:(block + 1) * PB].astype(F32)
    order_load.wait()
    loads[2].wait()


    def far_pair(p):
        windows, blocks = [], []
        for u in range(2):
            entry = jnp.clip(order[0, 2 * p + u], 0, ENTRIES)
            k = jnp.minimum(lax.shift_right_logical(entry, 4), K_DEV - 1)
            block = jnp.bitwise_and(entry, BLOCKS - 1)
            windows.append(signal[block, pl.ds(delay_ref[k, block], TW), :].astype(BF16))
            blocks.append(wv[jnp.where(entry < ENTRIES, block * K_DEV + k, ENTRIES)])
        term = jnp.dot(
            jnp.concatenate(windows, axis=1), jnp.concatenate(blocks, axis=0),
            preferred_element_type=F32)
        trail[p + 1] = term + trail[jnp.where(order[2, p] > 0, 0, p)]

    def far_pairs(first, amount, unroll):
        def chunk(i, carry):
            for u in range(unroll):
                far_pair(first + i * unroll + u)
            return carry
        lax.fori_loop(0, amount // unroll, chunk, 0)

    def core_start():
        for half in range(2):
            for j in range(half * 4, half * 4 + 4):
                end = jnp.clip(order[1, j], 0, PAIRS)
                for quarter in range(4):
                    found = trail[end, quarter * 128:(quarter + 1) * 128, :]
                    part[j, quarter] = found.reshape(4, 2, ROWS, DB)
            core_copy(half).start()

    loads[3].wait()

    def plane_coefficients(xs, carry):
        for x in xs:
            code = codes[x]
            for index, values in enumerate(COEFFICIENTS):
                coef[index, x] = jnp.where(
                    code == 0, values[0],
                    jnp.where(code == 1, values[1], jnp.where(code == 2, values[2], values[3])),
                ).astype(F32)
        return carry

    over_planes(plane_coefficients, 0)
    slot_lane = lax.broadcasted_iota(jnp.int32, (PB, PB), 1)
    for i in range(SLOT // PB):
        slots = slice(i * PB, (i + 1) * PB)
        cell = jnp.broadcast_to(surf_ref[:, slots].astype(F32), (PB, PB)).T.astype(jnp.int32)
        cell_row = lax.shift_right_arithmetic(cell, 7)
        cellmask[slots, :] = jnp.where(
            slot_lane == jnp.bitwise_and(cell, CZ - 1), 1.0, 0.0)
        for q in range(CX * CY // PB):
            onehot[slots, q * PB:(q + 1) * PB] = jnp.where(
                slot_lane + q * PB == cell_row, 1.0, 0.0).astype(BF16)
    loads[4].wait()

    def leap(step):
        here_ref, other_ref = fields[step % 2], fields[1 - step % 2]
        last = step == STEPS - 1
        halo_wait_recv(step, (1, 2))

        def y_rows(xs, carry):
            rows = [(yrecv[step, 0, pl.ds(x, 1), :], yrecv[step, 1, pl.ds(x, 1), :]) for x in xs]
            for x, (low, high) in zip(xs, rows):
                here_ref[x + 1, LOW - 1:LOW, :] = low
                here_ref[x + 1, HIGH:HIGH + 1, :] = high
            return carry

        over_planes(y_rows, 0, 16)
        z_halo = jnp.where(
            jnp.bitwise_and(lane, 1) == 0,
            pltpu.roll(zrecv[step, 0], 1, 1), pltpu.roll(zrecv[step, 1], CZ - 1, 1))
        ends = jnp.logical_or(lane == 0, lane == CZ - 1)

        def plane_step(xs, carry):
            planes = []
            for x in xs:
                here = here_ref[x + 1, LOW:HIGH, :]
                around = here_ref[x, LOW:HIGH, :] + here_ref[x + 2, LOW:HIGH, :]
                around = around + (
                    here_ref[x + 1, LOW - 1:HIGH - 1, :] + here_ref[x + 1, LOW + 1:HIGH + 1, :])
                beside_z = (jnp.where(lane == 0, 0.0, pltpu.roll(here, 1, 1))
                            + jnp.where(lane == CZ - 1, 0.0, pltpu.roll(here, CZ - 1, 1)))
                outside = pltpu.roll(z_halo, lax.rem(2 * (CZ - x), CZ), 1)
                around = around + (beside_z + jnp.where(ends, outside, 0.0))
                before = other_ref[x + 1, LOW:HIGH, :]
                planes.append(coef[0, x] * here + coef[1, x] * before + coef[2, x] * around)
            for x, new in zip(xs, planes):
                other_ref[x + 1, LOW:HIGH, :] = new
                rounded[step % 2, pl.ds(x * CY if isinstance(x, int) else pl.multiple_of(x * CY, CY), CY), :] = new.astype(BF16)
            if last:
                return carry
            return take_faces(step + 1, xs, planes, carry)

        def inner(i, carry):
            return plane_step([1 + i * 15 + u for u in range(15)], carry)

        carry = lax.fori_loop(
            0, (CX - 2) // 15, inner, 0 if last else zero_plane)
        halo_wait_recv(step, (0,))
        if step > 0:
            halo_wait_send(step - 1, (0,))
        here_ref[0, LOW:HIGH, :] = xrecv[step, 0]
        here_ref[CX + 1, LOW:HIGH, :] = xrecv[step, 1]
        carry = plane_step([0, CX - 1], carry)
        if not last:
            zstage[step + 1] = carry
            halo_start(step + 1)

    def sample(step):
        picked = jnp.dot(onehot[...], rounded[step % 2], preferred_element_type=F32)
        values = lax.dot_general(
            jnp.ones((8, CZ), BF16), (picked * cellmask[...]).astype(BF16),
            (((1,), (1,)), ((), ())), preferred_element_type=F32)
        if step < STEPS - 1:
            samp_send[4 + step:5 + step, :] = values[0:1, :]
        else:
            last_send[...] = values

    def wait_all_recv(ref, sem):
        pltpu.make_async_remote_copy(
            src_ref=ref, dst_ref=ref, send_sem=idle_sem, recv_sem=sem,
            device_id=sibling, device_id_type=MESH).wait_recv()

    def wait_all_send(ref, sem):
        pltpu.make_async_remote_copy(
            src_ref=ref, dst_ref=ref, send_sem=sem, recv_sem=idle_sem,
            device_id=sibling, device_id_type=MESH).wait_send()

    axes = (("z", "y"), ("y", "z"))

    def index_on(axis):
        return z if axis == "z" else y

    def ring_copy(half, kind, way):
        axis = axes[half][0]
        place_now = index_on(axis)
        step_to = 1 if way == 0 else 3
        chunk = lax.rem(place_now + (2 if kind == 0 else step_to), 4)
        part_now = pl.ds(0 if (kind == 1) == (way == 1) else 2, 2)
        return pltpu.make_async_remote_copy(
            src_ref=sums.at[half, chunk, part_now], dst_ref=ring1.at[half, kind, way],
            send_sem=ring_send, recv_sem=ring_recv.at[0 if kind == 0 else 1],
            device_id=ring_neighbour(axis, step_to), device_id_type=MESH,
        )

    def direct_copy(half, offset):
        axis = axes[half][1]
        return pltpu.make_async_remote_copy(
            src_ref=totals.at[half, lax.rem(index_on(axis) + offset, 4)],
            dst_ref=ring2.at[half, offset - 1],
            send_sem=direct_send, recv_sem=direct_recv,
            device_id=ring_neighbour(axis, offset), device_id_type=MESH,
        )

    def core_finish(half):
        core_copy(half).wait_recv()

        for yy in range(4):
            for zz in range(4):
                total = (part[half * 4:half * 4 + 4, yy, zz, core]
                         + core_recv[half * 4:half * 4 + 4, yy, zz])
                if half == 0:
                    sums[0, zz, yy] = total
                else:
                    sums[1, yy, zz] = total

    def ring_begin(half):
        for kind in (0, 1):
            for way in (0, 1):
                ring_copy(half, kind, way).start()

    def ring_forward():
        wait_all_recv(ring1.at[:, 0], ring_recv.at[0])
        for half in range(2):
            place_now = index_on(axes[half][0])
            for way in (0, 1):
                chunk = lax.rem(place_now + (1 if way == 0 else 3), 4)
                first = 0 if way == 0 else 2
                sums[half, chunk, first:first + 2] = (
                    sums[half, chunk, first:first + 2] + ring1[half, 0, way])
                ring_copy(half, 2, way).start()

    def ring_end():
        wait_all_recv(ring1.at[:, pl.ds(1, 2)], ring_recv.at[1])
        for half in range(2):
            place_now = index_on(axes[half][0])
            totals[half, 0:2] = (
                sums[half, place_now, 0:2] + (ring1[half, 2, 0] + ring1[half, 1, 1]))
            totals[half, 2:4] = (
                sums[half, place_now, 2:4] + (ring1[half, 1, 0] + ring1[half, 2, 1]))
            for offset in (2, 1, 3):
                direct_copy(half, offset).start()

    def direct_end():
        wait_all_recv(ring2, direct_recv)
        for half in range(2):
            result = totals[half, index_on(axes[half][1])]
            result = result + (ring2[half, 0] + (ring2[half, 1] + ring2[half, 2]))
            for j in range(4):
                columns = slice((half * 4 + j) * DB, (half * 4 + j + 1) * DB)
                far_ref[:, columns] = result[j]

    def samp_copy(last, offset):
        source, target = (last_send, last_all) if last else (samp_send, samp_all)
        return pltpu.make_async_remote_copy(
            src_ref=source, dst_ref=target.at[gy],
            send_sem=samp_ssem.at[last], recv_sem=samp_rsem.at[last],
            device_id=(gx, lax.rem(gy + offset, NY_DEV), gz), device_id_type=MESH,
        )

    def samp_start(last):
        for offset in range(1, NY_DEV):
            samp_copy(last, offset).start()
        if last:
            last_all[gy] = last_send[...]
        else:
            samp_all[gy] = samp_send[...]

    def samp_wait(last):
        wait_all_recv((last_all if last else samp_all).at[pl.ds(0, NY_DEV - 1)], samp_rsem.at[last])

    row = lax.broadcasted_iota(jnp.int32, (8, PB), 0)
    width = 4 * K_DEV * PB

    def entry_rows(i, carry):
        held = []
        for block in [i * 4 + u for u in range(4)]:
            for entry in range(K_DEV):
                offset = delay_ref[entry, block]
                target = dir_ref[entry, block]
                early = spad[block, pl.ds(offset + 4, 8), :]
                late = spad[block, pl.ds(offset, 8), :]
                pair = jnp.where(row < 4, early, late)
                pieces = []
                for k in range(TARGETS // 2):
                    wanted = jnp.where(row < 4, 2 * k, 2 * k + 1)
                    pieces.append(jnp.where(wanted == target, pair, 0.0))
                held.append(jnp.concatenate(pieces, axis=0).astype(BF16))
        part_rows = pl.ds(pl.multiple_of((i // 2) * 32, 32), 32)
        columns = pl.ds(pl.multiple_of(lax.rem(i, 2) * width, width), width)
        lhs[part_rows, columns] = jnp.concatenate(held, axis=1)
        return carry

    def last_rows():
        for brick in range(NY_DEV // 2):
            rows = []
            for part_of in (brick, brick + NY_DEV // 2):
                held = []
                for i in range(SLOT // PB):
                    block = part_of * (SLOT // PB) + i
                    samples = last_all[part_of, :, i * PB:(i + 1) * PB]
                    for entry in range(K_DEV):
                        target = jnp.where(
                            delay_ref[entry, block] == MAXOFF, dir_ref[entry, block], -1)
                        held.append(jnp.where(row == target, samples, 0.0))
                rows.append(jnp.concatenate(held, axis=1))
            last_lhs[:, brick * width:(brick + 1) * width] = (
                jnp.concatenate(rows, axis=0).astype(BF16))

    def times_weights(rows_ref):
        half = ENTRIES // 2
        beside_each_other = jnp.concatenate(
            [wv[:half].reshape(half * PB, DB), wv[half:ENTRIES].reshape(half * PB, DB)], axis=1)
        product = jnp.dot(rows_ref[...], beside_each_other, preferred_element_type=F32)
        count_rows = product.shape[0] // 2
        return product[:count_rows, :DB] + product[count_rows:, DB:]

    def corr_copy(last, member):
        source, target = (last_out, last_in) if last else (corr_out, corr_in)
        return pltpu.make_async_remote_copy(
            src_ref=source, dst_ref=target.at[member],
            send_sem=last_ssem if last else corr_ssem,
            recv_sem=last_rsem if last else corr_rsem,
            device_id=owner, device_id_type=MESH,
        )

    def corr_start(last):
        @pl.when(jnp.logical_not(is_owner))
        def _():
            corr_copy(last, group).start()

    far_pairs(0, 26, 26)
    leap(0)
    far_pairs(26, 26, 26)
    core_start()
    halo_wait_send(0, (1, 2))
    leap(1)
    sample(0)
    sample(1)
    for half in range(2):
        core_finish(half)
        ring_begin(half)
    halo_wait_send(1, (1, 2))
    leap(2)
    save_prev = pltpu.make_async_copy(
        field_b.at[pl.ds(1, CX), pl.ds(LOW, CY)], prev_ref, load_sem.at[5])
    save_prev.start()
    sample(2)
    samp_start(0)
    ring_forward()
    halo_wait_send(2, (1, 2))
    leap(3)
    sample(3)
    samp_start(1)
    save_next = pltpu.make_async_copy(
        field_a.at[pl.ds(1, CX), pl.ds(LOW, CY)], next_ref, load_sem.at[6])
    save_next.start()
    ring_end()
    halo_wait_send(STEPS - 1)
    for half in range(2):
        core_copy(half).wait_send()
    wait_all_send(ring1, ring_send)
    wait_all_send(samp_all.at[pl.ds(0, NY_DEV - 1)], samp_ssem.at[0])
    samp_wait(0)
    for brick in range(NY_DEV):
        for i in range(SLOT // PB):
            spad[brick * (SLOT // PB) + i, 32:40, :] = samp_all[brick, :, i * PB:(i + 1) * PB]
    lax.fori_loop(0, BLOCKS // 4, entry_rows, 0)
    corr_out[...] = times_weights(lhs)
    corr_start(0)
    samp_wait(1)
    last_rows()
    last_out[...] = times_weights(last_lhs)
    corr_start(1)
    direct_end()

    @pl.when(is_owner)
    def _():
        def arrivals(last):
            held, sem = (last_in, last_rsem) if last else (corr_in, corr_rsem)
            wait_all_recv(held.at[pl.ds(0, OWNERS - 1)], sem)

        arrivals(0)
        total = corr_out[...]
        for member in range(OWNERS - 1):
            total = total + corr_in[member]
        for j in range(TARGETS):
            piece = total[(j // 2) * 8:(j // 2) * 8 + 8, :]
            if j % 2 == 0:
                piece = pltpu.roll(piece, 4, 0)
            columns = slice(j * DB, (j + 1) * DB)
            far_ref[8:16, columns] = far_ref[8:16, columns] + jnp.where(row >= 4, piece, 0.0)
        arrivals(1)
        total = last_out[...]
        for member in range(OWNERS - 1):
            total = total + last_in[member]
        for j in range(TARGETS):
            columns = slice(j * DB, (j + 1) * DB)
            far_ref[15:16, columns] = far_ref[15:16, columns] + total[j:j + 1, :]

    wait_all_send(ring2, direct_send)
    wait_all_send(last_all.at[pl.ds(0, NY_DEV - 1)], samp_ssem.at[1])

    @pl.when(jnp.logical_not(is_owner))
    def _():
        corr_copy(0, group).wait_send()
        corr_copy(1, group).wait_send()

    save_prev.wait()
    save_next.wait()


def hall(dirs, delays, surf_index, now, old, code, history, weights):
    any_space = pl.BlockSpec(memory_space=pl.ANY)
    smem = pl.BlockSpec(memory_space=pltpu.SMEM)
    vmem = pl.BlockSpec(memory_space=pltpu.VMEM)
    dma = pltpu.SemaphoreType.DMA
    brick = jax.ShapeDtypeStruct((CX, CY, CZ), F32)
    return pl.pallas_call(
        hall_kernel,
        out_shape=(brick, brick, jax.ShapeDtypeStruct((ROWS, TARGETS * DB), F32)),
        in_specs=[smem, smem, vmem, vmem] + [any_space] * 5,
        out_specs=(any_space, any_space, vmem),
        scratch_shapes=[
            pltpu.VMEM((CX + 2, PADROWS, CZ), F32),
            pltpu.VMEM((CX + 2, PADROWS, CZ), F32),
            pltpu.VMEM((CX, CY, CZ), jnp.int32),
            pltpu.VMEM((3, CX, CY, CZ), F32),
            pltpu.VMEM((STEPS, 2, CX, CZ), F32),
            pltpu.VMEM((STEPS, CY, CZ), F32),
            pltpu.VMEM((STEPS, 2, CY, CZ), F32),
            pltpu.VMEM((STEPS, 2, CX, CZ), F32),
            pltpu.VMEM((STEPS, 2, CY, CZ), F32),
            pltpu.VMEM((SLOT, CX * CY), BF16),
            pltpu.VMEM((SLOT, CZ), F32),
            pltpu.VMEM((2, CX * CY, CZ), BF16),
            pltpu.VMEM((8, SLOT), F32),
            pltpu.VMEM((NY_DEV, 8, SLOT), F32),
            pltpu.VMEM((8, SLOT), F32),
            pltpu.VMEM((NY_DEV, 8, SLOT), F32),
            pltpu.VMEM((BLOCKS, 48, PB), F32),
            pltpu.VMEM((64, ENTRIES // 2 * PB), BF16),
            pltpu.VMEM((16, ENTRIES // 2 * PB), BF16),
            pltpu.VMEM((ENTRIES + 1, PB, DB), BF16),
            pltpu.VMEM((BLOCKS, TW + MAXOFF, PB), F32),
            pltpu.VMEM((PAIRS + 1, TW, DB), F32),
            pltpu.VMEM((8, PB), jnp.int32),
            pltpu.SMEM((8, PB), jnp.int32),
            pltpu.VMEM((HOLD, BLOCKS * PB), BF16),
            pltpu.VMEM((TARGETS, 4, 4, 2, ROWS, DB), F32),
            pltpu.VMEM((TARGETS, 4, 4, ROWS, DB), F32),
            pltpu.VMEM((2, 4, 4, 4, ROWS, DB), F32),
            pltpu.VMEM((2, 4, 4, ROWS, DB), F32),
            pltpu.VMEM((2, 3, 2, 2, 4, ROWS, DB), F32),
            pltpu.VMEM((2, 3, 4, ROWS, DB), F32),
            pltpu.VMEM((32, DB), F32),
            pltpu.VMEM((OWNERS, 32, DB), F32),
            pltpu.VMEM((8, DB), F32),
            pltpu.VMEM((OWNERS, 8, DB), F32),
            dma((8,)), dma,
            dma((STEPS, 3, 2)), dma((STEPS, 3, 2)),
            dma((2,)), dma((2,)),
            dma((2,)), dma((2,)),
            dma, dma((2,)), dma, dma,
            dma, dma, dma, dma,
        ],
        compiler_params=pltpu.CompilerParams(
            collective_id=0, has_side_effects=True, vmem_limit_bytes=58 * 1024 * 1024),
    )(dirs, delays, dirs, surf_index, history, now, old, code, weights)


def save_kernel(*refs):
    sources, targets, held, sems = refs[:3], refs[3:6], refs[6:9], refs[9]
    pieces = [(i, slice(first, first + CX // 4)) for first in range(0, CX, CX // 4) for i in (0, 1)]
    pieces.append((2, slice(0, ROWS)))
    arrivals, leaves = [], []
    for number, (i, part) in enumerate(pieces):
        arrivals.append(pltpu.make_async_copy(
            sources[i].at[part], held[i].at[part], sems.at[0, number]))
        leaves.append(pltpu.make_async_copy(
            held[i].at[part], targets[i].at[part], sems.at[1, number]))
    for copy in arrivals:
        copy.start()
    for arrival, leave in zip(arrivals, leaves):
        arrival.wait()
        leave.start()
    for copy in leaves:
        copy.wait()


def save(arrays):
    any_space = pl.BlockSpec(memory_space=pl.ANY)
    return pl.pallas_call(
        save_kernel,
        out_shape=tuple(jax.ShapeDtypeStruct(a.shape, a.dtype) for a in arrays),
        in_specs=[any_space] * 3,
        out_specs=(any_space,) * 3,
        scratch_shapes=[pltpu.VMEM(a.shape, a.dtype) for a in arrays]
        + [pltpu.SemaphoreType.DMA((2, 9))],
    )(*arrays)


def shards(pressure_now, pressure_old, cell_code, surf_index, history, dir_slot, delay, weights):
    flat_weights = weights.reshape(BLOCKS * K_DEV, PB, DB)
    return save(hall(
        dir_slot.T, delay.T, surf_index, pressure_now, pressure_old, cell_code, history,
        flat_weights))


def solution(mesh):
    return jax.shard_map(
        shards,
        mesh=mesh,
        in_specs=(
            P("gx", "gy", "gz"),
            P("gx", "gy", "gz"),
            P("gx", "gy", "gz"),
            P(("gx", "gz"), "gy"),
            P(None, ("gx", "gz")),
            P(("gx", "gz"), "gy"),
            P(("gx", "gz"), "gy"),
            P(("gx", "gz"), "gy", None, None),
        ),
        out_specs=(P("gx", "gy", "gz"), P("gx", "gy", "gz"), P(("gx", "gz"), "gy")),
        check_vma=False,
    )
```

```python
import functools

import jax
import jax.numpy as jnp
import numpy as np
from jax import lax
from jax.experimental import pallas as pl
from jax.experimental.pallas import tpu as pltpu
from jax.sharding import PartitionSpec as P

MESH = pl.DeviceIdType.MESH
F32 = jnp.float32
BF16 = jnp.bfloat16

STEPS = 4
CX, CY, CZ = 32, 32, 128
SLOT = 512
TW = 512
MAXOFF = 32
HOLD = 540
PB = 128
DB = 128
K_DEV = 6
BLOCKS = 16
ENTRIES = K_DEV * BLOCKS
PAIRS = ENTRIES // 2 + 4
TARGETS = 8
OWNERS = 32
ROWS = 16
NX_DEV, NY_DEV, NZ_DEV = 8, 4, 4
LOW, HIGH = 8, 40
PADROWS = 48


def coefficient_table():
    speeds = np.array([0.32, 0.26, 0.19, 0.11], np.float32).astype(np.float64)
    damping = np.array([0.0, 0.02, 0.08, 0.3], np.float32).astype(np.float64)
    here = (2.0 - 6.0 * speeds) / (1.0 + damping)
    before = -(1.0 - damping) / (1.0 + damping)
    around = speeds / (1.0 + damping)
    return [[float(np.float32(v)) for v in row] for row in (here, before, around)]


COEFFICIENTS = coefficient_table()


def hall_kernel(
    dir_ref, delay_ref, dirs_ref, surf_ref, hist_ref, now_ref, old_ref, code_ref, w_ref,
    next_ref, prev_ref, far_ref,
    field_a, field_b, codes, coef, ystage, zstage, xrecv, yrecv, zrecv,
    onehot, cellmask, rounded, samp_send, samp_all, last_send, last_all, spad, lhs, last_lhs, wv,
    signal, trail, table, order, hist, part, core_recv, sums, totals, ring1, ring2, corr_out, corr_in, last_out, last_in,
    load_sem, idle_sem, halo_send, halo_recv, samp_ssem, samp_rsem,
    core_ssem, core_rsem, ring_send, ring_recv, direct_send, direct_recv, corr_ssem, corr_rsem, last_ssem, last_rsem,
):
    fields = (field_a, field_b)
    gx, gy, gz = lax.axis_index("gx"), lax.axis_index("gy"), lax.axis_index("gz")
    y, z_hi = gx // 2, lax.rem(gx, 2)
    z_lo, core = gz // 2, lax.rem(gz, 2)
    z = z_hi * 2 + z_lo
    group = gx * 4 + gz
    is_owner = group == OWNERS - 1

    def place(yy, zz):
        return (yy * 2 + zz // 2, gy, lax.rem(zz, 2) * 2 + core)

    def ring_neighbour(axis, offset):
        if axis == "z":
            return place(y, lax.rem(z + offset, 4))
        return place(lax.rem(y + offset, 4), z)

    sibling = (gx, gy, z_lo * 2 + 1 - core)
    owner = (NX_DEV - 1, gy, NZ_DEV - 1)
    coords = (gx, gy, gz)
    extents = (NX_DEV, NY_DEV, NZ_DEV)

    def beside(axis, side):
        moved = list(coords)
        moved[axis] = coords[axis] + (1 if side else -1)
        return tuple(moved)

    def exists(axis, side):
        return coords[axis] < extents[axis] - 1 if side else coords[axis] > 0

    barrier = pltpu.get_barrier_semaphore()

    def greet(device):
        pl.semaphore_signal(barrier, inc=1, device_id=device, device_id_type=MESH)

    expected = jnp.int32(10)
    for axis in range(3):
        for side in range(2):
            @pl.when(exists(axis, side))
            def _():
                greet(beside(axis, side))
            expected = expected + exists(axis, side).astype(jnp.int32)
    greet(sibling)
    for axis in ("y", "z"):
        for offset in (1, 2, 3):
            greet(ring_neighbour(axis, offset))
    for offset in range(1, NY_DEV):
        greet((gx, lax.rem(gy + offset, NY_DEV), gz))

    @pl.when(is_owner)
    def _():
        def greet_one(member, carry):
            greet((member // 4, gy, lax.rem(member, 4)))
            return carry
        lax.fori_loop(0, OWNERS - 1, greet_one, 0)

    expected = expected + jnp.where(is_owner, 0, 1)

    loads = [
        pltpu.make_async_copy(now_ref, field_a.at[pl.ds(1, CX), pl.ds(LOW, CY)], load_sem.at[0]),
        pltpu.make_async_copy(hist_ref, hist, load_sem.at[3]),
        pltpu.make_async_copy(w_ref, wv.at[pl.ds(0, ENTRIES)], load_sem.at[4]),
        pltpu.make_async_copy(code_ref, codes, load_sem.at[2]),
        pltpu.make_async_copy(old_ref, field_b.at[pl.ds(1, CX), pl.ds(LOW, CY)], load_sem.at[1]),
    ]
    for load in loads:
        load.start()

    lane = lax.broadcasted_iota(jnp.int32, (CY, CZ), 1)
    zero_plane = jnp.zeros((CY, CZ), F32)

    def over_planes(body, init, unroll=8):
        def chunk(i, carry):
            return body([i * unroll + u for u in range(unroll)], carry)
        return lax.fori_loop(0, CX // unroll, chunk, init)

    def take_faces(step, xs, planes, held):
        for x, plane in zip(xs, planes):
            mine = jnp.logical_or(lane == 2 * x, lane == lax.rem(2 * x + CZ - 1, CZ))
            held = jnp.where(mine, pltpu.roll(plane, 2 * x, 1), held)
        for x, plane in zip(xs, planes):
            ystage[step, 0, pl.ds(x, 1), :] = plane[0:1, :]
            ystage[step, 1, pl.ds(x, 1), :] = plane[CY - 1:CY, :]
        return held

    def halo_copy(step, axis, side):
        current = step % 2
        if axis == 0:
            source = fields[current].at[CX if side else 1, pl.ds(LOW, CY)]
            target = xrecv.at[step, 1 - side]
        elif axis == 1:
            source, target = ystage.at[step, side], yrecv.at[step, 1 - side]
        else:
            source, target = zstage.at[step], zrecv.at[step, 1 - side]
        return pltpu.make_async_remote_copy(
            src_ref=source, dst_ref=target,
            send_sem=halo_send.at[step, axis, side],
            recv_sem=halo_recv.at[step, axis, 1 - side],
            device_id=beside(axis, side), device_id_type=MESH,
        )

    def halo_start(step):
        for axis in range(3):
            for side in range(2):
                @pl.when(exists(axis, side))
                def _():
                    halo_copy(step, axis, side).start()

    def halo_wait_send(step, axes=(0, 1, 2)):
        for axis in axes:
            for side in range(2):
                @pl.when(exists(axis, side))
                def _():
                    halo_copy(step, axis, side).wait_send()

    def halo_wait_recv(step, axes):
        for axis in axes:
            buffer = (xrecv, yrecv, zrecv)[axis]
            for side in range(2):
                @pl.when(exists(axis, side))
                def _():
                    halo_copy(step, axis, 1 - side).wait_recv()
                @pl.when(jnp.logical_not(exists(axis, side)))
                def _():
                    buffer[step, side] = zero_plane

    dirs = dirs_ref[...]
    targets = jnp.concatenate(
        [dirs[k:k + 1, :] for k in range(K_DEV)]
        + [jnp.full((1, PB - ENTRIES), -1, jnp.int32)], axis=1)
    targets = jnp.where(targets >= 0, targets, TARGETS).astype(F32)
    by_lane = jnp.broadcast_to(targets, (PB, PB))
    by_row = by_lane.T
    lanes = lax.broadcasted_iota(jnp.int32, (PB, PB), 1).astype(F32)
    rows = lax.broadcasted_iota(jnp.int32, (PB, PB), 0).astype(F32)

    def count(mask, axis):
        return jnp.sum(jnp.where(mask, 1.0, 0.0), axis=axis, keepdims=True)

    def even(amount):
        return 2.0 * jnp.floor(0.5 * (amount + 1.0))

    member = by_row == lanes
    along_lanes = count(member, 0)
    along_rows = count(by_lane == rows, 1)
    first_lanes = jnp.sum(jnp.where(rows < lanes, even(along_rows), 0.0), axis=0, keepdims=True)
    first_rows = jnp.sum(jnp.where(lanes < rows, even(along_lanes), 0.0), axis=1, keepdims=True)
    before = count(jnp.logical_and(by_lane == by_row, lanes < rows), 1)
    slot = before + jnp.sum(jnp.where(member, first_lanes, 0.0), axis=1, keepdims=True)
    taken = jnp.logical_and(slot == lanes, by_row < TARGETS)
    sequence = ENTRIES + jnp.sum(jnp.where(taken, rows - ENTRIES, 0.0), axis=0, keepdims=True)
    ends = jnp.where(along_lanes > 0, 0.5 * (first_lanes + even(along_lanes)), 0.0)
    opens = count(
        jnp.logical_and(jnp.logical_and(0.5 * first_rows == lanes, along_rows > 0), rows < TARGETS), 0)
    table[0:1, :] = sequence.astype(jnp.int32)
    table[1:2, :] = ends.astype(jnp.int32)
    table[2:3, :] = opens.astype(jnp.int32)
    table[3:8, :] = jnp.zeros((5, PB), jnp.int32)
    order_load = pltpu.make_async_copy(table, order, load_sem.at[7])
    order_load.start()

    def core_copy(half):
        return pltpu.make_async_remote_copy(
            src_ref=part.at[pl.ds(half * 4, 4), :, :, 1 - core],
            dst_ref=core_recv.at[pl.ds(half * 4, 4)],
            send_sem=core_ssem.at[half], recv_sem=core_rsem.at[half],
            device_id=sibling, device_id_type=MESH,
        )

    samp_send[...] = jnp.zeros_like(samp_send)
    spad[...] = jnp.zeros_like(spad)
    trail[0] = jnp.zeros((TW, DB), F32)
    wv[ENTRIES] = jnp.zeros((PB, DB), BF16)
    for block in range(BLOCKS):
        signal[block, HOLD:, :] = jnp.zeros((TW + MAXOFF - HOLD, PB), F32)

    loads[0].wait()

    def first_faces(xs, carry):
        return take_faces(0, xs, [field_a[x + 1, LOW:HIGH, :] for x in xs], carry)

    zstage[0] = over_planes(first_faces, zero_plane)

    pl.semaphore_wait(barrier, expected)
    halo_start(0)

    loads[1].wait()

    for block in range(BLOCKS):
        signal[block, :HOLD, :] = hist[:, block * PB:(block + 1) * PB].astype(F32)
    order_load.wait()
    loads[2].wait()


    def far_pair(p):
        windows, blocks = [], []
        for u in range(2):
            entry = jnp.clip(order[0, 2 * p + u], 0, ENTRIES)
            k = jnp.minimum(lax.shift_right_logical(entry, 4), K_DEV - 1)
            block = jnp.bitwise_and(entry, BLOCKS - 1)
            windows.append(signal[block, pl.ds(delay_ref[k, block], TW), :].astype(BF16))
            blocks.append(wv[jnp.where(entry < ENTRIES, block * K_DEV + k, ENTRIES)])
        term = jnp.dot(
            jnp.concatenate(windows, axis=1), jnp.concatenate(blocks, axis=0),
            preferred_element_type=F32)
        trail[p + 1] = term + trail[jnp.where(order[2, p] > 0, 0, p)]

    def far_pairs(first, amount, unroll):
        def chunk(i, carry):
            for u in range(unroll):
                far_pair(first + i * unroll + u)
            return carry
        lax.fori_loop(0, amount // unroll, chunk, 0)

    def core_start():
        for half in range(2):
            for j in range(half * 4, half * 4 + 4):
                end = jnp.clip(order[1, j], 0, PAIRS)
                for quarter in range(4):
                    found = trail[end, quarter * 128:(quarter + 1) * 128, :]
                    part[j, quarter] = found.reshape(4, 2, ROWS, DB)
            core_copy(half).start()

    loads[3].wait()

    def plane_coefficients(xs, carry):
        for x in xs:
            code = codes[x]
            for index, values in enumerate(COEFFICIENTS):
                coef[index, x] = jnp.where(
                    code == 0, values[0],
                    jnp.where(code == 1, values[1], jnp.where(code == 2, values[2], values[3])),
                ).astype(F32)
        return carry

    over_planes(plane_coefficients, 0)
    slot_lane = lax.broadcasted_iota(jnp.int32, (PB, PB), 1)
    for i in range(SLOT // PB):
        slots = slice(i * PB, (i + 1) * PB)
        cell = jnp.broadcast_to(surf_ref[:, slots].astype(F32), (PB, PB)).T.astype(jnp.int32)
        cell_row = lax.shift_right_arithmetic(cell, 7)
        cellmask[slots, :] = jnp.where(
            slot_lane == jnp.bitwise_and(cell, CZ - 1), 1.0, 0.0)
        for q in range(CX * CY // PB):
            onehot[slots, q * PB:(q + 1) * PB] = jnp.where(
                slot_lane + q * PB == cell_row, 1.0, 0.0).astype(BF16)
    loads[4].wait()

    def leap(step):
        here_ref, other_ref = fields[step % 2], fields[1 - step % 2]
        last = step == STEPS - 1
        parity = slice(step % 2 * CZ, (step % 2 + 1) * CZ)
        halo_wait_recv(step, (1, 2))

        def y_rows(xs, carry):
            rows = [(yrecv[step, 0, pl.ds(x, 1), :], yrecv[step, 1, pl.ds(x, 1), :]) for x in xs]
            for x, (low, high) in zip(xs, rows):
                here_ref[x + 1, LOW - 1:LOW, :] = low
                here_ref[x + 1, HIGH:HIGH + 1, :] = high
            return carry

        over_planes(y_rows, 0, 16)
        z_halo = jnp.where(
            jnp.bitwise_and(lane, 1) == 0,
            pltpu.roll(zrecv[step, 0], 1, 1), pltpu.roll(zrecv[step, 1], CZ - 1, 1))
        ends = jnp.logical_or(lane == 0, lane == CZ - 1)

        def plane_step(xs, carry):
            planes = []
            for x in xs:
                here = here_ref[x + 1, LOW:HIGH, :]
                around = here_ref[x, LOW:HIGH, :] + here_ref[x + 2, LOW:HIGH, :]
                around = around + (
                    here_ref[x + 1, LOW - 1:HIGH - 1, :] + here_ref[x + 1, LOW + 1:HIGH + 1, :])
                beside_z = (jnp.where(lane == 0, 0.0, pltpu.roll(here, 1, 1))
                            + jnp.where(lane == CZ - 1, 0.0, pltpu.roll(here, CZ - 1, 1)))
                outside = pltpu.roll(z_halo, lax.rem(2 * (CZ - x), CZ), 1)
                around = around + (beside_z + jnp.where(ends, outside, 0.0))
                before = other_ref[x + 1, LOW:HIGH, :]
                planes.append(coef[0, x] * here + coef[1, x] * before + coef[2, x] * around)
            for x, new in zip(xs, planes):
                other_ref[x + 1, LOW:HIGH, :] = new
                first = x * CY if isinstance(x, int) else pl.multiple_of(x * CY, CY)
                rounded[pl.ds(first, CY), parity] = new.astype(BF16)
            if last:
                return carry
            return take_faces(step + 1, xs, planes, carry)

        def inner(i, carry):
            return plane_step([1 + i * 10 + u for u in range(10)], carry)

        carry = lax.fori_loop(
            0, (CX - 2) // 10, inner, 0 if last else zero_plane)
        halo_wait_recv(step, (0,))
        if step > 0:
            halo_wait_send(step - 1, (0,))
        here_ref[0, LOW:HIGH, :] = xrecv[step, 0]
        here_ref[CX + 1, LOW:HIGH, :] = xrecv[step, 1]
        carry = plane_step([0, CX - 1], carry)
        if not last:
            zstage[step + 1] = carry
            halo_start(step + 1)

    def to_row(picked):
        return lax.dot_general(
            jnp.ones((8, CZ), BF16), (picked * cellmask[...]).astype(BF16),
            (((1,), (1,)), ((), ())), preferred_element_type=F32)

    def sample_first_two():
        picked = jnp.dot(onehot[...], rounded[...], preferred_element_type=F32)
        for step in range(2):
            samp_send[4 + step:5 + step, :] = to_row(picked[:, step * CZ:(step + 1) * CZ])[0:1, :]

    def sample(step):
        parity = slice(step % 2 * CZ, (step % 2 + 1) * CZ)
        values = to_row(jnp.dot(onehot[...], rounded[:, parity], preferred_element_type=F32))
        if step < STEPS - 1:
            samp_send[4 + step:5 + step, :] = values[0:1, :]
        else:
            last_send[...] = values

    def wait_all_recv(ref, sem):
        pltpu.make_async_remote_copy(
            src_ref=ref, dst_ref=ref, send_sem=idle_sem, recv_sem=sem,
            device_id=sibling, device_id_type=MESH).wait_recv()

    def wait_all_send(ref, sem):
        pltpu.make_async_remote_copy(
            src_ref=ref, dst_ref=ref, send_sem=sem, recv_sem=idle_sem,
            device_id=sibling, device_id_type=MESH).wait_send()

    axes = (("z", "y"), ("y", "z"))

    def index_on(axis):
        return z if axis == "z" else y

    def ring_copy(half, kind, way):
        axis = axes[half][0]
        place_now = index_on(axis)
        step_to = 1 if way == 0 else 3
        chunk = lax.rem(place_now + (2 if kind == 0 else step_to), 4)
        part_now = pl.ds(0 if (kind == 1) == (way == 1) else 2, 2)
        return pltpu.make_async_remote_copy(
            src_ref=sums.at[half, chunk, part_now], dst_ref=ring1.at[half, kind, way],
            send_sem=ring_send, recv_sem=ring_recv.at[0 if kind == 0 else 1],
            device_id=ring_neighbour(axis, step_to), device_id_type=MESH,
        )

    def direct_copy(half, offset):
        axis = axes[half][1]
        return pltpu.make_async_remote_copy(
            src_ref=totals.at[half, lax.rem(index_on(axis) + offset, 4)],
            dst_ref=ring2.at[half, offset - 1],
            send_sem=direct_send, recv_sem=direct_recv,
            device_id=ring_neighbour(axis, offset), device_id_type=MESH,
        )

    def core_finish(half):
        core_copy(half).wait_recv()

        for yy in range(4):
            for zz in range(4):
                total = (part[half * 4:half * 4 + 4, yy, zz, core]
                         + core_recv[half * 4:half * 4 + 4, yy, zz])
                if half == 0:
                    sums[0, zz, yy] = total
                else:
                    sums[1, yy, zz] = total

    def ring_begin(half):
        for kind in (0, 1):
            for way in (0, 1):
                ring_copy(half, kind, way).start()

    def ring_forward():
        wait_all_recv(ring1.at[:, 0], ring_recv.at[0])
        for half in range(2):
            place_now = index_on(axes[half][0])
            for way in (0, 1):
                chunk = lax.rem(place_now + (1 if way == 0 else 3), 4)
                first = 0 if way == 0 else 2
                sums[half, chunk, first:first + 2] = (
                    sums[half, chunk, first:first + 2] + ring1[half, 0, way])
                ring_copy(half, 2, way).start()

    def ring_end():
        wait_all_recv(ring1.at[:, pl.ds(1, 2)], ring_recv.at[1])
        for half in range(2):
            place_now = index_on(axes[half][0])
            totals[half, 0:2] = (
                sums[half, place_now, 0:2] + (ring1[half, 2, 0] + ring1[half, 1, 1]))
            totals[half, 2:4] = (
                sums[half, place_now, 2:4] + (ring1[half, 1, 0] + ring1[half, 2, 1]))
            for offset in (2, 1, 3):
                direct_copy(half, offset).start()

    def direct_end():
        wait_all_recv(ring2, direct_recv)
        for half in range(2):
            result = totals[half, index_on(axes[half][1])]
            result = result + (ring2[half, 0] + (ring2[half, 1] + ring2[half, 2]))
            for j in range(4):
                columns = slice((half * 4 + j) * DB, (half * 4 + j + 1) * DB)
                far_ref[:, columns] = result[j]

    def samp_copy(last, offset):
        source, target = (last_send, last_all) if last else (samp_send, samp_all)
        return pltpu.make_async_remote_copy(
            src_ref=source, dst_ref=target.at[gy],
            send_sem=samp_ssem.at[last], recv_sem=samp_rsem.at[last],
            device_id=(gx, lax.rem(gy + offset, NY_DEV), gz), device_id_type=MESH,
        )

    def samp_start(last):
        for offset in range(1, NY_DEV):
            samp_copy(last, offset).start()
        if last:
            last_all[gy] = last_send[...]
        else:
            samp_all[gy] = samp_send[...]

    def samp_wait(last):
        wait_all_recv((last_all if last else samp_all).at[pl.ds(0, NY_DEV - 1)], samp_rsem.at[last])

    row = lax.broadcasted_iota(jnp.int32, (8, PB), 0)
    width = 4 * K_DEV * PB

    def entry_rows(i, carry):
        held = []
        for block in [i * 4 + u for u in range(4)]:
            for entry in range(K_DEV):
                offset = delay_ref[entry, block]
                target = dir_ref[entry, block]
                early = spad[block, pl.ds(offset + 4, 8), :]
                late = spad[block, pl.ds(offset, 8), :]
                pair = jnp.where(row < 4, early, late)
                pieces = []
                for k in range(TARGETS // 2):
                    wanted = jnp.where(row < 4, 2 * k, 2 * k + 1)
                    pieces.append(jnp.where(wanted == target, pair, 0.0))
                held.append(jnp.concatenate(pieces, axis=0).astype(BF16))
        part_rows = pl.ds(pl.multiple_of((i // 2) * 32, 32), 32)
        columns = pl.ds(pl.multiple_of(lax.rem(i, 2) * width, width), width)
        lhs[part_rows, columns] = jnp.concatenate(held, axis=1)
        return carry

    def last_rows():
        for brick in range(NY_DEV // 2):
            rows = []
            for part_of in (brick, brick + NY_DEV // 2):
                held = []
                for i in range(SLOT // PB):
                    block = part_of * (SLOT // PB) + i
                    samples = last_all[part_of, :, i * PB:(i + 1) * PB]
                    for entry in range(K_DEV):
                        target = jnp.where(
                            delay_ref[entry, block] == MAXOFF, dir_ref[entry, block], -1)
                        held.append(jnp.where(row == target, samples, 0.0))
                rows.append(jnp.concatenate(held, axis=1))
            last_lhs[:, brick * width:(brick + 1) * width] = (
                jnp.concatenate(rows, axis=0).astype(BF16))

    def times_weights(rows_ref):
        half = ENTRIES // 2
        beside_each_other = jnp.concatenate(
            [wv[:half].reshape(half * PB, DB), wv[half:ENTRIES].reshape(half * PB, DB)], axis=1)
        product = jnp.dot(rows_ref[...], beside_each_other, preferred_element_type=F32)
        count_rows = product.shape[0] // 2
        return product[:count_rows, :DB] + product[count_rows:, DB:]

    def corr_copy(last, member):
        source, target = (last_out, last_in) if last else (corr_out, corr_in)
        return pltpu.make_async_remote_copy(
            src_ref=source, dst_ref=target.at[member],
            send_sem=last_ssem if last else corr_ssem,
            recv_sem=last_rsem if last else corr_rsem,
            device_id=owner, device_id_type=MESH,
        )

    def corr_start(last):
        @pl.when(jnp.logical_not(is_owner))
        def _():
            corr_copy(last, group).start()

    far_pairs(0, 28, 14)
    leap(0)
    far_pairs(28, PAIRS - 28, 12)
    core_start()
    halo_wait_send(0, (1, 2))
    leap(1)
    sample_first_two()
    for half in range(2):
        core_finish(half)
        ring_begin(half)
    halo_wait_send(1, (1, 2))
    leap(2)
    save_prev = pltpu.make_async_copy(
        field_b.at[pl.ds(1, CX), pl.ds(LOW, CY)], prev_ref, load_sem.at[5])
    save_prev.start()
    sample(2)
    samp_start(0)
    ring_forward()
    halo_wait_send(2, (1, 2))
    leap(3)
    sample(3)
    samp_start(1)
    save_next = pltpu.make_async_copy(
        field_a.at[pl.ds(1, CX), pl.ds(LOW, CY)], next_ref, load_sem.at[6])
    save_next.start()
    ring_end()
    halo_wait_send(STEPS - 1)
    for half in range(2):
        core_copy(half).wait_send()
    wait_all_send(ring1, ring_send)
    wait_all_send(samp_all.at[pl.ds(0, NY_DEV - 1)], samp_ssem.at[0])
    samp_wait(0)
    for brick in range(NY_DEV):
        for i in range(SLOT // PB):
            spad[brick * (SLOT // PB) + i, 32:40, :] = samp_all[brick, :, i * PB:(i + 1) * PB]
    lax.fori_loop(0, BLOCKS // 4, entry_rows, 0)
    corr_out[...] = times_weights(lhs)
    corr_start(0)
    samp_wait(1)
    last_rows()
    last_out[...] = times_weights(last_lhs)
    corr_start(1)
    direct_end()

    @pl.when(is_owner)
    def _():
        def arrivals(last):
            held, sem = (last_in, last_rsem) if last else (corr_in, corr_rsem)
            wait_all_recv(held.at[pl.ds(0, OWNERS - 1)], sem)

        arrivals(0)
        total = corr_out[...]
        for member in range(OWNERS - 1):
            total = total + corr_in[member]
        for j in range(TARGETS):
            piece = total[(j // 2) * 8:(j // 2) * 8 + 8, :]
            if j % 2 == 0:
                piece = pltpu.roll(piece, 4, 0)
            columns = slice(j * DB, (j + 1) * DB)
            far_ref[8:16, columns] = far_ref[8:16, columns] + jnp.where(row >= 4, piece, 0.0)
        arrivals(1)
        total = last_out[...]
        for member in range(OWNERS - 1):
            total = total + last_in[member]
        for j in range(TARGETS):
            columns = slice(j * DB, (j + 1) * DB)
            far_ref[15:16, columns] = far_ref[15:16, columns] + total[j:j + 1, :]

    wait_all_send(ring2, direct_send)
    wait_all_send(last_all.at[pl.ds(0, NY_DEV - 1)], samp_ssem.at[1])

    @pl.when(jnp.logical_not(is_owner))
    def _():
        corr_copy(0, group).wait_send()
        corr_copy(1, group).wait_send()

    save_prev.wait()
    save_next.wait()


def hall(dirs, delays, surf_index, now, old, code, history, weights):
    any_space = pl.BlockSpec(memory_space=pl.ANY)
    smem = pl.BlockSpec(memory_space=pltpu.SMEM)
    vmem = pl.BlockSpec(memory_space=pltpu.VMEM)
    dma = pltpu.SemaphoreType.DMA
    brick = jax.ShapeDtypeStruct((CX, CY, CZ), F32)
    return pl.pallas_call(
        hall_kernel,
        out_shape=(brick, brick, jax.ShapeDtypeStruct((ROWS, TARGETS * DB), F32)),
        in_specs=[smem, smem, vmem, vmem] + [any_space] * 5,
        out_specs=(any_space, any_space, vmem),
        scratch_shapes=[
            pltpu.VMEM((CX + 2, PADROWS, CZ), F32),
            pltpu.VMEM((CX + 2, PADROWS, CZ), F32),
            pltpu.VMEM((CX, CY, CZ), jnp.int32),
            pltpu.VMEM((3, CX, CY, CZ), F32),
            pltpu.VMEM((STEPS, 2, CX, CZ), F32),
            pltpu.VMEM((STEPS, CY, CZ), F32),
            pltpu.VMEM((STEPS, 2, CY, CZ), F32),
            pltpu.VMEM((STEPS, 2, CX, CZ), F32),
            pltpu.VMEM((STEPS, 2, CY, CZ), F32),
            pltpu.VMEM((SLOT, CX * CY), BF16),
            pltpu.VMEM((SLOT, CZ), F32),
            pltpu.VMEM((CX * CY, 2 * CZ), BF16),
            pltpu.VMEM((8, SLOT), F32),
            pltpu.VMEM((NY_DEV, 8, SLOT), F32),
            pltpu.VMEM((8, SLOT), F32),
            pltpu.VMEM((NY_DEV, 8, SLOT), F32),
            pltpu.VMEM((BLOCKS, 48, PB), F32),
            pltpu.VMEM((64, ENTRIES // 2 * PB), BF16),
            pltpu.VMEM((16, ENTRIES // 2 * PB), BF16),
            pltpu.VMEM((ENTRIES + 1, PB, DB), BF16),
            pltpu.VMEM((BLOCKS, TW + MAXOFF, PB), F32),
            pltpu.VMEM((PAIRS + 1, TW, DB), F32),
            pltpu.VMEM((8, PB), jnp.int32),
            pltpu.SMEM((8, PB), jnp.int32),
            pltpu.VMEM((HOLD, BLOCKS * PB), BF16),
            pltpu.VMEM((TARGETS, 4, 4, 2, ROWS, DB), F32),
            pltpu.VMEM((TARGETS, 4, 4, ROWS, DB), F32),
            pltpu.VMEM((2, 4, 4, 4, ROWS, DB), F32),
            pltpu.VMEM((2, 4, 4, ROWS, DB), F32),
            pltpu.VMEM((2, 3, 2, 2, 4, ROWS, DB), F32),
            pltpu.VMEM((2, 3, 4, ROWS, DB), F32),
            pltpu.VMEM((32, DB), F32),
            pltpu.VMEM((OWNERS, 32, DB), F32),
            pltpu.VMEM((8, DB), F32),
            pltpu.VMEM((OWNERS, 8, DB), F32),
            dma((8,)), dma,
            dma((STEPS, 3, 2)), dma((STEPS, 3, 2)),
            dma((2,)), dma((2,)),
            dma((2,)), dma((2,)),
            dma, dma((2,)), dma, dma,
            dma, dma, dma, dma,
        ],
        compiler_params=pltpu.CompilerParams(
            collective_id=0, has_side_effects=True, vmem_limit_bytes=58 * 1024 * 1024),
    )(dirs, delays, dirs, surf_index, history, now, old, code, weights)


def save_kernel(*refs):
    sources, targets, held, sems = refs[:3], refs[3:6], refs[6:9], refs[9]
    pieces = [(i, slice(0, CX)) for i in (0, 1)]
    pieces.append((2, slice(0, ROWS)))
    arrivals, leaves = [], []
    for number, (i, part) in enumerate(pieces):
        arrivals.append(pltpu.make_async_copy(
            sources[i].at[part], held[i].at[part], sems.at[0, number]))
        leaves.append(pltpu.make_async_copy(
            held[i].at[part], targets[i].at[part], sems.at[1, number]))
    for copy in arrivals:
        copy.start()
    for arrival, leave in zip(arrivals, leaves):
        arrival.wait()
        leave.start()
    for copy in leaves:
        copy.wait()


def save(arrays):
    any_space = pl.BlockSpec(memory_space=pl.ANY)
    return pl.pallas_call(
        save_kernel,
        out_shape=tuple(jax.ShapeDtypeStruct(a.shape, a.dtype) for a in arrays),
        in_specs=[any_space] * 3,
        out_specs=(any_space,) * 3,
        scratch_shapes=[pltpu.VMEM(a.shape, a.dtype) for a in arrays]
        + [pltpu.SemaphoreType.DMA((2, 3))],
    )(*arrays)


def shards(pressure_now, pressure_old, cell_code, surf_index, history, dir_slot, delay, weights):
    flat_weights = weights.reshape(BLOCKS * K_DEV, PB, DB)
    return save(hall(
        dir_slot.T, delay.T, surf_index, pressure_now, pressure_old, cell_code, history,
        flat_weights))


def solution(mesh):
    return jax.shard_map(
        shards,
        mesh=mesh,
        in_specs=(
            P("gx", "gy", "gz"),
            P("gx", "gy", "gz"),
            P("gx", "gy", "gz"),
            P(("gx", "gz"), "gy"),
            P(None, ("gx", "gz")),
            P(("gx", "gz"), "gy"),
            P(("gx", "gz"), "gy"),
            P(("gx", "gz"), "gy", None, None),
        ),
        out_specs=(P("gx", "gy", "gz"), P("gx", "gy", "gz"), P(("gx", "gz"), "gy")),
        check_vma=False,
    )
```
